32 devices in a mesh: seq: 8 (over z, x), head: 4 (over y, core).
Axes of the slice: x: 2, y: 2, z: 4, core: 2. Of those that a mesh axis runs over, the one named last changes fastest.
Arguments:
- frames: bfloat16 [16384, 768], P(('seq', 'head')), may hold values from -6 to 6
- output_grad: bfloat16 [16384, 768], P(('seq', 'head')), may hold values from -6 to 6
- segment_ids: int32 [8, 2048], P('seq'), may hold values from 0 to 1, as said below
- qkv_weight: float32 [768, 2304], P(('seq', 'head')), may hold values from -0.21875 to 0.21875
- proj_weight: float32 [768, 768], P(('seq', 'head')), may hold values from -0.875 to 0.875
- up_weight: float32 [768, 3072], P(('seq', 'head')), may hold values from -0.21875 to 0.21875
- down_weight: float32 [3072, 768], P(('seq', 'head')), may hold values from -0.109375 to 0.109375
- conv_weight: float32 [128, 768, 48], P(None, ('seq', 'head')), may hold values from -0.078125 to 0.078125
- bias_gains: float32 [9, 768], P(None, ('seq', 'head')), may hold values from -1.2 to 2, as said below
- ffn_bias: float32 [3072], P(('seq', 'head')), may hold values from -1.2 to 1.2
- qkv_first: float32 [768, 2304], P(('seq', 'head')), may hold values from -0.00018310547 to 0.00018310547
- proj_first: float32 [768, 768], P(('seq', 'head')), may hold values from -0.00018310547 to 0.00018310547
- up_first: float32 [768, 3072], P(('seq', 'head')), may hold values from -0.00018310547 to 0.00018310547
- down_first: float32 [3072, 768], P(('seq', 'head')), may hold values from -0.00018310547 to 0.00018310547
- conv_first: float32 [128, 768, 48], P(None, ('seq', 'head')), may hold values from -0.00018310547 to 0.00018310547
- bias_gains_first: float32 [9, 768], P(None, ('seq', 'head')), may hold values from -0.00018310547 to 0.00018310547
- ffn_bias_first: float32 [3072], P(('seq', 'head')), may hold values from -0.00018310547 to 0.00018310547
- qkv_second: float32 [768, 2304], P(('seq', 'head')), may hold values from 8.4699366e-11 to 3.3879746e-10
- proj_second: float32 [768, 768], P(('seq', 'head')), may hold values from 8.4699366e-11 to 3.3879746e-10
- up_second: float32 [768, 3072], P(('seq', 'head')), may hold values from 8.4699366e-11 to 3.3879746e-10
- down_second: float32 [3072, 768], P(('seq', 'head')), may hold values from 8.4699366e-11 to 3.3879746e-10
- conv_second: float32 [128, 768, 48], P(None, ('seq', 'head')), may hold values from 8.4699366e-11 to 3.3879746e-10
- bias_gains_second: float32 [9, 768], P(None, ('seq', 'head')), may hold values from 8.4699366e-11 to 3.3879746e-10
- ffn_bias_second: float32 [3072], P(('seq', 'head')), may hold values from 8.4699366e-11 to 3.3879746e-10
Outputs:
- layer_out: bfloat16 [16384, 768], P(('seq', 'head'))
- frames_grad: float32 [16384, 768], P(('seq', 'head'))
- grad_norm: float32 [], replicated
- qkv_new: float32 [768, 2304], P(('seq', 'head'))
- proj_new: float32 [768, 768], P(('seq', 'head'))
- up_new: float32 [768, 3072], P(('seq', 'head'))
- down_new: float32 [3072, 768], P(('seq', 'head'))
- conv_new: float32 [128, 768, 48], P(None, ('seq', 'head'))
- bias_gains_new: float32 [9, 768], P(None, ('seq', 'head'))
- ffn_bias_new: float32 [3072], P(('seq', 'head'))
- qkv_first_new: float32 [768, 2304], P(('seq', 'head'))
- proj_first_new: float32 [768, 768], P(('seq', 'head'))
- up_first_new: float32 [768, 3072], P(('seq', 'head'))
- down_first_new: float32 [3072, 768], P(('seq', 'head'))
- conv_first_new: float32 [128, 768, 48], P(None, ('seq', 'head'))
- bias_gains_first_new: float32 [9, 768], P(None, ('seq', 'head'))
- ffn_bias_first_new: float32 [3072], P(('seq', 'head'))
- qkv_second_new: float32 [768, 2304], P(('seq', 'head'))
- proj_second_new: float32 [768, 768], P(('seq', 'head'))
- up_second_new: float32 [768, 3072], P(('seq', 'head'))
- down_second_new: float32 [3072, 768], P(('seq', 'head'))
- conv_second_new: float32 [128, 768, 48], P(None, ('seq', 'head'))
- bias_gains_second_new: float32 [9, 768], P(None, ('seq', 'head'))
- ffn_bias_second_new: float32 [3072], P(('seq', 'head'))
The draws below stay inside these ranges and needn't reach their ends.
Inputs may be any that keep to these rules, and one draw needn't show every extreme that they name: `segment_ids`: each row of ids never falls and every id of 0 to 1 appears; an utterance has 1 to 1750 frames, and exactly one utterance of each row has exactly 1750. `bias_gains`: rows 4 and 7 are gains between 0.5 and 2; the other rows are biases.
All inputs are finite; a program needn't handle non-finite values.
Results may differ from the reference program's by a relative error of at most 0.015.
The reference program's roundings to bfloat16 on the way count: a program that leaves them out, or rounds other values in their place, can miss the bound.
Values may be sent and summed in bfloat16 or wider, within the bound.
A program may use at most 256 MiB of HBM per device.

```python
import math
import jax
import jax.numpy as jnp
from jax import lax

D = 768
HEADS = 12
HEAD_DIM = 64
FF = 3072
KERNEL = 128
NVEC = 9
STEP = 10
MAX_LEN = 1750
CG = 48
GROUP_TOK = 2048
TOKENS = 16384
UTTS = 2
PARAMS = 11806464
N_SEQ = 8


def draw_bias_gains(key, part):
    key_bias, key_gain = jax.random.split(jax.random.fold_in(key, 17))
    row_index = jnp.arange(NVEC)[:, None]
    gain_rows = (row_index == 4) | (row_index == 7)
    biases_all = 0.3 * jnp.clip(jax.random.normal(key_bias, (NVEC, D), jnp.float32), -4.0, 4.0)
    gains_all = jnp.exp(jax.random.uniform(key_gain, (NVEC, D), jnp.float32, -0.69, 0.69))
    return jnp.where(gain_rows, gains_all, biases_all)


def draw_segment_ids(key, part):
    base_key = jax.random.fold_in(key, 29)
    piece_count = UTTS - 1
    remaining = GROUP_TOK - MAX_LEN
    base_len = remaining // piece_count
    leftover = remaining - base_len * piece_count
    jitter = max(1, base_len * 3 // 4)

    def one_row(row_key):
        key_shift, key_spot = jax.random.split(row_key)
        shifts = jax.random.randint(key_shift, (piece_count + 1,), 0, jitter, dtype=jnp.int32)
        edge_index = jnp.arange(piece_count + 1, dtype=jnp.int32)
        shifts = jnp.where((edge_index == 0) | (edge_index == piece_count), 0, shifts)
        pieces = base_len + shifts[1:] - shifts[:-1]
        pieces = pieces + jnp.where(jnp.arange(piece_count, dtype=jnp.int32) == 0, leftover, 0)
        spot = jax.random.randint(key_spot, (), 0, UTTS, dtype=jnp.int32)
        slot_index = jnp.arange(UTTS, dtype=jnp.int32)
        before = pieces[jnp.clip(slot_index, 0, piece_count - 1)]
        after = pieces[jnp.clip(slot_index - 1, 0, piece_count - 1)]
        lengths = jnp.where(slot_index < spot, before, jnp.where(slot_index == spot, MAX_LEN, after))
        ends = jnp.cumsum(lengths)
        position = jnp.arange(GROUP_TOK, dtype=jnp.int32)
        return jnp.sum((position[:, None] >= ends[None, :]).astype(jnp.int32), axis=1).astype(jnp.int32)
    row_keys = jax.random.split(base_key, N_SEQ)
    return jax.vmap(one_row)(row_keys)


def strengthened(result, rng, source, target, shards_of, factor):
    owner, partner = [(jnp.arange(result.shape[dim]) // (result.shape[dim] // shards_of)).reshape([-1 if axis == dim else 1 for axis in range(result.ndim)]) for dim in (source, target)]
    chosen = jax.random.permutation(rng, shards_of)[partner]
    strong = (owner == chosen) | (owner == (partner + shards_of // 2) % shards_of)
    return jnp.where(strong, factor * result, result)


def levels(own_key, dims, cuts, low, high):
    gain = 1.0
    for dim, blocks in cuts:
        steps = jax.random.uniform(jax.random.fold_in(jax.random.fold_in(own_key, 6), dim), (blocks,), jnp.float32, low / len(cuts), high / len(cuts))
        gain = gain * jnp.repeat(jnp.exp(steps), dims[dim] // blocks).reshape((-1,) + (1,) * (len(dims) - 1 - dim))
    return gain


def gaussian(rng, shape, width, limit, shards=(), kind=jnp.bfloat16):
    array = jax.random.normal(rng, shape, jnp.float32) * width
    if len(shards) > 0:
        array = levels(rng, shape, shards, -0.22, 0.18) * array
    return jnp.clip(array, min=-limit, max=limit).astype(kind)


def gaussian_with(key, extent, width, reach, shards, heavy, kind=jnp.bfloat16):
    drawn = width * jax.random.normal(key, extent, jnp.float32)
    if shards:
        drawn = drawn * levels(key, extent, shards, -0.22, 0.18)
    return jnp.clip(strengthened(drawn, jax.random.fold_in(key, 3), *heavy), -reach, reach).astype(kind)


def setup_inputs(seed: int = 0) -> dict:
    keys = jax.random.split(jax.random.key(seed), 25)
    return {
        "frames": gaussian(keys[0], (TOKENS, D), 1.0, 6.0, ((0, 32),)),
        "output_grad": gaussian_with(keys[1], (TOKENS, D), 1.0, 6.0, ((0, 32),), (0, 1, 32, 2.75)),
        "segment_ids": draw_segment_ids(jax.random.fold_in(keys[24], 71), 0),
        "qkv_weight": gaussian(keys[3], (D, 3 * D), D ** -0.5, 0.21875, ((0, 32),), jnp.float32),
        "proj_weight": gaussian(keys[4], (D, D), (D // 16) ** -0.5, 0.875, ((0, 32),), jnp.float32),
        "up_weight": gaussian(keys[5], (D, FF), D ** -0.5, 0.21875, ((0, 32),), jnp.float32),
        "down_weight": gaussian(keys[6], (FF, D), FF ** -0.5, 0.109375, ((0, 32),), jnp.float32),
        "conv_weight": gaussian(keys[7], (KERNEL, D, CG), (KERNEL * CG) ** -0.5, 0.078125, ((1, 32),), jnp.float32),
        "bias_gains": draw_bias_gains(jax.random.fold_in(keys[24], 71), 0),
        "ffn_bias": gaussian(keys[9], (FF,), 0.3, 1.2, ((0, 32),), jnp.float32),
        "qkv_first": gaussian(keys[10], (D, 3 * D), (0.111 / PARAMS ** 0.5), 0.00018310547, ((0, 32),), jnp.float32),
        "proj_first": gaussian(keys[11], (D, D), (0.111 / PARAMS ** 0.5), 0.00018310547, ((0, 32),), jnp.float32),
        "up_first": gaussian(keys[12], (D, FF), (0.111 / PARAMS ** 0.5), 0.00018310547, ((0, 32),), jnp.float32),
        "down_first": gaussian(keys[13], (FF, D), (0.111 / PARAMS ** 0.5), 0.00018310547, ((0, 32),), jnp.float32),
        "conv_first": gaussian(keys[14], (KERNEL, D, CG), (0.111 / PARAMS ** 0.5), 0.00018310547, ((1, 32),), jnp.float32),
        "bias_gains_first": gaussian(keys[15], (NVEC, D), (0.111 / PARAMS ** 0.5), 0.00018310547, ((1, 32),), jnp.float32),
        "ffn_bias_first": gaussian(keys[16], (FF,), (0.111 / PARAMS ** 0.5), 0.00018310547, ((0, 32),), jnp.float32),
        "qkv_second": jnp.clip(jnp.exp(math.log(3.387974623070278e-10) - 1.3862944 * jax.random.uniform(keys[17], (D, 3 * D), jnp.float32) ** levels(keys[17], (D, 3 * D), ((0, 32),), -0.2, 0.2)), 8.469936557675695e-11, 3.387974623070278e-10),
        "proj_second": jnp.clip(jnp.exp(math.log(3.387974623070278e-10) - 1.3862944 * jax.random.uniform(keys[18], (D, D), jnp.float32) ** levels(keys[18], (D, D), ((0, 32),), -0.2, 0.2)), 8.469936557675695e-11, 3.387974623070278e-10),
        "up_second": jnp.clip(jnp.exp(math.log(3.387974623070278e-10) - 1.3862944 * jax.random.uniform(keys[19], (D, FF), jnp.float32) ** levels(keys[19], (D, FF), ((0, 32),), -0.2, 0.2)), 8.469936557675695e-11, 3.387974623070278e-10),
        "down_second": jnp.clip(jnp.exp(math.log(3.387974623070278e-10) - 1.3862944 * jax.random.uniform(keys[20], (FF, D), jnp.float32) ** levels(keys[20], (FF, D), ((0, 32),), -0.2, 0.2)), 8.469936557675695e-11, 3.387974623070278e-10),
        "conv_second": jnp.clip(jnp.exp(math.log(3.387974623070278e-10) - 1.3862944 * jax.random.uniform(keys[21], (KERNEL, D, CG), jnp.float32) ** levels(keys[21], (KERNEL, D, CG), ((1, 32),), -0.2, 0.2)), 8.469936557675695e-11, 3.387974623070278e-10),
        "bias_gains_second": jnp.clip(jnp.exp(math.log(3.387974623070278e-10) - 1.3862944 * jax.random.uniform(keys[22], (NVEC, D), jnp.float32) ** levels(keys[22], (NVEC, D), ((1, 32),), -0.2, 0.2)), 8.469936557675695e-11, 3.387974623070278e-10),
        "ffn_bias_second": jnp.clip(jnp.exp(math.log(3.387974623070278e-10) - 1.3862944 * jax.random.uniform(keys[23], (FF,), jnp.float32) ** levels(keys[23], (FF,), ((0, 32),), -0.2, 0.2)), 8.469936557675695e-11, 3.387974623070278e-10),
    }


@jax.custom_vjp
def low(v):
    return lax.optimization_barrier(v.astype(jnp.bfloat16)).astype(jnp.float32)

@jax.custom_vjp
def low_back(v):
    return v

def low_keep(v):
    return (low(v), None)

def low_pass(kept, grad):
    return (grad,)

def back_keep(v):
    return (v, None)

def back_low(kept, grad):
    return (low(grad),)
low.defvjp(low_keep, low_pass)
low_back.defvjp(back_keep, back_low)
beta_first = 0.9
beta_second = 0.999
adam_eps = 1e-08
weight_rates = (0.02, 0.1, 0.02, 0.02, 0.02, 0.2, 0.2)
matrix_decay = 0.01
clip_bound = 1.0

def layer_norm(values, scale_gain, shift_row):
    center = values - lax.optimization_barrier(jnp.mean(values, axis=-1, keepdims=True))
    spread = lax.optimization_barrier(jnp.mean(center * center, axis=-1, keepdims=True))
    return center * lax.rsqrt(spread + 1e-05) * scale_gain + shift_row

def gelu_exact(values):
    return jax.nn.gelu(values, approximate=False)

def matmul(left, right):
    return jnp.dot(left, right, precision=lax.Precision.HIGHEST, preferred_element_type=jnp.float32)

def conv_group(inputs, seg_group, conv_w):
    group_len = inputs.shape[0]
    kernel_len, model_width, group_width = conv_w.shape
    group_count = model_width // group_width
    half_kernel = kernel_len // 2
    padded = jnp.pad(inputs, ((half_kernel, half_kernel), (0, 0)))
    padded_seg = jnp.pad(seg_group, (half_kernel, half_kernel), constant_values=-1)

    def advance(running, block_index):
        first_tap = block_index * 8
        stacked = jnp.stack([lax.dynamic_slice_in_dim(padded, first_tap + offset, group_len, 0) for offset in range(8)], axis=1)
        seg_taps = jnp.stack([lax.dynamic_slice_in_dim(padded_seg, first_tap + offset, group_len, 0) for offset in range(8)], axis=1)
        linked = seg_taps == seg_group[:, None]
        stacked = jnp.where(linked[:, :, None], stacked, 0.0).reshape(group_len, 8, group_count, group_width)
        kernel_block = lax.dynamic_slice_in_dim(conv_w, first_tap, 8, 0).reshape(8, group_count, group_width, group_width)
        part = jnp.einsum('tkgc,kgdc->tgd', stacked, kernel_block, precision=lax.Precision.HIGHEST)
        return (running + part, None)
    start = jnp.zeros((group_len, group_count, group_width), jnp.float32)
    running, unused = lax.scan(jax.checkpoint(advance), start, jnp.arange(kernel_len // 8, dtype=jnp.int32))
    return running.reshape(group_len, model_width)

def attention_group(packed, seg_group):
    group_len = packed.shape[0]
    head_dim = packed.shape[2] // 3
    queries = packed[:, :, :head_dim]
    keys_all = packed[:, :, head_dim:2 * head_dim]
    values_all = packed[:, :, 2 * head_dim:]
    block_len = min(512, group_len)
    scale = head_dim ** (-0.5)

    def one_block(block_index):
        start = block_index * block_len
        query_block = lax.dynamic_slice_in_dim(queries, start, block_len, 0)
        seg_block = lax.dynamic_slice_in_dim(seg_group, start, block_len, 0)
        scores = low_back(jnp.einsum('qhe,khe->hqk', query_block, keys_all, precision=lax.Precision.HIGHEST) * scale)
        linked = (seg_block[:, None] == seg_group[None, :])[None]
        scores = jnp.where(linked, scores, -1e+30)
        peak = lax.optimization_barrier(jnp.max(scores, axis=-1, keepdims=True))
        expos = jnp.exp(scores - peak)
        prob = expos / lax.optimization_barrier(jnp.sum(expos, axis=-1, keepdims=True))
        return jnp.einsum('hqk,khe->qhe', low(prob), values_all, precision=lax.Precision.HIGHEST)
    contexts = lax.map(jax.checkpoint(one_block), jnp.arange(group_len // block_len, dtype=jnp.int32))
    return contexts.reshape(group_len, packed.shape[1] * head_dim)

def group_forward(rounded, inputs, seg_group):
    full_qkv, full_proj, full_up, full_down, full_conv, vectors, ffn_vector = rounded
    group_len = inputs.shape[0]
    conv_pre = low_back(conv_group(inputs, seg_group, full_conv) + vectors[0])
    hidden_one = inputs + gelu_exact(conv_pre)
    zero_part = jnp.zeros((HEADS, HEAD_DIM), jnp.float32)
    qkv_bias = jnp.stack([vectors[1].reshape(HEADS, HEAD_DIM), zero_part, vectors[2].reshape(HEADS, HEAD_DIM)], axis=1).reshape(3 * D)
    packed = low_back(low(matmul(low(hidden_one), full_qkv) + qkv_bias))
    context = low_back(low(attention_group(packed.reshape(group_len, HEADS, 3 * HEAD_DIM), seg_group)))
    attn_out = low_back(matmul(context, full_proj) + vectors[3])
    normed_one = layer_norm(hidden_one + attn_out, vectors[4], vectors[5])
    up_pre = low_back(matmul(low(normed_one), full_up) + ffn_vector)
    hidden_mid = low(gelu_exact(up_pre))
    ffn_out = low_back(matmul(hidden_mid, full_down) + vectors[6])
    return layer_norm(normed_one + ffn_out, vectors[7], vectors[8])

def adam_update(weight, grad, first, second, rate, decay):
    first_new = beta_first * first + (1.0 - beta_first) * grad
    second_new = beta_second * second + (1.0 - beta_second) * grad * grad
    first_hat = first_new / (1.0 - beta_first ** STEP)
    second_hat = second_new / (1.0 - beta_second ** STEP)
    new_weight = weight - rate * (first_hat / (jnp.sqrt(second_hat) + adam_eps) + decay * weight)
    return (new_weight, first_new, second_new)

def reference(frames, output_grad, segment_ids, qkv_weight, proj_weight, up_weight, down_weight, conv_weight, bias_gains, ffn_bias, qkv_first, proj_first, up_first, down_first, conv_first, bias_gains_first, ffn_bias_first, qkv_second, proj_second, up_second, down_second, conv_second, bias_gains_second, ffn_bias_second):
    masters = (qkv_weight, proj_weight, up_weight, down_weight, conv_weight, bias_gains, ffn_bias)
    inputs = frames.astype(jnp.float32).reshape(N_SEQ, GROUP_TOK, D)

    def forward(params, values):
        rounded = tuple((low(member) for member in params))

        def group_step(carry, pieces):
            return (carry, group_forward(rounded, pieces[0], pieces[1]))
        carry, outputs = lax.scan(jax.checkpoint(group_step), jnp.zeros((), jnp.float32), (values, segment_ids))
        return outputs
    outputs, pullback = jax.vjp(forward, masters, inputs)
    grads, grad_inputs = pullback(output_grad.astype(jnp.float32).reshape(N_SEQ, GROUP_TOK, D))
    square_sum = jnp.zeros((), jnp.float32)
    for member in grads:
        square_sum = square_sum + jnp.sum(member * member)
    grad_norm = jnp.sqrt(square_sum)
    factor = jnp.minimum(1.0, clip_bound / grad_norm)
    firsts = (qkv_first, proj_first, up_first, down_first, conv_first, bias_gains_first, ffn_bias_first)
    seconds = (qkv_second, proj_second, up_second, down_second, conv_second, bias_gains_second, ffn_bias_second)
    news, first_news, second_news = ([], [], [])
    for index in range(7):
        rate = weight_rates[index]
        decay = matrix_decay if index < 5 else 0.0
        new_weight, first_new, second_new = adam_update(masters[index], grads[index] * factor, firsts[index], seconds[index], rate, decay)
        news.append(new_weight)
        first_news.append(first_new)
        second_news.append(second_new)
    layer_out = outputs.reshape(TOKENS, D).astype(jnp.bfloat16)
    frames_grad = grad_inputs.reshape(TOKENS, D)
    return (layer_out, frames_grad, grad_norm, news[0], news[1], news[2], news[3], news[4], news[5], news[6], first_news[0], first_news[1], first_news[2], first_news[3], first_news[4], first_news[5], first_news[6], second_news[0], second_news[1], second_news[2], second_news[3], second_news[4], second_news[5], second_news[6])
```

```python
import functools

import jax
import jax.numpy as jnp
from jax import lax
from jax.experimental import pallas as pl
from jax.experimental.pallas import tpu as pltpu
from jax.sharding import PartitionSpec as P

HEADS = 12
HEAD_DIM = 64
STEP = 10


norm_eps = 1e-05
beta_first = 0.9
beta_second = 0.999
adam_eps = 1e-08
weight_rates = (0.02, 0.1, 0.02, 0.02, 0.02, 0.2, 0.2)
matrix_decay = 0.01
clip_bound = 1.0


def with_halo(cells, sides, width):
    for axis, dim in sides:
        count = lax.axis_size(axis)
        ends = count - 1
        head = lax.slice_in_dim(cells, 0, width, axis=dim)
        tail = lax.slice_in_dim(cells, cells.shape[dim] - width, cells.shape[dim], axis=dim)
        cells = jnp.concatenate(
            [
                lax.ppermute(tail, axis, [(i, (i + 1) % count) for i in range(ends)]),
                cells,
                lax.ppermute(head, axis, [((i + 1) % count, i) for i in range(ends)]),
            ],
            axis=dim,
        )
    return cells


def layer_norm(values, scale_gain, shift_row):
    center = values - jnp.mean(values, axis=-1, keepdims=True)
    spread = jnp.mean(center * center, axis=-1, keepdims=True)
    return center * lax.rsqrt(spread + norm_eps) * scale_gain + shift_row


def gelu_exact(values):
    return jax.nn.gelu(values, approximate=False)


def adam_update(weight, grad, first, second, rate, decay):
    first_new = beta_first * first + (1.0 - beta_first) * grad
    second_new = beta_second * second + (1.0 - beta_second) * grad * grad
    first_hat = first_new / (1.0 - beta_first**STEP)
    second_hat = second_new / (1.0 - beta_second**STEP)
    new_weight = weight - rate * (first_hat / (jnp.sqrt(second_hat) + adam_eps) + decay * weight)
    return (new_weight, first_new, second_new)


HALF = 64
OWN = 512
WIN = OWN + 2 * HALF
EXT = WIN + HALF
ZROWS = OWN + HALF + 8
CGW = 48

def up(v, n):
    return pltpu.roll(v, v.shape[0] - n, 0)

def down(v, n):
    return pltpu.roll(v, n, 0)

def left(v, n):
    return pltpu.roll(v, v.shape[1] - n, 1)

def right(v, n):
    return pltpu.roll(v, n, 1)

def place(g):
    tile = jnp.minimum(g * CGW // 128, 4)
    return pl.ds(pl.multiple_of(tile * 128, 128), 256), g * CGW - tile * 128

def take_group(ref, g):
    lanes, rem = place(g)
    wide = ref[:, lanes].astype(jnp.float32)
    return pltpu.roll(wide, 256 - rem, 1)[:, :128]

def gapped(xg, cut):
    row = lax.broadcasted_iota(jnp.int32, (EXT, 128), 0)
    zero = jnp.zeros((HALF, 128), jnp.float32)
    before = jnp.concatenate([xg, zero], axis=0)
    after = jnp.concatenate([zero, xg], axis=0)
    return jnp.where(row < cut, before, jnp.where(row < cut + HALF, 0.0, after))

def im2col(xg, rows):
    lane = lax.broadcasted_iota(jnp.int32, (rows, 128), 1)
    turned = {off: (right(xg, off) if off else xg) for off in range(0, 128, 16)}
    cols = []
    for v in range(6):
        acc = None
        for r in range(16):
            lo = CGW * r
            if lo + CGW <= 128 * v or lo >= 128 * (v + 1):
                continue
            piece = turned[lo % 128][8 * r : 8 * r + rows, :]
            acc = piece if acc is None else jnp.where(lane >= lo - 128 * v, piece, acc)
        cols.append(acc.astype(jnp.bfloat16))
    return jnp.concatenate(cols, axis=1)

def pad_weights(w_ref, wp_ref):
    for h in range(2):
        for a in range(8):
            wp_ref[pl.ds(h * 256 + a * 32, 24), :] = w_ref[0, h, a]

def fold_out(z):
    lane = lax.broadcasted_iota(jnp.int32, (ZROWS, 128), 1)
    u = []
    for h in range(2):
        t = z[:, h * 256 : h * 256 + 128] + up(z[:, h * 256 + 128 : h * 256 + 256], 4)
        u.append(t + left(up(t, 2), 64))
    v = jnp.where(lane < 64, u[0], right(u[1], 64))
    o = v + left(up(v, 1), 32)
    return jnp.where(lane < 24, o, left(o, 40))[: OWN + HALF]

def pick_own(o, cut):
    row = lax.broadcasted_iota(jnp.int32, (OWN, 128), 0) + HALF
    return jnp.where(row < cut, o[:OWN], o[HALF : OWN + HALF])

def put_group(out_ref, g, o):
    lanes, rem = place(g)
    lane = lax.broadcasted_iota(jnp.int32, (OWN, 128), 1)
    o = jnp.where(lane < CGW, o, 0.0)
    wide = jnp.concatenate([o, jnp.zeros((OWN, 128), jnp.float32)], axis=1)
    out_ref[:, lanes] += pltpu.roll(wide, rem, 1)

def conv_fwd_kernel(cut_ref, x_ref, w_ref, out_ref, wp_ref):
    g = pl.program_id(0)
    cut = cut_ref[0]
    @pl.when(g == 0)
    def _():
        wp_ref[...] = jnp.zeros_like(wp_ref)
        out_ref[...] = jnp.zeros_like(out_ref)
    pad_weights(w_ref, wp_ref)
    cols = im2col(gapped(take_group(x_ref, g), cut), ZROWS)
    z = lax.dot_general(cols, wp_ref[...], (((1,), (1,)), ((), ())), preferred_element_type=jnp.float32)
    put_group(out_ref, g, pick_own(fold_out(z), cut))

def conv_fwd(cut, xw, w):
    return pl.pallas_call(
        conv_fwd_kernel,
        grid_spec=pltpu.PrefetchScalarGridSpec(
            num_scalar_prefetch=1, grid=(16,),
            in_specs=[pl.BlockSpec((WIN, 768), lambda g, c: (0, 0)),
                      pl.BlockSpec((1, 2, 8, 24, 768), lambda g, c: (g, 0, 0, 0, 0))],
            out_specs=pl.BlockSpec((OWN, 768), lambda g, c: (0, 0)),
            scratch_shapes=[pltpu.VMEM((512, 768), jnp.bfloat16)]),
        out_shape=jax.ShapeDtypeStruct((OWN, 768), jnp.float32),
        compiler_params=pltpu.CompilerParams(vmem_limit_bytes=50 * 2**20),
        cost_estimate=pl.CostEstimate(flops=2 * 16 * 584 * 768 * 512, bytes_accessed=12_000_000, transcendentals=0),
    )(cut, xw, w)

def taps_of(gg):
    lane = lax.broadcasted_iota(jnp.int32, (EXT, 128), 1)
    low = jnp.where(lane < 24, gg, 0.0)
    high = jnp.where((lane >= 64) & (lane < 88), right(gg, 40), 0.0)
    s = low + high
    q = s + right(down(s, 1), 32)
    q2 = down(q, 2)
    parts = []
    for h in range(2):
        if h == 0:
            r = jnp.where(lane < 64, q, right(q2, 64))
        else:
            r = jnp.where(lane < 64, right(q, 64), q2)
        parts += [r, down(r, 4)]
    return jnp.concatenate([p.astype(jnp.bfloat16) for p in parts], axis=1)

def fold_back(z):
    n = OWN + HALF
    lane = lax.broadcasted_iota(jnp.int32, (n, 128), 1)
    a = [z[HALF:, 128 * i : 128 * i + 128] + z[: EXT - HALF, 384 + 128 * i : 512 + 128 * i] for i in range(3)]
    acc = None
    for r in range(8):
        lo = CGW * r
        first = HALF - 8 * r
        tile, off = lo // 128, lo % 128
        piece = a[tile][first : first + n]
        if off:
            piece = left(piece, off)
        if off + CGW > 128:
            piece = jnp.where(lane < 128 - off, piece, right(a[tile + 1][first : first + n], 128 - off))
        acc = piece if acc is None else acc + piece
    return acc

def conv_bwd_kernel(cut_ref, x_ref, g_ref, w_ref, dx_ref, dw_ref, wp_ref):
    g = pl.program_id(0)
    cut = cut_ref[0]
    @pl.when(g == 0)
    def _():
        wp_ref[...] = jnp.zeros_like(wp_ref)
        dx_ref[...] = jnp.zeros_like(dx_ref)
    pad_weights(w_ref, wp_ref)
    taps = taps_of(gapped(take_group(g_ref, g), cut))
    z = jnp.dot(taps, wp_ref[...], preferred_element_type=jnp.float32)
    put_group(dx_ref, g, pick_own(fold_back(z), cut))
    cols = im2col(gapped(take_group(x_ref, g), cut), ZROWS)
    row = lax.broadcasted_iota(jnp.int32, (ZROWS, 512), 0) + HALF
    begin = jnp.where(cut <= HALF, 2 * HALF, HALF)
    end = jnp.where(cut_ref[1] > 0, EXT, jnp.where(cut <= HALF + OWN, OWN + 2 * HALF, OWN + HALF))
    own = jnp.where((row >= begin) & (row < end), taps[HALF : HALF + ZROWS].astype(jnp.float32), 0.0).astype(jnp.bfloat16)
    dw = lax.dot_general(own, cols, (((0,), (0,)), ((), ())), preferred_element_type=jnp.float32)
    for h in range(2):
        for a in range(8):
            dw_ref[0, h, a] = dw[h * 256 + a * 32 : h * 256 + a * 32 + 24].astype(dw_ref.dtype)

def conv_bwd(cut, xw, gw, w, dtype=jnp.bfloat16):
    return pl.pallas_call(
        conv_bwd_kernel,
        grid_spec=pltpu.PrefetchScalarGridSpec(
            num_scalar_prefetch=1, grid=(16,),
            in_specs=[pl.BlockSpec((WIN, 768), lambda g, c: (0, 0)),
                      pl.BlockSpec((WIN, 768), lambda g, c: (0, 0)),
                      pl.BlockSpec((1, 2, 8, 24, 768), lambda g, c: (g, 0, 0, 0, 0))],
            out_specs=[pl.BlockSpec((OWN, 768), lambda g, c: (0, 0)),
                       pl.BlockSpec((1, 2, 8, 24, 768), lambda g, c: (g, 0, 0, 0, 0))],
            scratch_shapes=[pltpu.VMEM((512, 768), jnp.bfloat16)]),
        out_shape=[jax.ShapeDtypeStruct((OWN, 768), jnp.float32), jax.ShapeDtypeStruct((16, 2, 8, 24, 768), dtype)],
        compiler_params=pltpu.CompilerParams(vmem_limit_bytes=50 * 2**20),
        cost_estimate=pl.CostEstimate(flops=4 * 16 * 640 * 768 * 512, bytes_accessed=22_000_000, transcendentals=0),
    )(cut, xw, gw, w)


QT = 256
FAR = -1e30

def fill_keys(seg_ref, blocks, kq_ref, q_ref):
    n = seg_ref.shape[1]
    seg = seg_ref[...]
    row = lax.broadcasted_iota(jnp.int32, (64, n), 0)
    mark = jnp.where(row < 2, jnp.where(seg == row, 1.0, 0.0), 0.0)
    push = jnp.where(row < 2, jnp.where(seg == row, 0.0, FAR), 0.0)
    keys = jnp.concatenate([b[64:128, :] for b in blocks], axis=1).astype(jnp.float32)
    kq_ref[...] = jnp.transpose(jnp.concatenate([keys, mark], axis=0)).astype(jnp.bfloat16)
    queries = jnp.concatenate([b[0:64, :] for b in blocks], axis=1).astype(jnp.float32) * 0.125
    q_ref[...] = jnp.concatenate([queries, push], axis=0).astype(jnp.bfloat16)

def attn_fwd_kernel(seg_ref, b0, b1, b2, b3, c0, c1, c2, c3, lse_ref, o_ref, k_s, q_s, v_s):
    blocks = (b0, b1, b2, b3)
    n = seg_ref.shape[1]
    size = b0.shape[1]
    fill_keys(seg_ref, blocks, k_s, q_s)
    v_s[...] = jnp.concatenate([b[128:192, :] for b in blocks], axis=1)

    def tile(i, unused):
        at = pl.ds(pl.multiple_of(i * QT, QT), QT)
        s = jnp.dot(k_s[...], q_s[:, at], preferred_element_type=jnp.float32)
        peak = jnp.max(s, axis=0, keepdims=True)
        e = jnp.exp(s - peak)
        denom = jnp.sum(e, axis=0, keepdims=True)
        p = (e * (1.0 / denom)).astype(jnp.bfloat16)
        o_ref[0, :, at] = jnp.dot(v_s[...], p, preferred_element_type=jnp.float32)
        lse_ref[0, :, at] = peak + jnp.log(denom)
        return unused

    lax.fori_loop(0, n // QT, tile, 0)
    for j, c in enumerate((c0, c1, c2, c3)):
        c[...] = o_ref[0, :, j * size : (j + 1) * size].astype(jnp.bfloat16)

def attn_fwd(seg, blocks):
    size = blocks[0].shape[1]
    n = 4 * size
    heads = blocks[0].shape[0] // 192
    return pl.pallas_call(
        attn_fwd_kernel,
        grid=(heads,),
        in_specs=[pl.BlockSpec((1, n), lambda h: (0, 0))] + [pl.BlockSpec((192, size), lambda h: (h, 0))] * 4,
        out_specs=[pl.BlockSpec((64, size), lambda h: (h, 0))] * 4
        + [pl.BlockSpec((1, 1, n), lambda h: (h, 0, 0)), pl.BlockSpec((1, 64, n), lambda h: (h, 0, 0))],
        out_shape=[jax.ShapeDtypeStruct((heads * 64, size), jnp.bfloat16)] * 4
        + [jax.ShapeDtypeStruct((heads, 1, n), jnp.float32), jax.ShapeDtypeStruct((heads, 64, n), jnp.float32)],
        scratch_shapes=[pltpu.VMEM((n, 128), jnp.bfloat16), pltpu.VMEM((128, n), jnp.bfloat16), pltpu.VMEM((64, n), jnp.bfloat16)],
        compiler_params=pltpu.CompilerParams(vmem_limit_bytes=50 * 2**20),
        cost_estimate=pl.CostEstimate(flops=heads * n * n * 256, bytes_accessed=6_000_000, transcendentals=heads * n * n),
    )(seg, *blocks)

def attn_bwd_kernel(seg_ref, b0, b1, b2, b3, d0, d1, d2, d3, lse_ref, o_ref, g0, g1, g2, g3, k_s, q_s, v_s, kt_s, do_s, dk_s, dv_s, dq_s):
    blocks = (b0, b1, b2, b3)
    n = seg_ref.shape[1]
    size = b0.shape[1]
    fill_keys(seg_ref, blocks, k_s, q_s)
    v_s[...] = jnp.transpose(jnp.concatenate([b[128:192, :] for b in blocks], axis=1).astype(jnp.float32)).astype(jnp.bfloat16)
    kt_s[...] = jnp.concatenate([b[64:128, :] for b in blocks], axis=1)
    do_s[...] = jnp.concatenate([d[...] for d in (d0, d1, d2, d3)], axis=1)
    dk_s[...] = jnp.zeros_like(dk_s)
    dv_s[...] = jnp.zeros_like(dv_s)

    def tile(i, unused):
        at = pl.ds(pl.multiple_of(i * QT, QT), QT)
        q = q_s[:, at]
        do = do_s[:, at]
        delta = jnp.sum(do.astype(jnp.float32) * o_ref[0, :, at], axis=0, keepdims=True)
        s = jnp.dot(k_s[...], q, preferred_element_type=jnp.float32)
        p = jnp.exp(s - lse_ref[0, :, at])
        dp = jnp.dot(v_s[...], do, preferred_element_type=jnp.float32)
        ds = (p * (dp - delta)).astype(jnp.bfloat16)
        p = p.astype(jnp.bfloat16)
        nt = (((1,), (1,)), ((), ()))
        dv_s[...] += lax.dot_general(do, p, nt, preferred_element_type=jnp.float32)
        dk_s[...] += lax.dot_general(q[:64], ds, nt, preferred_element_type=jnp.float32)
        dq_s[:, at] = jnp.dot(kt_s[...], ds, preferred_element_type=jnp.float32) * 0.125
        return unused

    lax.fori_loop(0, n // QT, tile, 0)
    for j, g in enumerate((g0, g1, g2, g3)):
        span = slice(j * size, (j + 1) * size)
        g[0:64, :] = dq_s[:, span].astype(jnp.bfloat16)
        g[64:128, :] = dk_s[:, span].astype(jnp.bfloat16)
        g[128:192, :] = dv_s[:, span].astype(jnp.bfloat16)

def attn_bwd(seg, blocks, grads, lse, o):
    size = blocks[0].shape[1]
    n = 4 * size
    heads = blocks[0].shape[0] // 192
    return pl.pallas_call(
        attn_bwd_kernel,
        grid=(heads,),
        in_specs=[pl.BlockSpec((1, n), lambda h: (0, 0))] + [pl.BlockSpec((192, size), lambda h: (h, 0))] * 4
        + [pl.BlockSpec((64, size), lambda h: (h, 0))] * 4
        + [pl.BlockSpec((1, 1, n), lambda h: (h, 0, 0)), pl.BlockSpec((1, 64, n), lambda h: (h, 0, 0))],
        out_specs=[pl.BlockSpec((192, size), lambda h: (h, 0))] * 4,
        out_shape=[jax.ShapeDtypeStruct((heads * 192, size), jnp.bfloat16)] * 4,
        scratch_shapes=[pltpu.VMEM((n, 128), jnp.bfloat16), pltpu.VMEM((128, n), jnp.bfloat16), pltpu.VMEM((n, 64), jnp.bfloat16),
                        pltpu.VMEM((64, n), jnp.bfloat16), pltpu.VMEM((64, n), jnp.bfloat16),
                        pltpu.VMEM((64, n), jnp.float32), pltpu.VMEM((64, n), jnp.float32), pltpu.VMEM((64, n), jnp.float32)],
        compiler_params=pltpu.CompilerParams(vmem_limit_bytes=50 * 2**20),
        cost_estimate=pl.CostEstimate(flops=heads * n * n * 640, bytes_accessed=10_000_000, transcendentals=heads * n * n),
    )(seg, *blocks, *grads, lse, o)


MESH = pl.DeviceIdType.MESH

def spot():
    seq, head = lax.axis_index("seq"), lax.axis_index("head")
    return seq // 2, seq % 2, head // 2, head % 2

def device(z, x, y, c):
    return {"seq": z * 2 + x, "head": y * 2 + c}

def greet():
    z, x, y, c = spot()
    barrier = pltpu.get_barrier_semaphore()
    for where in (device(z, x, y, 1 - c), device(z, x, 1 - y, c), device(z, 1 - x, y, c)):
        pl.semaphore_signal(barrier, inc=1, device_id=where, device_id_type=MESH)

    @pl.when(z > 0)
    def _():
        pl.semaphore_signal(barrier, inc=1, device_id=device(z - 1, x, y, c), device_id_type=MESH)

    @pl.when(z < 3)
    def _():
        pl.semaphore_signal(barrier, inc=1, device_id=device(z + 1, x, y, c), device_id_type=MESH)

    pl.semaphore_wait(barrier, jnp.where((z == 0) | (z == 3), 4, 5))

class Spread:
    def __init__(self, own, whole, cut, x_first, send, recv):
        self.own, self.whole, self.cut, self.x_first, self.send, self.recv = own, whole, cut, x_first, send, recv

    def block(self, *lead):
        return self.whole.at[tuple(lead) + self.cut]

    def copy(self, src, dst, n, to):
        return pltpu.make_async_remote_copy(
            src_ref=src, dst_ref=dst, send_sem=self.send.at[n], recv_sem=self.recv.at[n], device_id=to, device_id_type=MESH
        )

    def up(self, k):
        z, x, y, c = spot()
        ref = self.block(z - (k - 1), x, y, c)
        src = self.own.at[self.cut] if k == 1 else ref
        return (z < 3) & (z >= k - 1), self.copy(src, ref, k - 1, device(z + 1, x, y, c))

    def up_landed(self, k):
        z, x, y, c = spot()
        ref = self.block(z - k, x, y, c)
        return z >= k, self.copy(ref, ref, k - 1, device(z, x, y, 1 - c))

    def down(self, k):
        z, x, y, c = spot()
        ref = self.block(z + (k - 1), x, y, c)
        src = self.own.at[self.cut] if k == 1 else ref
        return (z > 0) & (z + k - 1 <= 3), self.copy(src, ref, 2 + k, device(z - 1, x, y, c))

    def down_landed(self, k):
        z, x, y, c = spot()
        ref = self.block(z + k, x, y, c)
        return z + k <= 3, self.copy(ref, ref, 2 + k, device(z, x, y, 1 - c))

    def side(self, which):
        z, x, y, c = spot()
        if which == 2:
            return self.copy(self.block(slice(None), slice(None), slice(None), c), self.block(slice(None), slice(None), slice(None), c), 8, device(z, x, y, 1 - c)), None
        over_x = self.x_first == (which == 0)
        if which == 0:
            mine = self.block(slice(None), x, y, c)
        elif over_x:
            mine = self.block(slice(None), x, slice(None), c)
        else:
            mine = self.block(slice(None), slice(None), y, c)
        to = device(z, 1 - x, y, c) if over_x else device(z, x, 1 - y, c)
        return self.copy(mine, mine, 6 + which, to), None

    def stage(self, n):
        if n == 0:
            z, x, y, c = spot()
            self.local = pltpu.make_async_copy(self.own.at[self.cut], self.block(z, x, y, c), self.recv.at[9])
            self.local.start()
            for ok, copy in (self.up(1), self.down(1)):
                pl.when(ok)(copy.start)
        elif n in (1, 2):
            for landed, onward in ((self.up_landed, self.up), (self.down_landed, self.down)):
                ok, copy = landed(n)
                pl.when(ok)(copy.wait_recv)
                ok, copy = onward(n + 1)
                pl.when(ok)(copy.start)
        elif n == 3:
            for landed in (self.up_landed, self.down_landed):
                ok, copy = landed(3)
                pl.when(ok)(copy.wait_recv)
            self.local.wait()
            self.side(0)[0].start()
        elif n in (4, 5):
            self.side(n - 4)[0].wait_recv()
            self.side(n - 3)[0].start()
        elif n == 6:
            self.side(2)[0].wait_recv()

    def finish(self):
        for k in (1, 2, 3):
            for ok, copy in (self.up(k), self.down(k)):
                pl.when(ok)(copy.wait_send)
        for which in range(3):
            self.side(which)[0].wait_send()

def gather_kernel(plan, n_in, *refs):
    owns, wholes, send, recv = refs[:n_in], refs[n_in : 2 * n_in], refs[2 * n_in], refs[2 * n_in + 1]
    greet()
    units = [Spread(owns[i], wholes[i], cut, x_first, send.at[n], recv.at[n]) for n, (i, cut, x_first) in enumerate(plan)]
    pairs = [units[i : i + 2] for i in range(0, len(units), 2)]
    for t in range(len(pairs) + 6):
        for n in (3, 4, 5, 6, 2, 1, 0):
            if 0 <= t - n < len(pairs):
                for unit in pairs[t - n]:
                    unit.stage(n)
    for unit in units:
        unit.finish()

def gather_all(shards, plan, collective_id=1):
    n = len(shards)
    return pl.pallas_call(
        functools.partial(gather_kernel, plan, n),
        in_specs=[pl.BlockSpec(memory_space=pl.ANY)] * n,
        out_specs=[pl.BlockSpec(memory_space=pl.ANY)] * n,
        out_shape=[jax.ShapeDtypeStruct((4, 2, 2, 2) + s.shape, s.dtype) for s in shards],
        scratch_shapes=[pltpu.SemaphoreType.DMA((len(plan), 9)), pltpu.SemaphoreType.DMA((len(plan), 10))],
        compiler_params=pltpu.CompilerParams(collective_id=collective_id, has_side_effects=True),
    )(*shards)


def greet_plane():
    z, x, y, c = spot()
    barrier = pltpu.get_barrier_semaphore()
    for n in range(1, 8):
        pl.semaphore_signal(barrier, inc=1, device_id=device(z, x ^ (n >> 2), y ^ ((n >> 1) & 1), c ^ (n & 1)), device_id_type=MESH)
    for n in range(1, 4):
        pl.semaphore_signal(barrier, inc=1, device_id=device(z ^ n, x, y, c), device_id_type=MESH)
    pl.semaphore_wait(barrier, 10)


def add_into(dst, src, lead):
    def one(i, unused):
        for n in range(lead[1]):
            for m in range(lead[2]):
                d, s = dst(i, n, m), src(i, n, m)
                d[...] = (d[...].astype(jnp.float32) + s[...].astype(jnp.float32)).astype(d.dtype)
        return unused

    lax.fori_loop(0, lead[0], one, 0)


class Collect:
    def __init__(self, parts, out, cut, x_first, bufs, send, recv):
        self.parts, self.out, self.cut, self.x_first, self.send, self.recv = parts, out, cut, x_first, send, recv
        self.own, self.rc, self.r1, self.r2, self.rz = bufs

    def copy(self, src, dst, n, to):
        return pltpu.make_async_remote_copy(
            src_ref=src, dst_ref=dst, send_sem=self.send.at[n], recv_sem=self.recv.at[n], device_id=to, device_id_type=MESH
        )

    def load(self):
        z, x, y, c = spot()
        every = slice(None)
        return pltpu.make_async_copy(self.parts.at[(every, every, every, c) + self.cut], self.own, self.recv.at[9])

    def core(self):
        z, x, y, c = spot()
        every = slice(None)
        return self.copy(self.parts.at[(every, every, every, 1 - c) + self.cut], self.rc, 0, device(z, x, y, 1 - c))

    def first(self):
        z, x, y, c = spot()
        if self.x_first:
            return self.copy(self.own.at[:, 1 - x], self.r1, 1, device(z, 1 - x, y, c))
        return self.copy(self.own.at[:, :, 1 - y], self.r1, 1, device(z, x, 1 - y, c))

    def second(self):
        z, x, y, c = spot()
        if self.x_first:
            return self.copy(self.own.at[:, x, 1 - y], self.r2, 2, device(z, x, 1 - y, c))
        return self.copy(self.own.at[:, 1 - x, y], self.r2, 2, device(z, 1 - x, y, c))

    def down(self, k):
        z, x, y, c = spot()
        d = z - (4 - k)
        return d >= 0, self.copy(self.own.at[jnp.maximum(d, 0), x, y], self.rz.at[k - 1], 2 + k, device(z - 1, x, y, c))

    def down_landed(self, k):
        z, x, y, c = spot()
        d = z - (3 - k)
        ref = self.rz.at[k - 1]
        return (z < 3) & (d >= 0), d, ref, self.copy(ref, ref, 2 + k, device(z, x, y, 1 - c))

    def up(self, k):
        z, x, y, c = spot()
        d = z + (4 - k)
        return d <= 3, self.copy(self.own.at[jnp.minimum(d, 3), x, y], self.rz.at[2 + k], 5 + k, device(z + 1, x, y, c))

    def up_landed(self, k):
        z, x, y, c = spot()
        d = z + (3 - k)
        ref = self.rz.at[2 + k]
        return (z > 0) & (d <= 3), d, ref, self.copy(ref, ref, 5 + k, device(z, x, y, 1 - c))

    def stage(self, n):
        z, x, y, c = spot()
        if n == 0:
            self.core().start()
            self.load().start()
        elif n == 1:
            self.core().wait_recv()
            self.load().wait()
            add_into(lambda i, j, k: self.own.at[i, j, k], lambda i, j, k: self.rc.at[i, j, k], (4, 2, 2))
            self.first().start()
        elif n == 2:
            self.first().wait_recv()
            if self.x_first:
                add_into(lambda i, j, k: self.own.at[i, x, j], lambda i, j, k: self.r1.at[i, j], (4, 2, 1))
            else:
                add_into(lambda i, j, k: self.own.at[i, j, y], lambda i, j, k: self.r1.at[i, j], (4, 2, 1))
            self.second().start()
        elif n == 3:
            self.second().wait_recv()
            add_into(lambda i, j, k: self.own.at[i, x, y], lambda i, j, k: self.r2.at[i], (4, 1, 1))
            for ok, copy in (self.down(1), self.up(1)):
                pl.when(ok)(copy.start)
        elif n in (4, 5):
            for landed, onward in ((self.down_landed, self.down), (self.up_landed, self.up)):
                ok, d, ref, copy = landed(n - 3)

                @pl.when(ok)
                def _(d=d, ref=ref, copy=copy):
                    copy.wait_recv()
                    own = self.own.at[jnp.clip(d, 0, 3), x, y]
                    own[...] = (own[...].astype(jnp.float32) + ref[...].astype(jnp.float32)).astype(own.dtype)

                ok, copy = onward(n - 2)
                pl.when(ok)(copy.start)
        elif n == 6:
            out = self.out.at[self.cut] if self.cut else self.out
            out[...] = self.own[z, x, y].astype(jnp.float32)
            for landed in (self.down_landed, self.up_landed):
                ok, d, ref, copy = landed(3)

                @pl.when(ok)
                def _(ref=ref, copy=copy):
                    copy.wait_recv()
                    out[...] += ref[...].astype(jnp.float32)

    def finish(self):
        for copy in (self.core(), self.first(), self.second()):
            copy.wait_send()
        for k in (1, 2, 3):
            for ok, copy in (self.down(k), self.up(k)):
                pl.when(ok)(copy.wait_send)


def square_sum(refs, tile):
    tile[...] = jnp.zeros_like(tile)
    for ref in refs:
        v = ref[...]
        v = (v * v).reshape(-1, v.shape[-1])
        v = jnp.sum(v.reshape(-1, 8, v.shape[-1]), axis=0)
        for i in range(0, v.shape[-1], 128):
            tile[...] += v[:, i : i + 128]


def total_square(outs, norm, tiles, send, recv):
    z, x, y, c = spot()
    mine = x * 4 + y * 2 + c
    square_sum(outs, tiles.at[mine])
    copies = []
    for n in range(1, 8):
        to = device(z, x ^ (n >> 2), y ^ ((n >> 1) & 1), c ^ (n & 1))
        copies.append(pltpu.make_async_remote_copy(
            src_ref=tiles.at[mine], dst_ref=tiles.at[mine], send_sem=send.at[n], recv_sem=recv.at[n], device_id=to, device_id_type=MESH))
        copies[-1].start()
    for n in range(1, 8):
        ref = tiles.at[mine ^ n]
        pltpu.make_async_remote_copy(src_ref=ref, dst_ref=ref, send_sem=send.at[n], recv_sem=recv.at[n], device_id=device(z, x, y, 1 - c), device_id_type=MESH).wait_recv()
    total = tiles[0]
    for n in range(1, 8):
        total = total + tiles[n]
    tiles[8 + z] = total
    for n in range(1, 4):
        copies.append(pltpu.make_async_remote_copy(
            src_ref=tiles.at[8 + z], dst_ref=tiles.at[8 + z], send_sem=send.at[7 + n], recv_sem=recv.at[7 + n], device_id=device(z ^ n, x, y, c), device_id_type=MESH))
        copies[-1].start()
    for n in range(1, 4):
        ref = tiles.at[8 + (z ^ n)]
        pltpu.make_async_remote_copy(src_ref=ref, dst_ref=ref, send_sem=send.at[7 + n], recv_sem=recv.at[7 + n], device_id=device(z, x, y, 1 - c), device_id_type=MESH).wait_recv()
    norm[...] = (tiles[8] + tiles[9]) + (tiles[10] + tiles[11])
    for copy in copies:
        copy.wait_send()


def unit_shape(shape, cut):
    cut = tuple(cut) + (slice(None),) * (len(shape) - len(cut))
    return tuple(len(range(*s.indices(d))) for s, d in zip(cut, shape))


def collect_kernel(plan, n_in, *refs):
    parts, outs, norm = refs[:n_in], refs[n_in : 2 * n_in], refs[2 * n_in]
    send, recv, tiles, nsend, nrecv = refs[2 * n_in + 1 : 2 * n_in + 6]
    bufs = refs[2 * n_in + 6 :]
    greet_plane()
    units = [
        Collect(parts[i], outs[i], cut, x_first, bufs[5 * n : 5 * n + 5], send.at[n], recv.at[n])
        for n, (i, cut, x_first) in enumerate(plan)
    ]
    pairs = [units[i : i + 2] for i in range(0, len(units), 2)]
    for t in range(len(pairs) + 6):
        for n in range(7):
            if 0 <= t - n < len(pairs):
                for unit in pairs[t - n]:
                    unit.stage(n)
    for unit in units:
        unit.finish()
    total_square(outs, norm, tiles, nsend, nrecv)


def collect_scratch(plan, shapes, dtype):
    scratch = []
    for i, cut, x_first in plan:
        m = unit_shape(shapes[i], cut)
        scratch += [pltpu.VMEM(lead + m, dtype) for lead in ((4, 2, 2), (4, 2, 2), (4, 2), (4,), (6,))]
    return scratch


def collect_all(parts, plan, collective_id=2):
    n = len(parts)
    shapes = [p.shape[4:] for p in parts]
    return pl.pallas_call(
        functools.partial(collect_kernel, plan, n),
        in_specs=[pl.BlockSpec(memory_space=pl.ANY)] * n,
        out_specs=[pl.BlockSpec(memory_space=pltpu.VMEM)] * (n + 1),
        out_shape=[jax.ShapeDtypeStruct(s, jnp.float32) for s in shapes] + [jax.ShapeDtypeStruct((8, 128), jnp.float32)],
        scratch_shapes=[pltpu.SemaphoreType.DMA((len(plan), 9)), pltpu.SemaphoreType.DMA((len(plan), 10)),
                        pltpu.VMEM((12, 8, 128), jnp.float32), pltpu.SemaphoreType.DMA((11,)), pltpu.SemaphoreType.DMA((11,))]
        + collect_scratch(plan, shapes, parts[0].dtype),
        compiler_params=pltpu.CompilerParams(collective_id=collective_id, has_side_effects=True, vmem_limit_bytes=60 * 2**20),
    )(*parts)


S = slice


def gather_plan():
    plan = []
    for a in range(0, 8, 2):
        plan += [(0, (S(a, a + 1),), False), (0, (S(a + 1, a + 2),), True)]
    plan += [(1, (S(None), S(0, 1152)), False), (1, (S(None), S(1152, 2304)), True)]
    plan += [(2, (S(None), S(0, 384)), False), (2, (S(None), S(384, 768)), True)]
    for i in range(0, 3072, 1536):
        plan += [(3, (S(None), S(i, i + 768)), False), (3, (S(None), S(i + 768, i + 1536)), True)]
    plan += [(4, (S(0, 32),), False), (4, (S(32, 64),), True), (4, (S(64, 96),), False), (5, (), True)]
    return plan


def collect_plan():
    plan = [(4, (S(0, 32),), False), (4, (S(32, 64),), True), (4, (S(64, 96),), False)]
    for i in range(4):
        plan.append((3, (S(None), S(768 * i, 768 * i + 768)), i % 2 == 0))
    plan.append((2, (), True))
    for i in range(3):
        plan.append((1, (S(None), S(768 * i, 768 * i + 768)), i % 2 == 0))
    for a in range(0, 8, 2):
        plan += [(0, (S(a, a + 1),), True), (0, (S(a + 1, a + 2),), False)]
    plan.append((5, (), False))
    return plan


def by_chips():
    return lax.axis_size("seq") == 8 and lax.axis_size("head") == 4


def gather_weights(parts):
    if by_chips():
        return [w.reshape((32,) + w.shape[4:]) for w in gather_all(parts, gather_plan())]
    return [lax.all_gather(p, ("seq", "head"), axis=0) for p in parts]


def collect_grads(parts):
    if by_chips():
        outs = collect_all([p.reshape((4, 2, 2, 2) + p.shape[1:]) for p in parts], collect_plan())
        return outs[:-1], jnp.sum(outs[-1])
    outs = [lax.psum_scatter(p.astype(jnp.float32), ("seq", "head"), scatter_dimension=0, tiled=False) for p in parts]
    square = jnp.zeros((), jnp.float32)
    for out in outs:
        square = square + jnp.sum(out * out)
    return outs, lax.psum(square, ("seq", "head"))


def trade(pieces):
    count = lax.axis_size("head")
    return [pieces[0]] + [lax.ppermute(pieces[d], "head", [(i, i ^ d) for i in range(count)]) for d in range(1, count)]


def by_partner(stacked):
    me = lax.axis_index("head")
    return [lax.dynamic_index_in_dim(stacked, me ^ d, 0, keepdims=False) for d in range(stacked.shape[0])]


def from_partner(pieces):
    me = lax.axis_index("head")
    stacked = jnp.stack(pieces)
    return jnp.concatenate([lax.dynamic_index_in_dim(stacked, me ^ j, 0, keepdims=False) for j in range(len(pieces))], axis=0)


def shards(
    frames, output_grad, segment_ids, qkv_weight, proj_weight, up_weight, down_weight, conv_weight, bias_gains, ffn_bias,
    qkv_first, proj_first, up_first, down_first, conv_first, bias_gains_first, ffn_bias_first,
    qkv_second, proj_second, up_second, down_second, conv_second, bias_gains_second, ffn_bias_second,
):
    low_type = jnp.bfloat16
    f32 = jnp.float32
    count = lax.axis_size("seq") * lax.axis_size("head")
    row_count, model_width = frames.shape
    head_groups = lax.axis_size("head")
    head_index = lax.axis_index("head")
    kernel_len, conv_rows, group_width = conv_weight.shape
    vec_rows, vec_cols = bias_gains.shape
    ffn_cols = ffn_bias.shape[0]
    conv_low = conv_weight.astype(low_type).reshape(16, 8, conv_rows, group_width).transpose(1, 2, 0, 3).reshape(8, conv_rows, 768)
    small = jnp.concatenate([bias_gains.astype(low_type).reshape(-1), ffn_bias.astype(low_type)])
    small = jnp.pad(small, (0, 2048 - small.shape[0])).reshape(16, 128)
    all_conv, all_qkv, all_proj, all_up, all_down, all_small = gather_weights(
        [conv_low, qkv_weight.astype(low_type), proj_weight.astype(low_type), up_weight.astype(low_type), down_weight.astype(low_type), small]
    )
    full_qkv = all_qkv.reshape(model_width, -1)
    full_proj = all_proj.reshape(model_width, -1)
    full_up = all_up.reshape(model_width, -1)
    full_down = all_down.reshape(-1, model_width)
    full_conv = all_conv.reshape(16, 2, 24 // conv_rows, 8, conv_rows, 768).transpose(0, 1, 3, 2, 4, 5).reshape(16, 2, 8, 24, 768)
    all_small = all_small.reshape(count, 2048).astype(f32)
    vectors = all_small[:, : vec_rows * vec_cols].reshape(count, vec_rows, vec_cols).transpose(1, 0, 2).reshape(vec_rows, model_width)
    full_ffn = all_small[:, vec_rows * vec_cols : vec_rows * vec_cols + ffn_cols].reshape(-1)

    seg_group = segment_ids[0]
    half_kernel = kernel_len // 2
    boundary = jnp.sum((seg_group == 0).astype(jnp.int32))
    cut = jnp.clip(boundary - head_index * row_count + half_kernel, 0, row_count + kernel_len)
    cut = jnp.stack([cut, (head_index == head_groups - 1).astype(jnp.int32)]).astype(jnp.int32)
    seg_rows = jnp.concatenate(by_partner(seg_group.reshape(head_groups, 1, row_count)), axis=1)

    window = with_halo(frames, (("head", 0),), half_kernel)
    conv_pre = conv_fwd(cut, window, full_conv) + vectors[0]
    conv_act, conv_act_back = jax.vjp(gelu_exact, conv_pre)
    hidden_one = frames.astype(f32) + conv_act
    attn_in = hidden_one.astype(low_type)
    zero_part = jnp.zeros((HEADS, HEAD_DIM), f32)
    qkv_bias = jnp.stack(
        [vectors[1].reshape(HEADS, HEAD_DIM), zero_part, vectors[2].reshape(HEADS, HEAD_DIM)], axis=1
    ).reshape(3 * model_width)
    packed = (
        lax.dot_general(full_qkv, attn_in, (((0,), (1,)), ((), ())), preferred_element_type=f32) + qkv_bias[:, None]
    ).astype(low_type)
    blocks = trade(by_partner(packed.reshape(head_groups, -1, row_count)))
    fwd = attn_fwd(seg_rows, blocks)
    context = from_partner(trade(fwd[:4]))
    attn_out = lax.dot_general(context, full_proj, (((0,), (0,)), ((), ())), preferred_element_type=f32) + vectors[3]
    normed_one, norm_one_back = jax.vjp(layer_norm, hidden_one + attn_out, vectors[4], vectors[5])
    ffn_in = normed_one.astype(low_type)
    up_act, up_back = jax.vjp(gelu_exact, jnp.dot(ffn_in, full_up, preferred_element_type=f32) + full_ffn)
    hidden_mid = up_act.astype(low_type)
    hidden_three = normed_one + jnp.dot(hidden_mid, full_down, preferred_element_type=f32) + vectors[6]
    layer_out_full, norm_two_back = jax.vjp(layer_norm, hidden_three, vectors[7], vectors[8])
    grad_three, grad_gain_two, grad_shift_two = norm_two_back(output_grad.astype(f32))
    grad_ffn = grad_three.astype(low_type)
    grad_down = jnp.einsum("tf,td->fd", hidden_mid, grad_ffn, preferred_element_type=f32).astype(low_type)
    grad_down_bias = jnp.sum(grad_ffn.astype(f32), axis=0)
    (grad_up_pre,) = up_back(jnp.einsum("td,fd->tf", grad_ffn, full_down, preferred_element_type=f32))
    grad_up_low = grad_up_pre.astype(low_type)
    grad_up = jnp.einsum("td,tf->df", ffn_in, grad_up_low, preferred_element_type=f32).astype(low_type)
    grad_ffn_bias = jnp.sum(grad_up_low.astype(f32), axis=0)
    grad_normed = grad_three + jnp.einsum("tf,df->td", grad_up_low, full_up, preferred_element_type=f32)
    grad_two, grad_gain_one, grad_shift_one = norm_one_back(grad_normed)
    grad_attn = grad_two.astype(low_type)
    grad_proj = jnp.dot(context, grad_attn, preferred_element_type=f32).astype(low_type)
    grad_proj_bias = jnp.sum(grad_attn.astype(f32), axis=0)
    grad_context = lax.dot_general(full_proj, grad_attn, (((1,), (1,)), ((), ())), preferred_element_type=f32).astype(low_type)
    grad_blocks = trade(by_partner(grad_context.reshape(head_groups, -1, row_count)))
    grad_packed = from_partner(trade(attn_bwd(seg_rows, blocks, grad_blocks, fwd[4], fwd[5])))
    grad_qkv = lax.dot_general(attn_in, grad_packed, (((0,), (1,)), ((), ())), preferred_element_type=f32).astype(low_type)
    grad_split = jnp.sum(grad_packed.astype(f32), axis=1).reshape(HEADS, 3, HEAD_DIM)
    grad_query_bias = grad_split[:, 0].reshape(model_width)
    grad_value_bias = grad_split[:, 2].reshape(model_width)
    grad_hidden_one = grad_two + lax.dot_general(grad_packed, full_qkv, (((0,), (1,)), ((), ())), preferred_element_type=f32)
    (grad_conv_pre,) = conv_act_back(grad_hidden_one)
    grad_conv_low = grad_conv_pre.astype(low_type)
    grad_conv_bias = jnp.sum(grad_conv_low.astype(f32), axis=0)
    grad_window = with_halo(grad_conv_low, (("head", 0),), half_kernel)
    grad_frames_conv, grad_conv = conv_bwd(cut, window, grad_window, full_conv)
    frames_grad = grad_hidden_one + grad_frames_conv
    grad_conv = grad_conv.reshape(16, 2, 8, 24 // conv_rows, conv_rows, 768).transpose(0, 1, 3, 2, 4, 5).reshape(count, 8, conv_rows, 768)
    grad_vectors = jnp.stack(
        [
            grad_conv_bias, grad_query_bias, grad_value_bias, grad_proj_bias, grad_gain_one, grad_shift_one,
            grad_down_bias, grad_gain_two, grad_shift_two,
        ],
        axis=0,
    )
    grad_small = jnp.concatenate(
        [grad_vectors.reshape(vec_rows, count, vec_cols).transpose(1, 0, 2).reshape(count, -1), grad_ffn_bias.reshape(count, ffn_cols)], axis=1
    )
    grad_small = jnp.pad(grad_small, ((0, 0), (0, 2048 - grad_small.shape[1]))).astype(low_type).reshape(count, 16, 128)
    (sum_conv, sum_qkv, sum_proj, sum_up, sum_down, sum_small), square_sum = collect_grads(
        [
            grad_conv,
            grad_qkv.reshape((count,) + qkv_weight.shape),
            grad_proj.reshape((count,) + proj_weight.shape),
            grad_up.reshape((count,) + up_weight.shape),
            grad_down.reshape((count,) + down_weight.shape),
            grad_small,
        ]
    )
    sum_conv = sum_conv.reshape(8, conv_rows, 16, group_width).transpose(2, 0, 1, 3).reshape(conv_weight.shape)
    sum_small = sum_small.reshape(-1)
    sum_vectors = sum_small[: vec_rows * vec_cols].reshape(vec_rows, vec_cols)
    sum_ffn_bias = sum_small[vec_rows * vec_cols : vec_rows * vec_cols + ffn_cols]
    summed = (sum_qkv, sum_proj, sum_up, sum_down, sum_conv, sum_vectors, sum_ffn_bias)
    grad_norm = jnp.sqrt(square_sum)
    factor = jnp.minimum(1.0, clip_bound / grad_norm)
    masters = (qkv_weight, proj_weight, up_weight, down_weight, conv_weight, bias_gains, ffn_bias)
    firsts = (qkv_first, proj_first, up_first, down_first, conv_first, bias_gains_first, ffn_bias_first)
    seconds = (qkv_second, proj_second, up_second, down_second, conv_second, bias_gains_second, ffn_bias_second)
    news, first_news, second_news = [], [], []
    for index in range(7):
        decay = matrix_decay if index < 5 else 0.0
        new_weight, first_new, second_new = adam_update(
            masters[index], summed[index] * factor, firsts[index], seconds[index], weight_rates[index], decay
        )
        news.append(new_weight)
        first_news.append(first_new)
        second_news.append(second_new)
    return (layer_out_full.astype(low_type), frames_grad, grad_norm, *news, *first_news, *second_news)


def solution(mesh):
    rows, both = P(("seq", "head"), None), ("seq", "head")
    weights = (rows, rows, rows, rows, P(None, both, None), P(None, both), P(both))
    return jax.shard_map(
        shards,
        mesh=mesh,
        in_specs=(rows, rows, P("seq", None)) + weights * 3,
        out_specs=(rows, rows, P()) + weights * 3,
        check_vma=False,
    )
```

```python
import functools

import jax
import jax.numpy as jnp
from jax import lax
from jax.experimental import pallas as pl
from jax.experimental.pallas import tpu as pltpu
from jax.sharding import PartitionSpec as P

HEADS = 12
HEAD_DIM = 64
STEP = 10


norm_eps = 1e-05
beta_first = 0.9
beta_second = 0.999
adam_eps = 1e-08
weight_rates = (0.02, 0.1, 0.02, 0.02, 0.02, 0.2, 0.2)
matrix_decay = 0.01
clip_bound = 1.0


def with_halo(cells, sides, width):
    for axis, dim in sides:
        count = lax.axis_size(axis)
        ends = count - 1
        head = lax.slice_in_dim(cells, 0, width, axis=dim)
        tail = lax.slice_in_dim(cells, cells.shape[dim] - width, cells.shape[dim], axis=dim)
        cells = jnp.concatenate(
            [
                lax.ppermute(tail, axis, [(i, (i + 1) % count) for i in range(ends)]),
                cells,
                lax.ppermute(head, axis, [((i + 1) % count, i) for i in range(ends)]),
            ],
            axis=dim,
        )
    return cells


def layer_norm(values, scale_gain, shift_row):
    center = values - jnp.mean(values, axis=-1, keepdims=True)
    spread = jnp.mean(center * center, axis=-1, keepdims=True)
    return center * lax.rsqrt(spread + norm_eps) * scale_gain + shift_row


def gelu_exact(values):
    return jax.nn.gelu(values, approximate=False)


def adam_update(weight, grad, first, second, rate, decay):
    first_new = beta_first * first + (1.0 - beta_first) * grad
    second_new = beta_second * second + (1.0 - beta_second) * grad * grad
    first_hat = first_new / (1.0 - beta_first**STEP)
    second_hat = second_new / (1.0 - beta_second**STEP)
    new_weight = weight - rate * (first_hat / (jnp.sqrt(second_hat) + adam_eps) + decay * weight)
    return (new_weight, first_new, second_new)


HALF = 64
OWN = 512
WIN = OWN + 2 * HALF
EXT = WIN + HALF
ZROWS = OWN + HALF + 8
CGW = 48

def up(v, n):
    return pltpu.roll(v, v.shape[0] - n, 0)

def down(v, n):
    return pltpu.roll(v, n, 0)

def left(v, n):
    return pltpu.roll(v, v.shape[1] - n, 1)

def right(v, n):
    return pltpu.roll(v, n, 1)

def place(g):
    tile = jnp.minimum(g * CGW // 128, 4)
    return pl.ds(pl.multiple_of(tile * 128, 128), 256), g * CGW - tile * 128

def take_group(ref, g):
    lanes, rem = place(g)
    wide = ref[:, lanes].astype(jnp.float32)
    return pltpu.roll(wide, 256 - rem, 1)[:, :128]

def gapped(xg, cut):
    row = lax.broadcasted_iota(jnp.int32, (EXT, 128), 0)
    zero = jnp.zeros((HALF, 128), jnp.float32)
    before = jnp.concatenate([xg, zero], axis=0)
    after = jnp.concatenate([zero, xg], axis=0)
    return jnp.where(row < cut, before, jnp.where(row < cut + HALF, 0.0, after))

def im2col(xg, rows):
    lane = lax.broadcasted_iota(jnp.int32, (rows, 128), 1)
    turned = {off: (right(xg, off) if off else xg) for off in range(0, 128, 16)}
    cols = []
    for v in range(6):
        acc = None
        for r in range(16):
            lo = CGW * r
            if lo + CGW <= 128 * v or lo >= 128 * (v + 1):
                continue
            piece = turned[lo % 128][8 * r : 8 * r + rows, :]
            acc = piece if acc is None else jnp.where(lane >= lo - 128 * v, piece, acc)
        cols.append(acc.astype(jnp.bfloat16))
    return jnp.concatenate(cols, axis=1)

def pad_weights(w_ref, wp_ref):
    for h in range(2):
        for a in range(8):
            wp_ref[pl.ds(h * 256 + a * 32, 24), :] = w_ref[0, h, a]

def fold_out(z):
    lane = lax.broadcasted_iota(jnp.int32, (ZROWS, 128), 1)
    u = []
    for h in range(2):
        t = z[:, h * 256 : h * 256 + 128] + up(z[:, h * 256 + 128 : h * 256 + 256], 4)
        u.append(t + left(up(t, 2), 64))
    v = jnp.where(lane < 64, u[0], right(u[1], 64))
    o = v + left(up(v, 1), 32)
    return jnp.where(lane < 24, o, left(o, 40))[: OWN + HALF]

def pick_own(o, cut):
    row = lax.broadcasted_iota(jnp.int32, (OWN, 128), 0) + HALF
    return jnp.where(row < cut, o[:OWN], o[HALF : OWN + HALF])

def put_group(out_ref, g, o):
    lanes, rem = place(g)
    lane = lax.broadcasted_iota(jnp.int32, (OWN, 128), 1)
    o = jnp.where(lane < CGW, o, 0.0)
    wide = jnp.concatenate([o, jnp.zeros((OWN, 128), jnp.float32)], axis=1)
    out_ref[:, lanes] += pltpu.roll(wide, rem, 1)

def conv_fwd_kernel(cut_ref, x_ref, w_ref, out_ref, wp_ref):
    g = pl.program_id(0)
    cut = cut_ref[0]
    @pl.when(g == 0)
    def _():
        wp_ref[...] = jnp.zeros_like(wp_ref)
        out_ref[...] = jnp.zeros_like(out_ref)
    pad_weights(w_ref, wp_ref)
    cols = im2col(gapped(take_group(x_ref, g), cut), ZROWS)
    z = lax.dot_general(cols, wp_ref[...], (((1,), (1,)), ((), ())), preferred_element_type=jnp.float32)
    put_group(out_ref, g, pick_own(fold_out(z), cut))

def conv_fwd(cut, xw, w):
    return pl.pallas_call(
        conv_fwd_kernel,
        grid_spec=pltpu.PrefetchScalarGridSpec(
            num_scalar_prefetch=1, grid=(16,),
            in_specs=[pl.BlockSpec((WIN, 768), lambda g, c: (0, 0)),
                      pl.BlockSpec((1, 2, 8, 24, 768), lambda g, c: (g, 0, 0, 0, 0))],
            out_specs=pl.BlockSpec((OWN, 768), lambda g, c: (0, 0)),
            scratch_shapes=[pltpu.VMEM((512, 768), jnp.bfloat16)]),
        out_shape=jax.ShapeDtypeStruct((OWN, 768), jnp.float32),
        compiler_params=pltpu.CompilerParams(vmem_limit_bytes=50 * 2**20),
        cost_estimate=pl.CostEstimate(flops=2 * 16 * 584 * 768 * 512, bytes_accessed=12_000_000, transcendentals=0),
    )(cut, xw, w)

def taps_of(gg):
    lane = lax.broadcasted_iota(jnp.int32, (EXT, 128), 1)
    low = jnp.where(lane < 24, gg, 0.0)
    high = jnp.where((lane >= 64) & (lane < 88), right(gg, 40), 0.0)
    s = low + high
    q = s + right(down(s, 1), 32)
    q2 = down(q, 2)
    parts = []
    for h in range(2):
        if h == 0:
            r = jnp.where(lane < 64, q, right(q2, 64))
        else:
            r = jnp.where(lane < 64, right(q, 64), q2)
        parts += [r, down(r, 4)]
    return jnp.concatenate([p.astype(jnp.bfloat16) for p in parts], axis=1)

def fold_back(z):
    n = OWN + HALF
    lane = lax.broadcasted_iota(jnp.int32, (n, 128), 1)
    a = [z[HALF:, 128 * i : 128 * i + 128] + z[: EXT - HALF, 384 + 128 * i : 512 + 128 * i] for i in range(3)]
    acc = None
    for r in range(8):
        lo = CGW * r
        first = HALF - 8 * r
        tile, off = lo // 128, lo % 128
        piece = a[tile][first : first + n]
        if off:
            piece = left(piece, off)
        if off + CGW > 128:
            piece = jnp.where(lane < 128 - off, piece, right(a[tile + 1][first : first + n], 128 - off))
        acc = piece if acc is None else acc + piece
    return acc

def conv_bwd_kernel(cut_ref, x_ref, g_ref, w_ref, dx_ref, dw_ref, wp_ref):
    g = pl.program_id(0)
    cut = cut_ref[0]
    @pl.when(g == 0)
    def _():
        wp_ref[...] = jnp.zeros_like(wp_ref)
        dx_ref[...] = jnp.zeros_like(dx_ref)
    pad_weights(w_ref, wp_ref)
    taps = taps_of(gapped(take_group(g_ref, g), cut))
    z = jnp.dot(taps, wp_ref[...], preferred_element_type=jnp.float32)
    put_group(dx_ref, g, pick_own(fold_back(z), cut))
    cols = im2col(gapped(take_group(x_ref, g), cut), ZROWS)
    row = lax.broadcasted_iota(jnp.int32, (ZROWS, 512), 0) + HALF
    begin = jnp.where(cut <= HALF, 2 * HALF, HALF)
    end = jnp.where(cut_ref[1] > 0, EXT, jnp.where(cut <= HALF + OWN, OWN + 2 * HALF, OWN + HALF))
    own = jnp.where((row >= begin) & (row < end), taps[HALF : HALF + ZROWS].astype(jnp.float32), 0.0).astype(jnp.bfloat16)
    dw = lax.dot_general(own, cols, (((0,), (0,)), ((), ())), preferred_element_type=jnp.float32)
    for h in range(2):
        for a in range(8):
            dw_ref[0, h, a] = dw[h * 256 + a * 32 : h * 256 + a * 32 + 24].astype(dw_ref.dtype)

def conv_bwd(cut, xw, gw, w, dtype=jnp.bfloat16):
    return pl.pallas_call(
        conv_bwd_kernel,
        grid_spec=pltpu.PrefetchScalarGridSpec(
            num_scalar_prefetch=1, grid=(16,),
            in_specs=[pl.BlockSpec((WIN, 768), lambda g, c: (0, 0)),
                      pl.BlockSpec((WIN, 768), lambda g, c: (0, 0)),
                      pl.BlockSpec((1, 2, 8, 24, 768), lambda g, c: (g, 0, 0, 0, 0))],
            out_specs=[pl.BlockSpec((OWN, 768), lambda g, c: (0, 0)),
                       pl.BlockSpec((1, 2, 8, 24, 768), lambda g, c: (g, 0, 0, 0, 0))],
            scratch_shapes=[pltpu.VMEM((512, 768), jnp.bfloat16)]),
        out_shape=[jax.ShapeDtypeStruct((OWN, 768), jnp.float32), jax.ShapeDtypeStruct((16, 2, 8, 24, 768), dtype)],
        compiler_params=pltpu.CompilerParams(vmem_limit_bytes=50 * 2**20),
        cost_estimate=pl.CostEstimate(flops=4 * 16 * 640 * 768 * 512, bytes_accessed=22_000_000, transcendentals=0),
    )(cut, xw, gw, w)


QT = 256
QF = 512
FAR = -1e30

def fold_rows(v, op):
    while v.shape[0] > 8:
        n = v.shape[0] // 2
        v = op(v[:n], v[n:])
    return v


def fill_keys(seg_ref, blocks, kq_ref, q_ref):
    n = seg_ref.shape[1]
    seg = seg_ref[...]
    row = lax.broadcasted_iota(jnp.int32, (64, n), 0)
    mark = jnp.where(row < 2, jnp.where(seg == row, 1.0, 0.0), 0.0)
    push = jnp.where(row < 2, jnp.where(seg == row, 0.0, FAR), 0.0)
    keys = jnp.concatenate([b[64:128, :] for b in blocks], axis=1).astype(jnp.float32)
    kq_ref[...] = jnp.transpose(jnp.concatenate([keys, mark], axis=0)).astype(jnp.bfloat16)
    queries = jnp.concatenate([b[0:64, :] for b in blocks], axis=1).astype(jnp.float32) * 0.125
    q_ref[...] = jnp.concatenate([queries, push], axis=0).astype(jnp.bfloat16)

def attn_fwd_kernel(seg_ref, b0, b1, b2, b3, c0, c1, c2, c3, lse_ref, o_ref, k_s, q_s, v_s):
    blocks = (b0, b1, b2, b3)
    n = seg_ref.shape[1]
    size = b0.shape[1]
    fill_keys(seg_ref, blocks, k_s, q_s)
    v_s[...] = jnp.concatenate([b[128:192, :] for b in blocks], axis=1)

    def tile(i, unused):
        at = pl.ds(pl.multiple_of(i * QT, QT), QT)
        s = jnp.dot(k_s[...], q_s[:, at], preferred_element_type=jnp.float32)
        peak = jnp.max(fold_rows(s, jnp.maximum), axis=0, keepdims=True)
        e = jnp.exp(s - peak)
        denom = jnp.sum(fold_rows(e, jnp.add), axis=0, keepdims=True)
        o = jnp.dot(v_s[...], e.astype(jnp.bfloat16), preferred_element_type=jnp.float32)
        o_ref[0, :, at] = o * (1.0 / denom)
        lse_ref[0, :, at] = peak + jnp.log(denom)
        return unused

    lax.fori_loop(0, n // QT, tile, 0)
    for j, c in enumerate((c0, c1, c2, c3)):
        c[...] = o_ref[0, :, j * size : (j + 1) * size].astype(jnp.bfloat16)

def attn_fwd(seg, blocks):
    size = blocks[0].shape[1]
    n = 4 * size
    heads = blocks[0].shape[0] // 192
    return pl.pallas_call(
        attn_fwd_kernel,
        grid=(heads,),
        in_specs=[pl.BlockSpec((1, n), lambda h: (0, 0))] + [pl.BlockSpec((192, size), lambda h: (h, 0))] * 4,
        out_specs=[pl.BlockSpec((64, size), lambda h: (h, 0))] * 4
        + [pl.BlockSpec((1, 1, n), lambda h: (h, 0, 0)), pl.BlockSpec((1, 64, n), lambda h: (h, 0, 0))],
        out_shape=[jax.ShapeDtypeStruct((heads * 64, size), jnp.bfloat16)] * 4
        + [jax.ShapeDtypeStruct((heads, 1, n), jnp.float32), jax.ShapeDtypeStruct((heads, 64, n), jnp.float32)],
        scratch_shapes=[pltpu.VMEM((n, 128), jnp.bfloat16), pltpu.VMEM((128, n), jnp.bfloat16), pltpu.VMEM((64, n), jnp.bfloat16)],
        compiler_params=pltpu.CompilerParams(vmem_limit_bytes=50 * 2**20),
        cost_estimate=pl.CostEstimate(flops=heads * n * n * 256, bytes_accessed=6_000_000, transcendentals=heads * n * n),
    )(seg, *blocks)

def attn_bwd_kernel(seg_ref, b0, b1, b2, b3, d0, d1, d2, d3, lse_ref, o_ref, g0, g1, g2, g3, k_s, q_s, v_s, kt_s, do_s, dk_s, dv_s, dq_s):
    blocks = (b0, b1, b2, b3)
    n = seg_ref.shape[1]
    size = b0.shape[1]
    fill_keys(seg_ref, blocks, k_s, q_s)
    v_s[...] = jnp.transpose(jnp.concatenate([b[128:192, :] for b in blocks], axis=1).astype(jnp.float32)).astype(jnp.bfloat16)
    kt_s[...] = jnp.concatenate([b[64:128, :] for b in blocks], axis=1)
    do_s[...] = jnp.concatenate([d[...] for d in (d0, d1, d2, d3)], axis=1)
    dk_s[...] = jnp.zeros_like(dk_s)
    dv_s[...] = jnp.zeros_like(dv_s)

    def tile(i, unused):
        at = pl.ds(pl.multiple_of(i * QT, QT), QT)
        q = q_s[:, at]
        do = do_s[:, at]
        delta = jnp.sum(do.astype(jnp.float32) * o_ref[0, :, at], axis=0, keepdims=True)
        s = jnp.dot(k_s[...], q, preferred_element_type=jnp.float32)
        p = jnp.exp(s - lse_ref[0, :, at])
        dp = jnp.dot(v_s[...], do, preferred_element_type=jnp.float32)
        ds = (p * (dp - delta)).astype(jnp.bfloat16)
        p = p.astype(jnp.bfloat16)
        nt = (((1,), (1,)), ((), ()))
        dv_s[...] += lax.dot_general(do, p, nt, preferred_element_type=jnp.float32)
        dk_s[...] += lax.dot_general(q[:64], ds, nt, preferred_element_type=jnp.float32)
        dq_s[:, at] = jnp.dot(kt_s[...], ds, preferred_element_type=jnp.float32) * 0.125
        return unused

    lax.fori_loop(0, n // QT, tile, 0)
    for j, g in enumerate((g0, g1, g2, g3)):
        span = slice(j * size, (j + 1) * size)
        g[0:64, :] = dq_s[:, span].astype(jnp.bfloat16)
        g[64:128, :] = dk_s[:, span].astype(jnp.bfloat16)
        g[128:192, :] = dv_s[:, span].astype(jnp.bfloat16)

def attn_bwd(seg, blocks, grads, lse, o):
    size = blocks[0].shape[1]
    n = 4 * size
    heads = blocks[0].shape[0] // 192
    return pl.pallas_call(
        attn_bwd_kernel,
        grid=(heads,),
        in_specs=[pl.BlockSpec((1, n), lambda h: (0, 0))] + [pl.BlockSpec((192, size), lambda h: (h, 0))] * 4
        + [pl.BlockSpec((64, size), lambda h: (h, 0))] * 4
        + [pl.BlockSpec((1, 1, n), lambda h: (h, 0, 0)), pl.BlockSpec((1, 64, n), lambda h: (h, 0, 0))],
        out_specs=[pl.BlockSpec((192, size), lambda h: (h, 0))] * 4,
        out_shape=[jax.ShapeDtypeStruct((heads * 192, size), jnp.bfloat16)] * 4,
        scratch_shapes=[pltpu.VMEM((n, 128), jnp.bfloat16), pltpu.VMEM((128, n), jnp.bfloat16), pltpu.VMEM((n, 64), jnp.bfloat16),
                        pltpu.VMEM((64, n), jnp.bfloat16), pltpu.VMEM((64, n), jnp.bfloat16),
                        pltpu.VMEM((64, n), jnp.float32), pltpu.VMEM((64, n), jnp.float32), pltpu.VMEM((64, n), jnp.float32)],
        compiler_params=pltpu.CompilerParams(vmem_limit_bytes=50 * 2**20),
        cost_estimate=pl.CostEstimate(flops=heads * n * n * 640, bytes_accessed=10_000_000, transcendentals=heads * n * n),
    )(seg, *blocks, *grads, lse, o)


MESH = pl.DeviceIdType.MESH
EVERY = slice(None)


def spot():
    seq, head = lax.axis_index("seq"), lax.axis_index("head")
    return seq // 2, seq % 2, head // 2, head % 2


def device(z, x, y, c):
    return {"seq": z * 2 + x, "head": y * 2 + c}


def hail(where):
    pl.semaphore_signal(pltpu.get_barrier_semaphore(), inc=1, device_id=where, device_id_type=MESH)


def greet(plane=False, group=False, halo=False):
    z, x, y, c = spot()
    if plane:
        for n in range(1, 8):
            hail(device(z, x ^ (n >> 2), y ^ ((n >> 1) & 1), c ^ (n & 1)))
        for n in range(1, 4):
            hail(device(z ^ n, x, y, c))
        pl.semaphore_wait(pltpu.get_barrier_semaphore(), 10)
        return
    count = jnp.where((z == 0) | (z == 3), 4, 5)
    hail(device(z, x, y, 1 - c))
    hail(device(z, x, 1 - y, c))
    hail(device(z, 1 - x, y, c))
    pl.when(z > 0)(lambda: hail(device(z - 1, x, y, c)))
    pl.when(z < 3)(lambda: hail(device(z + 1, x, y, c)))
    if group:
        hail(device(z, x, 1 - y, 1 - c))
        count = count + 1
    elif halo:
        far = y != c
        pl.when(far)(lambda: hail(device(z, x, 1 - y, 1 - c)))
        count = count + jnp.where(far, 1, 0)
    pl.semaphore_wait(pltpu.get_barrier_semaphore(), count)


class Unit:
    def remote(self, src, dst, n, to):
        return pltpu.make_async_remote_copy(
            src_ref=src, dst_ref=dst, send_sem=self.send.at[n], recv_sem=self.recv.at[n], device_id=to, device_id_type=MESH
        )

    def landed(self, ref, n):
        z, x, y, c = spot()
        return self.remote(ref, ref, n, device(z, x, y, 1 - c))


class Spread(Unit):
    def __init__(self, own, whole, cut, order, send, recv):
        self.own, self.whole, self.cut, self.order, self.send, self.recv = own, whole, cut, order, send, recv
        self.steps = []
        for at, axis in enumerate(order):
            self.steps += [("z", 1), ("z", 2), ("z", 3)] if axis == "z" else [(axis, at)]
        self.steps.append(("c", 3))

    def block(self, at, **given):
        z, x, y, c = spot()
        here = {"z": z, "x": x, "y": y, "c": c}
        done = self.order[:at]
        lead = tuple(given[a] if a in given else (EVERY if a in done else here[a]) for a in "zxyc")
        return self.whole.at[lead + self.cut]

    def source(self, at, ref):
        return self.own.at[self.cut] if at == 0 and self.cut else (self.own if at == 0 else ref)

    def up(self, k):
        z, x, y, c = spot()
        at = self.order.index("z")
        ref = self.block(at, z=z - (k - 1))
        src = self.source(at, ref) if k == 1 else ref
        return (z < 3) & (z >= k - 1), self.remote(src, ref, k - 1, device(z + 1, x, y, c))

    def down(self, k):
        z, x, y, c = spot()
        at = self.order.index("z")
        ref = self.block(at, z=z + (k - 1))
        src = self.source(at, ref) if k == 1 else ref
        return (z > 0) & (z + k - 1 <= 3), self.remote(src, ref, 2 + k, device(z - 1, x, y, c))

    def came_up(self, k):
        z, x, y, c = spot()
        ref = self.block(self.order.index("z"), z=z - k)
        return z >= k, self.landed(ref, k - 1)

    def came_down(self, k):
        z, x, y, c = spot()
        ref = self.block(self.order.index("z"), z=z + k)
        return z + k <= 3, self.landed(ref, 2 + k)

    def swap(self, axis, at):
        z, x, y, c = spot()
        ref = self.block(at)
        to = {"x": device(z, 1 - x, y, c), "y": device(z, x, 1 - y, c), "c": device(z, x, y, 1 - c)}[axis]
        return self.remote(self.source(at, ref), ref, 6 + "xyc".index(axis), to)

    def came_over(self, axis, at):
        z, x, y, c = spot()
        other = {"x": 1 - x, "y": 1 - y, "c": 1 - c}[axis]
        return self.landed(self.block(at, **{axis: other}), 6 + "xyc".index(axis))

    def start(self, step):
        axis, k = step
        if axis == "z":
            for ok, copy in (self.up(k), self.down(k)):
                pl.when(ok)(copy.start)
        else:
            self.swap(axis, k).start()

    def end(self, step):
        axis, k = step
        if axis == "z":
            for ok, copy in (self.came_up(k), self.came_down(k)):
                pl.when(ok)(copy.wait_recv)
        else:
            self.came_over(axis, k).wait_recv()

    def stage(self, n):
        z, x, y, c = spot()
        if n < 2:
            local = pltpu.make_async_copy(self.source(0, None), self.block(0), self.recv.at[9])
            local.start() if n == 0 else local.wait()
        if n > 0:
            self.end(self.steps[n - 1])
        if n < len(self.steps):
            self.start(self.steps[n])

    stages = 7

    def finish(self):
        for axis, k in self.steps:
            if axis == "z":
                for ok, copy in (self.up(k), self.down(k)):
                    pl.when(ok)(copy.wait_send)
            else:
                self.swap(axis, k).wait_send()


def add_rows(dst, src):
    dst[...] = (dst[...].astype(jnp.float32) + src[...].astype(jnp.float32)).astype(dst.dtype)


class Collect(Unit):
    def __init__(self, parts, out, cut, order, own, rc, r1, r2, rz, send, recv):
        self.parts, self.out, self.cut, self.order, self.send, self.recv = parts, out, cut, order, send, recv
        self.own, self.rc, self.r1, self.r2, self.rz = own, rc, r1, r2, rz
        self.steps = [("c", 0)]
        for at, axis in enumerate(order):
            self.steps += [("z", 1), ("z", 2), ("z", 3)] if axis == "z" else [(axis, at)]

    def block(self, *lead):
        if self.own is None:
            z, x, y, c = spot()
            return self.parts.at[tuple(lead) + (c,) + self.cut]
        return self.own.at[tuple(lead)]

    def lead(self, at, **given):
        z, x, y, c = spot()
        here = {"z": z, "x": x, "y": y}
        done = self.order[:at]
        return tuple(given[a] if a in given else (here[a] if a in done else EVERY) for a in "zxy")

    def swap(self, axis, at):
        z, x, y, c = spot()
        if axis == "c":
            return self.remote(self.parts.at[(EVERY, EVERY, EVERY, 1 - c) + self.cut], self.rc, 0, device(z, x, y, 1 - c))
        other = {"x": 1 - x, "y": 1 - y}[axis]
        to = {"x": device(z, 1 - x, y, c), "y": device(z, x, 1 - y, c)}[axis]
        return self.remote(self.block(*self.lead(at, **{axis: other})), self.r1 if at == 0 else self.r2, 1 + min(at, 1), to)

    def load(self):
        z, x, y, c = spot()
        return pltpu.make_async_copy(self.parts.at[(EVERY, EVERY, EVERY, c) + self.cut], self.own, self.recv.at[9])

    def hop(self, k, rising):
        z, x, y, c = spot()
        at = self.order.index("z")
        d = z + (4 - k) if rising else z - (4 - k)
        ok = d <= 3 if rising else d >= 0
        slot = 2 + k if rising else k - 1
        to = device(z + 1, x, y, c) if rising else device(z - 1, x, y, c)
        return ok, self.remote(self.block(*self.lead(at, z=jnp.clip(d, 0, 3))), self.rz.at[slot], 3 + slot, to)

    def hopped(self, k, rising):
        z, x, y, c = spot()
        d = z + (3 - k) if rising else z - (3 - k)
        ok = (z > 0) & (d <= 3) if rising else (z < 3) & (d >= 0)
        slot = 2 + k if rising else k - 1
        return ok, jnp.clip(d, 0, 3), self.rz.at[slot], self.landed(self.rz.at[slot], 3 + slot)

    def start(self, step):
        axis, k = step
        if axis == "z":
            for rising in (False, True):
                ok, copy = self.hop(k, rising)
                pl.when(ok)(copy.start)
        else:
            self.swap(axis, k).start()
            if axis == "c" and self.own is not None:
                self.load().start()

    def end(self, step, last):
        z, x, y, c = spot()
        axis, k = step
        if axis == "z":
            at = self.order.index("z")
            pair = "x" if "x" not in self.order[:at] else ("y" if "y" not in self.order[:at] else None)
            for rising in (False, True):
                ok, d, ref, copy = self.hopped(k, rising)

                @pl.when(ok)
                def _(d=d, ref=ref, copy=copy):
                    copy.wait_recv()
                    for n in range(2 if pair else 1):
                        given = {"z": d, pair: n} if pair else {"z": d}
                        add_rows(self.block(*self.lead(at, **given)), ref.at[n] if pair else ref)
        elif axis == "c":
            self.landed(self.rc, 0).wait_recv()
            if self.own is not None:
                self.load().wait()

            def one(i, unused):
                for n in range(2):
                    for m in range(2):
                        add_rows(self.block(i, n, m), self.rc.at[i, n, m])
                return unused

            lax.fori_loop(0, 4, one, 0)
        else:
            ref = self.r1 if k == 0 else self.r2
            self.landed(ref, 1 + min(k, 1)).wait_recv()
            here = {"x": x, "y": y}[axis]
            rest = [a for a in "zxy" if a not in self.order[: k + 1]]
            if not rest:
                add_rows(self.block(z, x, y), ref)
            else:

                def one(i, unused):
                    for n in range(2 if len(rest) == 2 else 1):
                        given = {"z": i, axis: here}
                        if len(rest) == 2:
                            given[rest[1]] = n
                        add_rows(self.block(*self.lead(k, **given)), ref.at[i, n] if len(rest) == 2 else ref.at[i])
                    return unused

                lax.fori_loop(0, 4, one, 0)
        if last:
            out = self.out.at[self.cut] if self.cut else self.out
            out[...] = self.block(z, x, y)[...].astype(jnp.float32)

    stages = 7

    def stage(self, n):
        if n > 0:
            self.end(self.steps[n - 1], n == len(self.steps))
        if n < len(self.steps):
            self.start(self.steps[n])

    def finish(self):
        for axis, k in self.steps:
            if axis == "z":
                for rising in (False, True):
                    ok, copy = self.hop(k, rising)
                    pl.when(ok)(copy.wait_send)
            else:
                self.swap(axis, k).wait_send()


def unit_shape(shape, cut):
    cut = tuple(cut) + (slice(None),) * (len(shape) - len(cut))
    return tuple(len(range(*s.indices(d))) for s, d in zip(cut, shape))


def collect_scratch(plan, shapes, dtype, inside):
    scratch = []
    for i, cut, order in plan:
        m = unit_shape(shapes[i], cut)
        leads = [] if i in inside else [(4, 2, 2)]
        leads += [(4, 2, 2), (4, 2), () if order[1] == "z" else (4,), (6, 2) if order[1] == "z" else (6,)]
        scratch += [pltpu.VMEM(lead + m, dtype) for lead in leads]
    return scratch


def collect_units(plan, parts, outs, bufs, inside, send, recv):
    units, bufs = [], list(bufs)
    for n, (i, cut, order) in enumerate(plan):
        own = None if i in inside else bufs.pop(0)
        units.append(Collect(parts[i], outs[i], cut, order, own, bufs.pop(0), bufs.pop(0), bufs.pop(0), bufs.pop(0), send.at[n], recv.at[n]))
    return units


def waves(units, width=2):
    rows = [units[i : i + width] for i in range(0, len(units), width)]
    steps = []
    for t in range(len(rows) + 6):
        steps.append([(unit, n) for n in (3, 4, 5, 6, 2, 1, 0) if 0 <= t - n < len(rows) for unit in rows[t - n]])
    return steps


def go(step):
    for unit, n in step:
        unit.stage(n)


def square_sum(refs, tile):
    tile[...] = jnp.zeros_like(tile)
    for ref in refs:
        v = ref[...]
        v = (v * v).reshape(-1, v.shape[-1])
        v = jnp.sum(v.reshape(-1, 8, v.shape[-1]), axis=0)
        for i in range(0, v.shape[-1], 128):
            tile[...] += v[:, i : i + 128]


def total_square(norm, tiles, send, recv):
    z, x, y, c = spot()
    mine = x * 4 + y * 2 + c
    copies = []

    def push(slot, n, to):
        copies.append(pltpu.make_async_remote_copy(
            src_ref=tiles.at[slot], dst_ref=tiles.at[slot], send_sem=send.at[n], recv_sem=recv.at[n], device_id=to, device_id_type=MESH))
        copies[-1].start()

    def pull(slot, n):
        ref = tiles.at[slot]
        pltpu.make_async_remote_copy(
            src_ref=ref, dst_ref=ref, send_sem=send.at[n], recv_sem=recv.at[n], device_id=device(z, x, y, 1 - c), device_id_type=MESH).wait_recv()

    for n in range(1, 8):
        push(mine, n, device(z, x ^ (n >> 2), y ^ ((n >> 1) & 1), c ^ (n & 1)))
    for n in range(1, 8):
        pull(mine ^ n, n)
    total = tiles[0]
    for n in range(1, 8):
        total = total + tiles[n]
    tiles[8 + z] = total
    for n in range(1, 4):
        push(8 + z, 7 + n, device(z ^ n, x, y, c))
    for n in range(1, 4):
        pull(8 + (z ^ n), 7 + n)
    norm[...] = (tiles[8] + tiles[9]) + (tiles[10] + tiles[11])
    for copy in copies:
        copy.wait_send()


def take_rows(win_ref, g, cut):
    return gapped(take_group(win_ref, g), cut)


def halo_copies(edges_ref, win_ref, send, recv):
    z, x, y, c = spot()
    h = y * 2 + c
    n = edges_ref.shape[0]

    def to(other):
        return {"seq": z * 2 + x, "head": other}

    def copy(src, dst, k, other):
        return pltpu.make_async_remote_copy(
            src_ref=src, dst_ref=dst, send_sem=send.at[k], recv_sem=recv.at[k], device_id=to(other), device_id_type=MESH)

    after = copy(edges_ref.at[n - HALF : n], win_ref.at[0:HALF], 0, h + 1)
    before = copy(edges_ref.at[0:HALF], win_ref.at[n + HALF : n + 2 * HALF], 1, h - 1)
    from_before = copy(win_ref.at[0:HALF], win_ref.at[0:HALF], 0, h ^ 1)
    from_after = copy(win_ref.at[n + HALF : n + 2 * HALF], win_ref.at[n + HALF : n + 2 * HALF], 1, h ^ 1)
    return (h < 3, after), (h > 0, before), (h > 0, from_before), (h < 3, from_after)


def halo_start(edges_ref, win_ref, send, recv):
    for ok, copy in halo_copies(edges_ref, win_ref, send, recv)[:2]:
        pl.when(ok)(copy.start)


def halo_end(edges_ref, win_ref, send, recv):
    n = edges_ref.shape[0]
    after, before, from_before, from_after = halo_copies(edges_ref, win_ref, send, recv)
    for (ok, copy), rows in ((from_before, slice(0, HALF)), (from_after, slice(n + HALF, n + 2 * HALF))):
        pl.when(ok)(copy.wait_recv)

        @pl.when(jnp.logical_not(ok))
        def _(rows=rows):
            win_ref[rows, :] = jnp.zeros((HALF, win_ref.shape[1]), win_ref.dtype)

    for ok, copy in (after, before):
        pl.when(ok)(copy.wait_send)


def open_kernel(plan, n_in, early, *refs):
    cut_ref, frames_ref = refs[:2]
    owns = refs[2 : 2 + n_in]
    out_ref, win_ref = refs[2 + n_in : 4 + n_in]
    wholes = refs[4 + n_in : 4 + 2 * n_in]
    cols_s, low_s, w_s, wp_s, send, recv, hsend, hrecv, wsem = refs[4 + 2 * n_in :]
    cut = cut_ref[0]
    greet(halo=True)
    halo_start(frames_ref, win_ref, hsend, hrecv)
    units = [Spread(owns[i], wholes[i], where, order, send.at[n], recv.at[n]) for n, (i, where, order) in enumerate(plan)]
    steps = waves(units)
    go(steps[0])
    win_ref[HALF : HALF + OWN, :] = frames_ref[...]
    out_ref[...] = jnp.zeros_like(out_ref)
    wp_s[...] = jnp.zeros_like(wp_s)
    go(steps[1])
    halo_end(frames_ref, win_ref, hsend, hrecv)

    def columns(g, unused):
        cols_s[g] = im2col(take_rows(win_ref, g, cut), ZROWS)
        return unused

    def load(half, z):
        return pltpu.make_async_copy(wholes[0].at[z, :, :, :, 4 * half : 4 * half + 4], w_s.at[z], wsem.at[z])

    def product(g):
        z, x, y = g // 4, (g // 2) % 2, g % 2
        for h in range(2):
            for a in range(4):
                wp_s[h * 128 + a * 32 : h * 128 + a * 32 + 24, :] = w_s[z, x, y, h, a]
        return lax.dot_general(cols_s[g], wp_s[...], (((1,), (1,)), ((), ())), preferred_element_type=jnp.float32)

    def low(g, unused):
        low_s[g] = product(g)
        return unused

    def high(g, unused):
        z = jnp.concatenate([low_s[g], product(g)], axis=1)
        z = jnp.concatenate([z[:, 0:128], z[:, 256:384], z[:, 128:256], z[:, 384:512]], axis=1)
        put_group(out_ref, g, pick_own(fold_out(z), cut))
        return unused

    t = 2
    for chunk in range(4):
        lax.fori_loop(4 * chunk, 4 * chunk + 4, columns, 0)
        go(steps[t])
        t += 1
    done = 0
    while t < len(steps) or done < 2:
        if done < 2 and t - 1 - 6 >= early[done]:
            for z in range(4):
                load(done, z).start()
            for z in range(4):
                load(done, z).wait()
                lax.fori_loop(4 * z, 4 * z + 4, (low, high)[done], 0)
                if t < len(steps) and z % 2 == 1:
                    go(steps[t])
                    t += 1
            done += 1
        elif t < len(steps):
            go(steps[t])
            t += 1
    for unit in units:
        unit.finish()


def open_step(cut, frames, shards, plan, early, collective_id=1):
    n = len(shards)
    vmem = pl.BlockSpec(memory_space=pltpu.VMEM)
    anywhere = pl.BlockSpec(memory_space=pl.ANY)
    return pl.pallas_call(
        functools.partial(open_kernel, plan, n, early),
        in_specs=[pl.BlockSpec(memory_space=pltpu.SMEM), vmem] + [anywhere] * n,
        out_specs=[vmem, vmem] + [anywhere] * n,
        out_shape=[jax.ShapeDtypeStruct((OWN, 768), jnp.float32), jax.ShapeDtypeStruct((WIN, 768), jnp.bfloat16)]
        + [jax.ShapeDtypeStruct((4, 2, 2, 2) + s.shape, s.dtype) for s in shards],
        scratch_shapes=[
            pltpu.VMEM((16, ZROWS, 768), jnp.bfloat16),
            pltpu.VMEM((16, ZROWS, 256), jnp.float32),
            pltpu.VMEM((4, 2, 2, 2, 4, 24, 768), jnp.bfloat16),
            pltpu.VMEM((256, 768), jnp.bfloat16),
            pltpu.SemaphoreType.DMA((len(plan), 9)),
            pltpu.SemaphoreType.DMA((len(plan), 10)),
            pltpu.SemaphoreType.DMA((2,)),
            pltpu.SemaphoreType.DMA((2,)),
            pltpu.SemaphoreType.DMA((4,)),
        ],
        compiler_params=pltpu.CompilerParams(collective_id=collective_id, has_side_effects=True, vmem_limit_bytes=56 * 2**20),
    )(cut, frames, *shards)


HEADS_HERE = 3
ROWS_HERE = 192 * HEADS_HERE


def group_copy(src, dst, send, recv, other):
    return pltpu.make_async_remote_copy(
        src_ref=src, dst_ref=dst, send_sem=send, recv_sem=recv, device_id={"head": other}, device_id_type=MESH
    )


def spaced(steps, slots):
    out = [[] for _ in range(slots)]
    for t, step in enumerate(steps):
        out[min(t * slots // max(len(steps), 1), slots - 1)].append(step)
    return out


def go_at(slot, by_slot):
    for t, steps in enumerate(by_slot):
        if steps:

            @pl.when(slot == t)
            def _(steps=steps):
                for step in steps:
                    go(step)


def fill_heads(seg_ref, qkv_ref, h, k_s, q_s):
    n = seg_ref.shape[1]
    seg = seg_ref[...]
    row = lax.broadcasted_iota(jnp.int32, (64, n), 0)
    mark = jnp.where(row < 2, jnp.where(seg == row, 1.0, 0.0), 0.0)
    push = jnp.where(row < 2, jnp.where(seg == row, 0.0, FAR), 0.0)
    at = pl.multiple_of(h * 192, 64)
    keys = qkv_ref[pl.ds(at + 64, 64), :].astype(jnp.float32)
    k_s[...] = jnp.transpose(jnp.concatenate([keys, mark], axis=0)).astype(jnp.bfloat16)
    queries = qkv_ref[pl.ds(at, 64), :].astype(jnp.float32) * 0.125
    q_s[...] = jnp.concatenate([queries, push], axis=0).astype(jnp.bfloat16)


def attend_kernel(plan, n_in, *refs):
    seg_ref, packed_ref = refs[:2]
    owns = refs[2 : 2 + n_in]
    qkv_ref, ctx_ref, lse_ref, o_ref = refs[2 + n_in : 6 + n_in]
    wholes = refs[6 + n_in : 6 + 2 * n_in]
    k_s, q_s, ctx_s, asend, arecv, csend, crecv, osem, send, recv = refs[6 + 2 * n_in :]
    z, x, y, c = spot()
    me = y * 2 + c
    size = packed_ref.shape[1]
    greet(group=True)

    def bring(h, d):
        return group_copy(
            packed_ref.at[pl.ds((me ^ d) * ROWS_HERE + h * 192, 192)],
            qkv_ref.at[pl.ds(h * 192, 192), d * size : d * size + size],
            asend.at[h, d - 1], arecv.at[h, d - 1], me ^ d,
        )

    def give(h, d):
        return group_copy(
            ctx_s.at[pl.ds(h * 64, 64), d * size : d * size + size],
            ctx_ref.at[pl.ds(me * 64 * HEADS_HERE + h * 64, 64)],
            csend.at[h, d - 1], crecv.at[h, d - 1], me ^ d,
        )

    def given(h, d):
        ref = ctx_ref.at[pl.ds((me ^ d) * 64 * HEADS_HERE + h * 64, 64)]
        return group_copy(ref, ref, csend.at[h, d - 1], crecv.at[h, d - 1], me ^ d)

    own = pltpu.make_async_copy(packed_ref.at[pl.ds(me * ROWS_HERE, ROWS_HERE)], qkv_ref.at[:, 0:size], osem)
    own.start()
    for h in range(HEADS_HERE):
        for d in (2, 3, 1):
            bring(h, d).start()
    units = [Spread(owns[i], wholes[i], where, order, send.at[n], recv.at[n]) for n, (i, where, order) in enumerate(plan)]
    steps = waves(units)
    go(steps[0])
    tiles = 4 * size // QF
    by_slot = spaced(steps[1:], HEADS_HERE * tiles)
    own.wait()

    def head(h, unused):
        for d in (1, 2, 3):
            bring(h, d).wait_recv()
        fill_heads(seg_ref, qkv_ref, h, k_s, q_s)

        def tile(i, unused):
            at = pl.ds(pl.multiple_of(i * QF, QF), QF)
            s = jnp.dot(k_s[...], q_s[:, at], preferred_element_type=jnp.float32)
            peak = jnp.max(fold_rows(s, jnp.maximum), axis=0, keepdims=True)
            e = jnp.exp(s - peak)
            denom = jnp.sum(fold_rows(e, jnp.add), axis=0, keepdims=True)
            values = qkv_ref[pl.ds(pl.multiple_of(h * 192 + 128, 64), 64), :]
            o = jnp.dot(values, e.astype(jnp.bfloat16), preferred_element_type=jnp.float32) * (1.0 / denom)
            rows = pl.ds(pl.multiple_of(h * 64, 64), 64)
            o_ref[rows, at] = o
            ctx_s[rows, at] = o.astype(jnp.bfloat16)
            lse_ref[h, :, at] = peak + jnp.log(denom)
            go_at(h * tiles + i, by_slot)
            return unused

        lax.fori_loop(0, tiles, tile, 0)
        for d in (2, 3, 1):
            give(h, d).start()
        ctx_ref[pl.ds(pl.multiple_of(me * 64 * HEADS_HERE + h * 64, 64), 64), :] = ctx_s[pl.ds(pl.multiple_of(h * 64, 64), 64), 0:size]
        return unused

    lax.fori_loop(0, HEADS_HERE, head, 0)
    for h in range(HEADS_HERE):
        for d in (1, 2, 3):
            given(h, d).wait_recv()
            give(h, d).wait_send()
            bring(h, d).wait_send()
    for unit in units:
        unit.finish()


def attend(seg, packed, shards, plan, collective_id=3):
    n = len(shards)
    size = packed.shape[1]
    vmem = pl.BlockSpec(memory_space=pltpu.VMEM)
    anywhere = pl.BlockSpec(memory_space=pl.ANY)
    sem = pltpu.SemaphoreType.DMA
    return pl.pallas_call(
        functools.partial(attend_kernel, plan, n),
        in_specs=[vmem, anywhere] + [anywhere] * n,
        out_specs=[vmem] * 4 + [anywhere] * n,
        out_shape=[
            jax.ShapeDtypeStruct((ROWS_HERE, 4 * size), jnp.bfloat16),
            jax.ShapeDtypeStruct((768, size), jnp.bfloat16),
            jax.ShapeDtypeStruct((HEADS_HERE, 1, 4 * size), jnp.float32),
            jax.ShapeDtypeStruct((64 * HEADS_HERE, 4 * size), jnp.float32),
        ]
        + [jax.ShapeDtypeStruct((4, 2, 2, 2) + s.shape, s.dtype) for s in shards],
        scratch_shapes=[
            pltpu.VMEM((4 * size, 128), jnp.bfloat16),
            pltpu.VMEM((128, 4 * size), jnp.bfloat16),
            pltpu.VMEM((64 * HEADS_HERE, 4 * size), jnp.bfloat16),
            sem((3, 3)), sem((3, 3)), sem((3, 3)), sem((3, 3)), sem,
            sem((max(len(plan), 1), 9)), sem((max(len(plan), 1), 10)),
        ],
        compiler_params=pltpu.CompilerParams(collective_id=collective_id, has_side_effects=True, vmem_limit_bytes=50 * 2**20),
    )(seg, packed, *shards)


def attend_back_kernel(plan, n_in, *refs):
    seg_ref, qkv_ref, lse_ref, o_ref, gc_ref = refs[:5]
    parts = refs[5 : 5 + n_in]
    gp_ref, norm_ref = refs[5 + n_in : 7 + n_in]
    outs = refs[7 + n_in : 7 + 2 * n_in]
    k_s, q_s, v_s, do_s, dk_s, dv_s, dq_s, gp_s, asend, arecv, csend, crecv, osem, send, recv = refs[7 + 2 * n_in : 22 + 2 * n_in]
    bufs = refs[22 + 2 * n_in :]
    z, x, y, c = spot()
    me = y * 2 + c
    size = gc_ref.shape[1]
    greet(group=True)

    def bring(h, d):
        return group_copy(
            gc_ref.at[pl.ds((me ^ d) * 64 * HEADS_HERE + h * 64, 64)],
            do_s.at[pl.ds(h * 64, 64), d * size : d * size + size],
            asend.at[h, d - 1], arecv.at[h, d - 1], me ^ d,
        )

    def give(h, d):
        return group_copy(
            gp_s.at[pl.ds(h * 192, 192), d * size : d * size + size],
            gp_ref.at[pl.ds(me * ROWS_HERE + h * 192, 192)],
            csend.at[h, d - 1], crecv.at[h, d - 1], me ^ d,
        )

    def given(h, d):
        ref = gp_ref.at[pl.ds((me ^ d) * ROWS_HERE + h * 192, 192)]
        return group_copy(ref, ref, csend.at[h, d - 1], crecv.at[h, d - 1], me ^ d)

    own = pltpu.make_async_copy(gc_ref.at[pl.ds(me * 64 * HEADS_HERE, 64 * HEADS_HERE)], do_s.at[:, 0:size], osem)
    own.start()
    for h in range(HEADS_HERE):
        for d in (2, 3, 1):
            bring(h, d).start()
    units = collect_units(plan, parts, outs, bufs, (), send, recv)
    steps = waves(units)
    go(steps[0])
    tiles = 4 * size // QT
    by_slot = spaced(steps[1:], HEADS_HERE * tiles)
    own.wait()

    def head(h, unused):
        for d in (1, 2, 3):
            bring(h, d).wait_recv()
        fill_heads(seg_ref, qkv_ref, h, k_s, q_s)
        first = pl.multiple_of(h * 192, 64)
        v_s[...] = jnp.transpose(qkv_ref[pl.ds(first + 128, 64), :].astype(jnp.float32)).astype(jnp.bfloat16)
        dk_s[...] = jnp.zeros_like(dk_s)
        dv_s[...] = jnp.zeros_like(dv_s)
        rows = pl.ds(pl.multiple_of(h * 64, 64), 64)

        def tile(i, unused):
            at = pl.ds(pl.multiple_of(i * QT, QT), QT)
            q = q_s[:, at]
            do = do_s[rows, at]
            delta = jnp.sum(do.astype(jnp.float32) * o_ref[rows, at], axis=0, keepdims=True)
            s = jnp.dot(k_s[...], q, preferred_element_type=jnp.float32)
            p = jnp.exp(s - lse_ref[h, :, at])
            dp = jnp.dot(v_s[...], do, preferred_element_type=jnp.float32)
            ds = (p * (dp - delta)).astype(jnp.bfloat16)
            p = p.astype(jnp.bfloat16)
            nt = (((1,), (1,)), ((), ()))
            dv_s[...] += lax.dot_general(do, p, nt, preferred_element_type=jnp.float32)
            dk_s[...] += lax.dot_general(q[:64], ds, nt, preferred_element_type=jnp.float32)
            dq_s[:, at] = jnp.dot(qkv_ref[pl.ds(first + 64, 64), :], ds, preferred_element_type=jnp.float32) * 0.125
            go_at(h * tiles + i, by_slot)
            return unused

        lax.fori_loop(0, tiles, tile, 0)
        gp_s[pl.ds(first, 64), :] = dq_s[...].astype(jnp.bfloat16)
        gp_s[pl.ds(first + 64, 64), :] = dk_s[...].astype(jnp.bfloat16)
        gp_s[pl.ds(first + 128, 64), :] = dv_s[...].astype(jnp.bfloat16)
        for d in (2, 3, 1):
            give(h, d).start()
        gp_ref[pl.ds(pl.multiple_of(me * ROWS_HERE + h * 192, 64), 192), :] = gp_s[pl.ds(first, 192), 0:size]
        return unused

    lax.fori_loop(0, HEADS_HERE, head, 0)
    for h in range(HEADS_HERE):
        for d in (1, 2, 3):
            given(h, d).wait_recv()
            give(h, d).wait_send()
            bring(h, d).wait_send()
    for unit in units:
        unit.finish()
    square_sum(outs, norm_ref)


def attend_back(seg, qkv, lse, o, gc, parts, plan, collective_id=4):
    n = len(parts)
    size = gc.shape[1]
    shapes = [p.shape[4:] for p in parts]
    vmem = pl.BlockSpec(memory_space=pltpu.VMEM)
    anywhere = pl.BlockSpec(memory_space=pl.ANY)
    sem = pltpu.SemaphoreType.DMA
    return pl.pallas_call(
        functools.partial(attend_back_kernel, plan, n),
        in_specs=[vmem] * 4 + [anywhere] + [anywhere] * n,
        out_specs=[vmem] * 2 + [vmem] * n,
        out_shape=[jax.ShapeDtypeStruct((4 * ROWS_HERE, size), jnp.bfloat16), jax.ShapeDtypeStruct((8, 128), jnp.float32)]
        + [jax.ShapeDtypeStruct(s, jnp.float32) for s in shapes],
        scratch_shapes=[
            pltpu.VMEM((4 * size, 128), jnp.bfloat16),
            pltpu.VMEM((128, 4 * size), jnp.bfloat16),
            pltpu.VMEM((4 * size, 64), jnp.bfloat16),
            pltpu.VMEM((64 * HEADS_HERE, 4 * size), jnp.bfloat16),
            pltpu.VMEM((64, 4 * size), jnp.float32),
            pltpu.VMEM((64, 4 * size), jnp.float32),
            pltpu.VMEM((64, 4 * size), jnp.float32),
            pltpu.VMEM((ROWS_HERE, 4 * size), jnp.bfloat16),
            sem((3, 3)), sem((3, 3)), sem((3, 3)), sem((3, 3)), sem,
            sem((len(plan), 9)), sem((len(plan), 10)),
        ]
        + collect_scratch(plan, shapes, jnp.bfloat16, ()),
        compiler_params=pltpu.CompilerParams(collective_id=collective_id, has_side_effects=True, vmem_limit_bytes=58 * 2**20),
    )(seg, qkv, lse, o, gc, *parts)


def close_kernel(side_plan, main_plan, n_in, *refs):
    cut_ref, win_ref, grad_ref, conv_ref, tile_ref = refs[:5]
    parts = refs[5 : 5 + n_in]
    dx_ref, norm_ref, conv_out = refs[5 + n_in : 8 + n_in]
    outs = refs[8 + n_in : 8 + 2 * n_in]
    (gwin_s, taps_s, dw_s, w_s, wp_s, tiles, send, recv, msend, mrecv, hsend, hrecv, nsend, nrecv, wsem) = refs[8 + 2 * n_in : 23 + 2 * n_in]
    bufs = refs[23 + 2 * n_in :]
    cut, last = cut_ref[0], cut_ref[1]
    greet(plane=True)
    halo_start(grad_ref, gwin_s, hsend, hrecv)
    count = len(collect_scratch(side_plan, [o.shape for o in outs], jnp.bfloat16, ()))
    side = collect_units(side_plan, parts, outs, bufs[:count], (), send, recv)
    main = collect_units(main_plan, [dw_s], [conv_out], bufs[count:], (0,), msend, mrecv)
    side_steps, main_steps = waves(side), waves(main)
    go(side_steps[0])
    gwin_s[HALF : HALF + OWN, :] = grad_ref[...]
    dx_ref[...] = jnp.zeros_like(dx_ref)
    wp_s[...] = jnp.zeros_like(wp_s)
    halo_end(grad_ref, gwin_s, hsend, hrecv)

    def load(z):
        return pltpu.make_async_copy(conv_ref.at[z], w_s.at[z % 2], wsem.at[z % 2])

    load(0).start()
    load(1).start()
    begin = jnp.where(cut <= HALF, 2 * HALF, HALF)
    end = jnp.where(last > 0, EXT, jnp.where(cut <= HALF + OWN, OWN + 2 * HALF, OWN + HALF))

    def weights(g, unused):
        taps = taps_of(take_rows(gwin_s, g, cut))
        taps_s[g] = taps
        row = lax.broadcasted_iota(jnp.int32, (ZROWS, 512), 0) + HALF
        own = jnp.where((row >= begin) & (row < end), taps[HALF : HALF + ZROWS].astype(jnp.float32), 0.0).astype(jnp.bfloat16)
        cols = im2col(take_rows(win_ref, g, cut), ZROWS)
        dw = lax.dot_general(own, cols, (((0,), (0,)), ((), ())), preferred_element_type=jnp.float32).astype(jnp.bfloat16)
        for h in range(2):
            for a in range(8):
                dw_s[g // 4, (g // 2) % 2, g % 2, h, a] = dw[h * 256 + a * 32 : h * 256 + a * 32 + 24]
        return unused

    def inputs(g, unused):
        z, x, y = g // 4, (g // 2) % 2, g % 2
        for h in range(2):
            for a in range(8):
                wp_s[h * 256 + a * 32 : h * 256 + a * 32 + 24, :] = w_s[z % 2, x, y, h, a]
        out = jnp.dot(taps_s[g], wp_s[...], preferred_element_type=jnp.float32)
        put_group(dx_ref, g, pick_own(fold_back(out), cut))
        return unused

    by_slot = spaced(side_steps[1:], 8)
    for k in range(8):
        lax.fori_loop(2 * k, 2 * k + 2, weights, 0)
        for step in by_slot[k]:
            go(step)
    by_slot = spaced(main_steps, 8)
    for k in range(8):
        for step in by_slot[k]:
            go(step)
        if k % 2 == 0:
            load(k // 2).wait()
        lax.fori_loop(2 * k, 2 * k + 2, inputs, 0)
        if k % 2 == 1 and k < 4:
            load(k // 2 + 2).start()
    for unit in side + main:
        unit.finish()
    z, x, y, c = spot()
    mine = tiles.at[x * 4 + y * 2 + c]
    square_sum([conv_out] + list(outs), mine)
    mine[...] += tile_ref[...]
    total_square(norm_ref, tiles, nsend, nrecv)


def close_step(cut, window, grad, conv, tile, parts, side_plan, main_plan, collective_id=2):
    n = len(parts)
    shapes = [p.shape[4:] for p in parts]
    vmem = pl.BlockSpec(memory_space=pltpu.VMEM)
    anywhere = pl.BlockSpec(memory_space=pl.ANY)
    sem = pltpu.SemaphoreType.DMA
    low = jnp.bfloat16
    return pl.pallas_call(
        functools.partial(close_kernel, side_plan, main_plan, n),
        in_specs=[pl.BlockSpec(memory_space=pltpu.SMEM), vmem, vmem, anywhere, vmem] + [anywhere] * n,
        out_specs=[vmem] * (3 + n),
        out_shape=[
            jax.ShapeDtypeStruct((OWN, 768), jnp.float32),
            jax.ShapeDtypeStruct((8, 128), jnp.float32),
            jax.ShapeDtypeStruct(conv.shape[4:], jnp.float32),
        ]
        + [jax.ShapeDtypeStruct(s, jnp.float32) for s in shapes],
        scratch_shapes=[
            pltpu.VMEM((WIN, 768), low),
            pltpu.VMEM((16, EXT, 512), low),
            pltpu.VMEM(conv.shape, low),
            pltpu.VMEM((2,) + conv.shape[1:], low),
            pltpu.VMEM((512, 768), low),
            pltpu.VMEM((12, 8, 128), jnp.float32),
            sem((len(side_plan), 9)), sem((len(side_plan), 10)), sem((len(main_plan), 9)), sem((len(main_plan), 10)),
            sem((2,)), sem((2,)), sem((11,)), sem((11,)), sem((2,)),
        ]
        + collect_scratch(side_plan, shapes, low, ())
        + collect_scratch(main_plan, [conv.shape[4:]], low, (0,)),
        compiler_params=pltpu.CompilerParams(collective_id=collective_id, has_side_effects=True, vmem_limit_bytes=60 * 2**20),
    )(cut, window, grad, conv, tile, *parts)


S = slice


def sliced(index, axis, size, count, orders, first=0):
    step = size // count
    return [
        (index, (S(None),) * axis + (S(step * i, step * i + step),), orders[(first + i) % len(orders)]) for i in range(count)
    ]


GATHER = ("zxy", "zyx", "xzy", "yzx")
REDUCE = ("yxz", "xyz", "yzx", "xzy")


def open_plan():
    return sliced(0, 0, 8, 8, GATHER) + sliced(1, 1, 2304, 2, GATHER) + [(3, (), "zxy"), (2, (), "yzx")]


def attend_plan():
    return sliced(0, 1, 3072, 4, GATHER) + sliced(1, 0, 96, 3, GATHER[1:])


def attend_back_plan():
    return sliced(2, 0, 96, 3, REDUCE) + sliced(1, 1, 3072, 4, REDUCE, 3) + [(0, (), "yxz")]


def side_plan():
    return sliced(0, 1, 2304, 3, REDUCE) + [(1, (), "xyz")]


def main_plan():
    return sliced(0, 0, 8, 8, REDUCE)


def by_chips():
    return lax.axis_size("seq") == 8 and lax.axis_size("head") == 4


def gather_weights(parts):
    return [lax.all_gather(p, ("seq", "head"), axis=0) for p in parts]


def collect_grads(parts):
    outs = [lax.psum_scatter(p.astype(jnp.float32), ("seq", "head"), scatter_dimension=0, tiled=False) for p in parts]
    square = jnp.zeros((), jnp.float32)
    for out in outs:
        square = square + jnp.sum(out * out)
    return outs, lax.psum(square, ("seq", "head"))


def by_owner(part):
    return part.reshape((4, 2, 2, 2) + part.shape[1:])


def trade(pieces):
    count = lax.axis_size("head")
    return [pieces[0]] + [lax.ppermute(pieces[d], "head", [(i, i ^ d) for i in range(count)]) for d in range(1, count)]


def by_partner(stacked):
    me = lax.axis_index("head")
    return [lax.dynamic_index_in_dim(stacked, me ^ d, 0, keepdims=False) for d in range(stacked.shape[0])]


def from_partner(pieces):
    me = lax.axis_index("head")
    stacked = jnp.stack(pieces)
    return jnp.concatenate([lax.dynamic_index_in_dim(stacked, me ^ j, 0, keepdims=False) for j in range(len(pieces))], axis=0)


def shards(
    frames, output_grad, segment_ids, qkv_weight, proj_weight, up_weight, down_weight, conv_weight, bias_gains, ffn_bias,
    qkv_first, proj_first, up_first, down_first, conv_first, bias_gains_first, ffn_bias_first,
    qkv_second, proj_second, up_second, down_second, conv_second, bias_gains_second, ffn_bias_second,
):
    low_type = jnp.bfloat16
    f32 = jnp.float32
    count = lax.axis_size("seq") * lax.axis_size("head")
    row_count, model_width = frames.shape
    head_groups = lax.axis_size("head")
    head_index = lax.axis_index("head")
    kernel_len, conv_rows, group_width = conv_weight.shape
    vec_rows, vec_cols = bias_gains.shape
    ffn_cols = ffn_bias.shape[0]
    conv_low = conv_weight.astype(low_type).reshape(16, 8, conv_rows, group_width).transpose(1, 2, 0, 3).reshape(8, conv_rows, 768)
    small = jnp.concatenate([bias_gains.astype(low_type).reshape(-1), ffn_bias.astype(low_type)])
    small = jnp.pad(small, (0, 2048 - small.shape[0])).reshape(16, 128)
    own_parts = [
        conv_low, qkv_weight.astype(low_type), proj_weight.astype(low_type), up_weight.astype(low_type), down_weight.astype(low_type), small
    ]
    seg_group = segment_ids[0]
    half_kernel = kernel_len // 2
    boundary = jnp.sum((seg_group == 0).astype(jnp.int32))
    cut = jnp.clip(boundary - head_index * row_count + half_kernel, 0, row_count + kernel_len)
    cut = jnp.stack([cut, (head_index == head_groups - 1).astype(jnp.int32)]).astype(jnp.int32)
    if by_chips():
        early = own_parts[:3] + own_parts[5:]
        conv_pre, window, *parts = open_step(cut, frames, early, open_plan(), (1, 3))
        all_conv, all_qkv, all_proj, all_small = [w.reshape((32,) + w.shape[4:]) for w in parts]
        whole_conv = parts[0]
    else:
        all_conv, all_qkv, all_proj, all_up, all_down, all_small = gather_weights(own_parts)
    full_qkv = all_qkv.reshape(model_width, -1)
    full_proj = all_proj.reshape(model_width, -1)
    full_conv = all_conv.reshape(16, 2, 24 // conv_rows, 8, conv_rows, 768).transpose(0, 1, 3, 2, 4, 5).reshape(16, 2, 8, 24, 768)
    all_small = all_small.reshape(count, 2048).astype(f32)
    vectors = all_small[:, : vec_rows * vec_cols].reshape(count, vec_rows, vec_cols).transpose(1, 0, 2).reshape(vec_rows, model_width)
    full_ffn = all_small[:, vec_rows * vec_cols : vec_rows * vec_cols + ffn_cols].reshape(-1)

    seg_rows = jnp.concatenate(by_partner(seg_group.reshape(head_groups, 1, row_count)), axis=1)

    if not by_chips():
        window = with_halo(frames, (("head", 0),), half_kernel)
        conv_pre = conv_fwd(cut, window, full_conv)
    conv_pre = conv_pre + vectors[0]
    conv_act, conv_act_back = jax.vjp(gelu_exact, conv_pre)
    hidden_one = frames.astype(f32) + conv_act
    attn_in = hidden_one.astype(low_type)
    zero_part = jnp.zeros((HEADS, HEAD_DIM), f32)
    qkv_bias = jnp.stack(
        [vectors[1].reshape(HEADS, HEAD_DIM), zero_part, vectors[2].reshape(HEADS, HEAD_DIM)], axis=1
    ).reshape(3 * model_width)
    packed = (
        lax.dot_general(full_qkv, attn_in, (((0,), (1,)), ((), ())), preferred_element_type=f32) + qkv_bias[:, None]
    ).astype(low_type)
    if by_chips():
        heads_qkv, context, log_sums, context_wide, all_up, all_down = attend(seg_rows, packed, own_parts[3:5], attend_plan())
    else:
        blocks = trade(by_partner(packed.reshape(head_groups, -1, row_count)))
        fwd = attn_fwd(seg_rows, blocks)
        context = from_partner(trade(fwd[:4]))
    full_up = all_up.reshape(model_width, -1)
    full_down = all_down.reshape(-1, model_width)
    attn_out = lax.dot_general(context, full_proj, (((0,), (0,)), ((), ())), preferred_element_type=f32) + vectors[3]
    normed_one, norm_one_back = jax.vjp(layer_norm, hidden_one + attn_out, vectors[4], vectors[5])
    ffn_in = normed_one.astype(low_type)
    up_act, up_back = jax.vjp(gelu_exact, jnp.dot(ffn_in, full_up, preferred_element_type=f32) + full_ffn)
    hidden_mid = up_act.astype(low_type)
    hidden_three = normed_one + jnp.dot(hidden_mid, full_down, preferred_element_type=f32) + vectors[6]
    layer_out_full, norm_two_back = jax.vjp(layer_norm, hidden_three, vectors[7], vectors[8])
    grad_three, grad_gain_two, grad_shift_two = norm_two_back(output_grad.astype(f32))
    grad_ffn = grad_three.astype(low_type)
    grad_down = jnp.einsum("tf,td->fd", hidden_mid, grad_ffn, preferred_element_type=f32).astype(low_type)
    grad_down_bias = jnp.sum(grad_ffn.astype(f32), axis=0)
    (grad_up_pre,) = up_back(jnp.einsum("td,fd->tf", grad_ffn, full_down, preferred_element_type=f32))
    grad_up_low = grad_up_pre.astype(low_type)
    grad_up = jnp.einsum("td,tf->df", ffn_in, grad_up_low, preferred_element_type=f32).astype(low_type)
    grad_ffn_bias = jnp.sum(grad_up_low.astype(f32), axis=0)
    grad_normed = grad_three + jnp.einsum("tf,df->td", grad_up_low, full_up, preferred_element_type=f32)
    grad_two, grad_gain_one, grad_shift_one = norm_one_back(grad_normed)
    grad_attn = grad_two.astype(low_type)
    grad_proj = jnp.dot(context, grad_attn, preferred_element_type=f32).astype(low_type)
    grad_proj_bias = jnp.sum(grad_attn.astype(f32), axis=0)
    grad_context = lax.dot_general(full_proj, grad_attn, (((1,), (1,)), ((), ())), preferred_element_type=f32).astype(low_type)
    grad_proj, grad_up, grad_down = [
        g.reshape((count,) + w.shape) for g, w in ((grad_proj, proj_weight), (grad_up, up_weight), (grad_down, down_weight))
    ]
    if by_chips():
        grad_packed, square_tile, sum_proj, sum_up, sum_down = attend_back(
            seg_rows, heads_qkv, log_sums, context_wide, grad_context, [by_owner(g) for g in (grad_proj, grad_up, grad_down)], attend_back_plan()
        )
    else:
        grad_blocks = trade(by_partner(grad_context.reshape(head_groups, -1, row_count)))
        grad_packed = from_partner(trade(attn_bwd(seg_rows, blocks, grad_blocks, fwd[4], fwd[5])))
    grad_qkv = lax.dot_general(attn_in, grad_packed, (((0,), (1,)), ((), ())), preferred_element_type=f32).astype(low_type)
    grad_split = jnp.sum(grad_packed.astype(f32), axis=1).reshape(HEADS, 3, HEAD_DIM)
    grad_query_bias = grad_split[:, 0].reshape(model_width)
    grad_value_bias = grad_split[:, 2].reshape(model_width)
    grad_hidden_one = grad_two + lax.dot_general(grad_packed, full_qkv, (((0,), (1,)), ((), ())), preferred_element_type=f32)
    (grad_conv_pre,) = conv_act_back(grad_hidden_one)
    grad_conv_low = grad_conv_pre.astype(low_type)
    grad_conv_bias = jnp.sum(grad_conv_low.astype(f32), axis=0)
    grad_vectors = jnp.stack(
        [
            grad_conv_bias, grad_query_bias, grad_value_bias, grad_proj_bias, grad_gain_one, grad_shift_one,
            grad_down_bias, grad_gain_two, grad_shift_two,
        ],
        axis=0,
    )
    grad_small = jnp.concatenate(
        [grad_vectors.reshape(vec_rows, count, vec_cols).transpose(1, 0, 2).reshape(count, -1), grad_ffn_bias.reshape(count, ffn_cols)], axis=1
    )
    grad_small = jnp.pad(grad_small, ((0, 0), (0, 2048 - grad_small.shape[1]))).astype(low_type).reshape(count, 16, 128)
    grad_qkv = grad_qkv.reshape((count,) + qkv_weight.shape)
    if by_chips():
        grad_frames_conv, norm_tile, sum_conv, sum_qkv, sum_small = close_step(
            cut, window, grad_conv_low, whole_conv, square_tile, [by_owner(grad_qkv), by_owner(grad_small)], side_plan(), main_plan()
        )
        square_total = jnp.sum(norm_tile)
    else:
        grad_window = with_halo(grad_conv_low, (("head", 0),), half_kernel)
        grad_frames_conv, grad_conv = conv_bwd(cut, window, grad_window, full_conv)
        grad_conv = grad_conv.reshape(16, 2, 8, 24 // conv_rows, conv_rows, 768).transpose(0, 1, 3, 2, 4, 5).reshape(count, 8, conv_rows, 768)
        (sum_conv, sum_qkv, sum_proj, sum_up, sum_down, sum_small), square_total = collect_grads(
            [grad_conv, grad_qkv, grad_proj, grad_up, grad_down, grad_small]
        )
    frames_grad = grad_hidden_one + grad_frames_conv
    sum_conv = sum_conv.reshape(8, conv_rows, 16, group_width).transpose(2, 0, 1, 3).reshape(conv_weight.shape)
    sum_small = sum_small.reshape(-1)
    sum_vectors = sum_small[: vec_rows * vec_cols].reshape(vec_rows, vec_cols)
    sum_ffn_bias = sum_small[vec_rows * vec_cols : vec_rows * vec_cols + ffn_cols]
    summed = (sum_qkv, sum_proj, sum_up, sum_down, sum_conv, sum_vectors, sum_ffn_bias)
    grad_norm = jnp.sqrt(square_total)
    factor = jnp.minimum(1.0, clip_bound / grad_norm)
    masters = (qkv_weight, proj_weight, up_weight, down_weight, conv_weight, bias_gains, ffn_bias)
    firsts = (qkv_first, proj_first, up_first, down_first, conv_first, bias_gains_first, ffn_bias_first)
    seconds = (qkv_second, proj_second, up_second, down_second, conv_second, bias_gains_second, ffn_bias_second)
    news, first_news, second_news = [], [], []
    for index in range(7):
        decay = matrix_decay if index < 5 else 0.0
        new_weight, first_new, second_new = adam_update(
            masters[index], summed[index] * factor, firsts[index], seconds[index], weight_rates[index], decay
        )
        news.append(new_weight)
        first_news.append(first_new)
        second_news.append(second_new)
    return (layer_out_full.astype(low_type), frames_grad, grad_norm, *news, *first_news, *second_news)


def solution(mesh):
    rows, both = P(("seq", "head"), None), ("seq", "head")
    weights = (rows, rows, rows, rows, P(None, both, None), P(None, both), P(both))
    return jax.shard_map(
        shards,
        mesh=mesh,
        in_specs=(rows, rows, P("seq", None)) + weights * 3,
        out_specs=(rows, rows, P()) + weights * 3,
        check_vma=False,
    )
```

```python
import functools

import jax
import jax.numpy as jnp
from jax import lax
from jax.experimental import pallas as pl
from jax.experimental.pallas import tpu as pltpu
from jax.sharding import PartitionSpec as P

HEADS = 12
HEAD_DIM = 64
STEP = 10


norm_eps = 1e-05
beta_first = 0.9
beta_second = 0.999
adam_eps = 1e-08
weight_rates = (0.02, 0.1, 0.02, 0.02, 0.02, 0.2, 0.2)
matrix_decay = 0.01
clip_bound = 1.0


def with_halo(cells, sides, width):
    for axis, dim in sides:
        count = lax.axis_size(axis)
        ends = count - 1
        head = lax.slice_in_dim(cells, 0, width, axis=dim)
        tail = lax.slice_in_dim(cells, cells.shape[dim] - width, cells.shape[dim], axis=dim)
        cells = jnp.concatenate(
            [
                lax.ppermute(tail, axis, [(i, (i + 1) % count) for i in range(ends)]),
                cells,
                lax.ppermute(head, axis, [((i + 1) % count, i) for i in range(ends)]),
            ],
            axis=dim,
        )
    return cells


def layer_norm(values, scale_gain, shift_row):
    center = values - jnp.mean(values, axis=-1, keepdims=True)
    spread = jnp.mean(center * center, axis=-1, keepdims=True)
    return center * lax.rsqrt(spread + norm_eps) * scale_gain + shift_row


def gelu_exact(values):
    return jax.nn.gelu(values, approximate=False)


def adam_update(weight, grad, first, second, rate, decay):
    first_new = beta_first * first + (1.0 - beta_first) * grad
    second_new = beta_second * second + (1.0 - beta_second) * grad * grad
    first_hat = first_new / (1.0 - beta_first**STEP)
    second_hat = second_new / (1.0 - beta_second**STEP)
    new_weight = weight - rate * (first_hat / (jnp.sqrt(second_hat) + adam_eps) + decay * weight)
    return (new_weight, first_new, second_new)


HALF = 64
OWN = 512
WIN = OWN + 2 * HALF
EXT = WIN + HALF
ZROWS = OWN + HALF + 8
CGW = 48

def up(v, n):
    return pltpu.roll(v, v.shape[0] - n, 0)

def down(v, n):
    return pltpu.roll(v, n, 0)

def left(v, n):
    return pltpu.roll(v, v.shape[1] - n, 1)

def right(v, n):
    return pltpu.roll(v, n, 1)

def place(g):
    tile = jnp.minimum(g * CGW // 128, 4)
    return pl.ds(pl.multiple_of(tile * 128, 128), 256), g * CGW - tile * 128

def take_group(ref, g):
    lanes, rem = place(g)
    wide = ref[:, lanes].astype(jnp.float32)
    return pltpu.roll(wide, 256 - rem, 1)[:, :128]

def gapped(xg, cut):
    row = lax.broadcasted_iota(jnp.int32, (EXT, 128), 0)
    zero = jnp.zeros((HALF, 128), jnp.float32)
    before = jnp.concatenate([xg, zero], axis=0)
    after = jnp.concatenate([zero, xg], axis=0)
    return jnp.where(row < cut, before, jnp.where(row < cut + HALF, 0.0, after))

def im2col(xg, rows):
    lane = lax.broadcasted_iota(jnp.int32, (rows, 128), 1)
    turned = {off: (right(xg, off) if off else xg) for off in range(0, 128, 16)}
    cols = []
    for v in range(6):
        acc = None
        for r in range(16):
            lo = CGW * r
            if lo + CGW <= 128 * v or lo >= 128 * (v + 1):
                continue
            piece = turned[lo % 128][8 * r : 8 * r + rows, :]
            acc = piece if acc is None else jnp.where(lane >= lo - 128 * v, piece, acc)
        cols.append(acc.astype(jnp.bfloat16))
    return jnp.concatenate(cols, axis=1)

def pad_weights(w_ref, wp_ref):
    for h in range(2):
        for a in range(8):
            wp_ref[pl.ds(h * 256 + a * 32, 24), :] = w_ref[0, h, a]

def fold_out(z):
    lane = lax.broadcasted_iota(jnp.int32, (ZROWS, 128), 1)
    u = []
    for h in range(2):
        t = z[:, h * 256 : h * 256 + 128] + up(z[:, h * 256 + 128 : h * 256 + 256], 4)
        u.append(t + left(up(t, 2), 64))
    v = jnp.where(lane < 64, u[0], right(u[1], 64))
    o = v + left(up(v, 1), 32)
    return jnp.where(lane < 24, o, left(o, 40))[: OWN + HALF]

def pick_own(o, cut):
    row = lax.broadcasted_iota(jnp.int32, (OWN, 128), 0) + HALF
    return jnp.where(row < cut, o[:OWN], o[HALF : OWN + HALF])

def put_group(out_ref, g, o):
    lanes, rem = place(g)
    lane = lax.broadcasted_iota(jnp.int32, (OWN, 128), 1)
    o = jnp.where(lane < CGW, o, 0.0)
    wide = jnp.concatenate([o, jnp.zeros((OWN, 128), jnp.float32)], axis=1)
    out_ref[:, lanes] += pltpu.roll(wide, rem, 1)

def conv_fwd_kernel(cut_ref, x_ref, w_ref, out_ref, wp_ref):
    g = pl.program_id(0)
    cut = cut_ref[0]
    @pl.when(g == 0)
    def _():
        wp_ref[...] = jnp.zeros_like(wp_ref)
        out_ref[...] = jnp.zeros_like(out_ref)
    pad_weights(w_ref, wp_ref)
    cols = im2col(gapped(take_group(x_ref, g), cut), ZROWS)
    z = lax.dot_general(cols, wp_ref[...], (((1,), (1,)), ((), ())), preferred_element_type=jnp.float32)
    put_group(out_ref, g, pick_own(fold_out(z), cut))

def conv_fwd(cut, xw, w):
    return pl.pallas_call(
        conv_fwd_kernel,
        grid_spec=pltpu.PrefetchScalarGridSpec(
            num_scalar_prefetch=1, grid=(16,),
            in_specs=[pl.BlockSpec((WIN, 768), lambda g, c: (0, 0)),
                      pl.BlockSpec((1, 2, 8, 24, 768), lambda g, c: (g, 0, 0, 0, 0))],
            out_specs=pl.BlockSpec((OWN, 768), lambda g, c: (0, 0)),
            scratch_shapes=[pltpu.VMEM((512, 768), jnp.bfloat16)]),
        out_shape=jax.ShapeDtypeStruct((OWN, 768), jnp.float32),
        compiler_params=pltpu.CompilerParams(vmem_limit_bytes=50 * 2**20),
        cost_estimate=pl.CostEstimate(flops=2 * 16 * 584 * 768 * 512, bytes_accessed=12_000_000, transcendentals=0),
    )(cut, xw, w)

def taps_of(gg):
    lane = lax.broadcasted_iota(jnp.int32, (EXT, 128), 1)
    low = jnp.where(lane < 24, gg, 0.0)
    high = jnp.where((lane >= 64) & (lane < 88), right(gg, 40), 0.0)
    s = low + high
    q = s + right(down(s, 1), 32)
    q2 = down(q, 2)
    parts = []
    for h in range(2):
        if h == 0:
            r = jnp.where(lane < 64, q, right(q2, 64))
        else:
            r = jnp.where(lane < 64, right(q, 64), q2)
        parts += [r, down(r, 4)]
    return jnp.concatenate([p.astype(jnp.bfloat16) for p in parts], axis=1)

def fold_back(z):
    n = OWN + HALF
    lane = lax.broadcasted_iota(jnp.int32, (n, 128), 1)
    a = [z[HALF:, 128 * i : 128 * i + 128] + z[: EXT - HALF, 384 + 128 * i : 512 + 128 * i] for i in range(3)]
    acc = None
    for r in range(8):
        lo = CGW * r
        first = HALF - 8 * r
        tile, off = lo // 128, lo % 128
        piece = a[tile][first : first + n]
        if off:
            piece = left(piece, off)
        if off + CGW > 128:
            piece = jnp.where(lane < 128 - off, piece, right(a[tile + 1][first : first + n], 128 - off))
        acc = piece if acc is None else acc + piece
    return acc

def conv_bwd_kernel(cut_ref, x_ref, g_ref, w_ref, dx_ref, dw_ref, wp_ref):
    g = pl.program_id(0)
    cut = cut_ref[0]
    @pl.when(g == 0)
    def _():
        wp_ref[...] = jnp.zeros_like(wp_ref)
        dx_ref[...] = jnp.zeros_like(dx_ref)
    pad_weights(w_ref, wp_ref)
    taps = taps_of(gapped(take_group(g_ref, g), cut))
    z = jnp.dot(taps, wp_ref[...], preferred_element_type=jnp.float32)
    put_group(dx_ref, g, pick_own(fold_back(z), cut))
    cols = im2col(gapped(take_group(x_ref, g), cut), ZROWS)
    row = lax.broadcasted_iota(jnp.int32, (ZROWS, 512), 0) + HALF
    begin = jnp.where(cut <= HALF, 2 * HALF, HALF)
    end = jnp.where(cut_ref[1] > 0, EXT, jnp.where(cut <= HALF + OWN, OWN + 2 * HALF, OWN + HALF))
    own = jnp.where((row >= begin) & (row < end), taps[HALF : HALF + ZROWS].astype(jnp.float32), 0.0).astype(jnp.bfloat16)
    dw = lax.dot_general(own, cols, (((0,), (0,)), ((), ())), preferred_element_type=jnp.float32)
    for h in range(2):
        for a in range(8):
            dw_ref[0, h, a] = dw[h * 256 + a * 32 : h * 256 + a * 32 + 24].astype(dw_ref.dtype)

def conv_bwd(cut, xw, gw, w, dtype=jnp.bfloat16):
    return pl.pallas_call(
        conv_bwd_kernel,
        grid_spec=pltpu.PrefetchScalarGridSpec(
            num_scalar_prefetch=1, grid=(16,),
            in_specs=[pl.BlockSpec((WIN, 768), lambda g, c: (0, 0)),
                      pl.BlockSpec((WIN, 768), lambda g, c: (0, 0)),
                      pl.BlockSpec((1, 2, 8, 24, 768), lambda g, c: (g, 0, 0, 0, 0))],
            out_specs=[pl.BlockSpec((OWN, 768), lambda g, c: (0, 0)),
                       pl.BlockSpec((1, 2, 8, 24, 768), lambda g, c: (g, 0, 0, 0, 0))],
            scratch_shapes=[pltpu.VMEM((512, 768), jnp.bfloat16)]),
        out_shape=[jax.ShapeDtypeStruct((OWN, 768), jnp.float32), jax.ShapeDtypeStruct((16, 2, 8, 24, 768), dtype)],
        compiler_params=pltpu.CompilerParams(vmem_limit_bytes=50 * 2**20),
        cost_estimate=pl.CostEstimate(flops=4 * 16 * 640 * 768 * 512, bytes_accessed=22_000_000, transcendentals=0),
    )(cut, xw, gw, w)


QT = 256
QF = 512
FAR = -1e30

def fold_rows(v, op):
    while v.shape[0] > 8:
        n = v.shape[0] // 2
        v = op(v[:n], v[n:])
    return v


def fill_keys(seg_ref, blocks, kq_ref, q_ref):
    n = seg_ref.shape[1]
    seg = seg_ref[...]
    row = lax.broadcasted_iota(jnp.int32, (64, n), 0)
    mark = jnp.where(row < 2, jnp.where(seg == row, 1.0, 0.0), 0.0)
    push = jnp.where(row < 2, jnp.where(seg == row, 0.0, FAR), 0.0)
    keys = jnp.concatenate([b[64:128, :] for b in blocks], axis=1).astype(jnp.float32)
    kq_ref[...] = jnp.transpose(jnp.concatenate([keys, mark], axis=0)).astype(jnp.bfloat16)
    queries = jnp.concatenate([b[0:64, :] for b in blocks], axis=1).astype(jnp.float32) * 0.125
    q_ref[...] = jnp.concatenate([queries, push], axis=0).astype(jnp.bfloat16)

def attn_fwd_kernel(seg_ref, b0, b1, b2, b3, c0, c1, c2, c3, lse_ref, o_ref, k_s, q_s, v_s):
    blocks = (b0, b1, b2, b3)
    n = seg_ref.shape[1]
    size = b0.shape[1]
    fill_keys(seg_ref, blocks, k_s, q_s)
    v_s[...] = jnp.concatenate([b[128:192, :] for b in blocks], axis=1)

    def tile(i, unused):
        at = pl.ds(pl.multiple_of(i * QT, QT), QT)
        s = jnp.dot(k_s[...], q_s[:, at], preferred_element_type=jnp.float32)
        peak = jnp.max(fold_rows(s, jnp.maximum), axis=0, keepdims=True)
        e = jnp.exp(s - peak)
        denom = jnp.sum(fold_rows(e, jnp.add), axis=0, keepdims=True)
        o = jnp.dot(v_s[...], e.astype(jnp.bfloat16), preferred_element_type=jnp.float32)
        o_ref[0, :, at] = o * (1.0 / denom)
        lse_ref[0, :, at] = peak + jnp.log(denom)
        return unused

    lax.fori_loop(0, n // QT, tile, 0)
    for j, c in enumerate((c0, c1, c2, c3)):
        c[...] = o_ref[0, :, j * size : (j + 1) * size].astype(jnp.bfloat16)

def attn_fwd(seg, blocks):
    size = blocks[0].shape[1]
    n = 4 * size
    heads = blocks[0].shape[0] // 192
    return pl.pallas_call(
        attn_fwd_kernel,
        grid=(heads,),
        in_specs=[pl.BlockSpec((1, n), lambda h: (0, 0))] + [pl.BlockSpec((192, size), lambda h: (h, 0))] * 4,
        out_specs=[pl.BlockSpec((64, size), lambda h: (h, 0))] * 4
        + [pl.BlockSpec((1, 1, n), lambda h: (h, 0, 0)), pl.BlockSpec((1, 64, n), lambda h: (h, 0, 0))],
        out_shape=[jax.ShapeDtypeStruct((heads * 64, size), jnp.bfloat16)] * 4
        + [jax.ShapeDtypeStruct((heads, 1, n), jnp.float32), jax.ShapeDtypeStruct((heads, 64, n), jnp.float32)],
        scratch_shapes=[pltpu.VMEM((n, 128), jnp.bfloat16), pltpu.VMEM((128, n), jnp.bfloat16), pltpu.VMEM((64, n), jnp.bfloat16)],
        compiler_params=pltpu.CompilerParams(vmem_limit_bytes=50 * 2**20),
        cost_estimate=pl.CostEstimate(flops=heads * n * n * 256, bytes_accessed=6_000_000, transcendentals=heads * n * n),
    )(seg, *blocks)

def attn_bwd_kernel(seg_ref, b0, b1, b2, b3, d0, d1, d2, d3, lse_ref, o_ref, g0, g1, g2, g3, k_s, q_s, v_s, kt_s, do_s, dk_s, dv_s, dq_s):
    blocks = (b0, b1, b2, b3)
    n = seg_ref.shape[1]
    size = b0.shape[1]
    fill_keys(seg_ref, blocks, k_s, q_s)
    v_s[...] = jnp.transpose(jnp.concatenate([b[128:192, :] for b in blocks], axis=1).astype(jnp.float32)).astype(jnp.bfloat16)
    kt_s[...] = jnp.concatenate([b[64:128, :] for b in blocks], axis=1)
    do_s[...] = jnp.concatenate([d[...] for d in (d0, d1, d2, d3)], axis=1)
    dk_s[...] = jnp.zeros_like(dk_s)
    dv_s[...] = jnp.zeros_like(dv_s)

    def tile(i, unused):
        at = pl.ds(pl.multiple_of(i * QT, QT), QT)
        q = q_s[:, at]
        do = do_s[:, at]
        delta = jnp.sum(do.astype(jnp.float32) * o_ref[0, :, at], axis=0, keepdims=True)
        s = jnp.dot(k_s[...], q, preferred_element_type=jnp.float32)
        p = jnp.exp(s - lse_ref[0, :, at])
        dp = jnp.dot(v_s[...], do, preferred_element_type=jnp.float32)
        ds = (p * (dp - delta)).astype(jnp.bfloat16)
        p = p.astype(jnp.bfloat16)
        nt = (((1,), (1,)), ((), ()))
        dv_s[...] += lax.dot_general(do, p, nt, preferred_element_type=jnp.float32)
        dk_s[...] += lax.dot_general(q[:64], ds, nt, preferred_element_type=jnp.float32)
        dq_s[:, at] = jnp.dot(kt_s[...], ds, preferred_element_type=jnp.float32) * 0.125
        return unused

    lax.fori_loop(0, n // QT, tile, 0)
    for j, g in enumerate((g0, g1, g2, g3)):
        span = slice(j * size, (j + 1) * size)
        g[0:64, :] = dq_s[:, span].astype(jnp.bfloat16)
        g[64:128, :] = dk_s[:, span].astype(jnp.bfloat16)
        g[128:192, :] = dv_s[:, span].astype(jnp.bfloat16)

def attn_bwd(seg, blocks, grads, lse, o):
    size = blocks[0].shape[1]
    n = 4 * size
    heads = blocks[0].shape[0] // 192
    return pl.pallas_call(
        attn_bwd_kernel,
        grid=(heads,),
        in_specs=[pl.BlockSpec((1, n), lambda h: (0, 0))] + [pl.BlockSpec((192, size), lambda h: (h, 0))] * 4
        + [pl.BlockSpec((64, size), lambda h: (h, 0))] * 4
        + [pl.BlockSpec((1, 1, n), lambda h: (h, 0, 0)), pl.BlockSpec((1, 64, n), lambda h: (h, 0, 0))],
        out_specs=[pl.BlockSpec((192, size), lambda h: (h, 0))] * 4,
        out_shape=[jax.ShapeDtypeStruct((heads * 192, size), jnp.bfloat16)] * 4,
        scratch_shapes=[pltpu.VMEM((n, 128), jnp.bfloat16), pltpu.VMEM((128, n), jnp.bfloat16), pltpu.VMEM((n, 64), jnp.bfloat16),
                        pltpu.VMEM((64, n), jnp.bfloat16), pltpu.VMEM((64, n), jnp.bfloat16),
                        pltpu.VMEM((64, n), jnp.float32), pltpu.VMEM((64, n), jnp.float32), pltpu.VMEM((64, n), jnp.float32)],
        compiler_params=pltpu.CompilerParams(vmem_limit_bytes=50 * 2**20),
        cost_estimate=pl.CostEstimate(flops=heads * n * n * 640, bytes_accessed=10_000_000, transcendentals=heads * n * n),
    )(seg, *blocks, *grads, lse, o)


MESH = pl.DeviceIdType.MESH
EVERY = slice(None)


def spot():
    seq, head = lax.axis_index("seq"), lax.axis_index("head")
    return seq // 2, seq % 2, head // 2, head % 2


def device(z, x, y, c):
    return {"seq": z * 2 + x, "head": y * 2 + c}


def hail(where):
    pl.semaphore_signal(pltpu.get_barrier_semaphore(), inc=1, device_id=where, device_id_type=MESH)


def greet(plane=False, group=False, halo=False):
    z, x, y, c = spot()
    for n in range(1, 4):
        hail(device(z ^ n, x, y, c))
    if plane:
        for n in range(1, 8):
            hail(device(z, x ^ (n >> 2), y ^ ((n >> 1) & 1), c ^ (n & 1)))
        pl.semaphore_wait(pltpu.get_barrier_semaphore(), 10)
        return
    count = 6
    hail(device(z, x, y, 1 - c))
    hail(device(z, x, 1 - y, c))
    hail(device(z, 1 - x, y, c))
    if group:
        hail(device(z, x, 1 - y, 1 - c))
        count = count + 1
    elif halo:
        far = y != c
        pl.when(far)(lambda: hail(device(z, x, 1 - y, 1 - c)))
        count = count + jnp.where(far, 1, 0)
    pl.semaphore_wait(pltpu.get_barrier_semaphore(), count)


class Unit:
    def remote(self, src, dst, n, to):
        return pltpu.make_async_remote_copy(
            src_ref=src, dst_ref=dst, send_sem=self.send.at[n], recv_sem=self.recv.at[n], device_id=to, device_id_type=MESH
        )

    def landed(self, ref, n):
        z, x, y, c = spot()
        return self.remote(ref, ref, n, device(z, x, y, 1 - c))


class Spread(Unit):
    heavy = (2, 1, 0, 3, 4)

    def __init__(self, own, whole, cut, order, send, recv):
        self.own, self.whole, self.cut, self.order, self.send, self.recv = own, whole, cut, order, send, recv

    def block(self, done, **given):
        z, x, y, c = spot()
        here = {"z": z, "x": x, "y": y, "c": c}
        lead = tuple(given[a] if a in given else (EVERY if a in done else here[a]) for a in "zxyc")
        return self.whole.at[lead + self.cut]

    def mine(self):
        return self.own.at[self.cut] if self.cut else self.own

    def columns(self):
        z, x, y, c = spot()
        return [self.remote(self.mine(), self.block(""), n - 1, device(z ^ n, x, y, c)) for n in range(1, 4)]

    def swap(self, k):
        z, x, y, c = spot()
        axis = (self.order + "c")[k]
        ref = self.block("z" + self.order[:k])
        to = {"x": device(z, 1 - x, y, c), "y": device(z, x, 1 - y, c), "c": device(z, x, y, 1 - c)}[axis]
        return self.remote(ref, ref, 3 + k, to)

    def swapped(self, k):
        z, x, y, c = spot()
        axis = (self.order + "c")[k]
        return self.landed(self.block("z" + self.order[:k], **{axis: {"x": 1 - x, "y": 1 - y, "c": 1 - c}[axis]}), 3 + k)

    def stage(self, n):
        z, x, y, c = spot()
        if n < 2:
            local = pltpu.make_async_copy(self.mine(), self.block(""), self.recv.at[6])
            local.start() if n == 0 else local.wait()
        if n == 0:
            for copy in self.columns():
                copy.start()
        elif n == 1:
            for m in range(1, 4):
                self.landed(self.block("", z=z ^ m), m - 1).wait_recv()
            self.swap(0).start()
        else:
            self.swapped(n - 2).wait_recv()
            if n < 4:
                self.swap(n - 1).start()

    def finish(self):
        for copy in self.columns() + [self.swap(k) for k in range(3)]:
            copy.wait_send()


def add_rows(dst, src):
    dst[...] = (dst[...].astype(jnp.float32) + src[...].astype(jnp.float32)).astype(dst.dtype)


class Collect(Unit):
    heavy = (0, 1, 2, 3, 4)

    def __init__(self, parts, out, cut, order, own, rc, r1, r2, rz, send, recv):
        self.parts, self.out, self.cut, self.order, self.send, self.recv = parts, out, cut, order, send, recv
        self.own, self.rc, self.r1, self.r2, self.rz = own, rc, r1, r2, rz

    def block(self, *lead):
        if self.own is None:
            z, x, y, c = spot()
            return self.parts.at[tuple(lead) + (c,) + self.cut]
        return self.own.at[tuple(lead)]

    def core(self):
        z, x, y, c = spot()
        return self.remote(self.parts.at[(EVERY, EVERY, EVERY, 1 - c) + self.cut], self.rc, 0, device(z, x, y, 1 - c))

    def load(self):
        z, x, y, c = spot()
        return pltpu.make_async_copy(self.parts.at[(EVERY, EVERY, EVERY, c) + self.cut], self.own, self.recv.at[6])

    def first(self):
        z, x, y, c = spot()
        if self.order[0] == "x":
            return self.remote(self.block(EVERY, 1 - x, EVERY), self.r1, 1, device(z, 1 - x, y, c))
        return self.remote(self.block(EVERY, EVERY, 1 - y), self.r1, 1, device(z, x, 1 - y, c))

    def second(self):
        z, x, y, c = spot()
        if self.order[0] == "x":
            return self.remote(self.block(EVERY, x, 1 - y), self.r2, 2, device(z, x, 1 - y, c))
        return self.remote(self.block(EVERY, 1 - x, y), self.r2, 2, device(z, 1 - x, y, c))

    def columns(self):
        z, x, y, c = spot()
        return [self.remote(self.block(z ^ n, x, y), self.rz.at[n - 1], 2 + n, device(z ^ n, x, y, c)) for n in range(1, 4)]

    def stage(self, n):
        z, x, y, c = spot()
        if n == 0:
            self.core().start()
            if self.own is not None:
                self.load().start()
        elif n == 1:
            self.landed(self.rc, 0).wait_recv()
            if self.own is not None:
                self.load().wait()

            def one(i, unused):
                for k in range(2):
                    for m in range(2):
                        add_rows(self.block(i, k, m), self.rc.at[i, k, m])
                return unused

            lax.fori_loop(0, 4, one, 0)
            self.first().start()
        elif n == 2:
            self.landed(self.r1, 1).wait_recv()

            def one(i, unused):
                for k in range(2):
                    add_rows(self.block(i, x, k) if self.order[0] == "x" else self.block(i, k, y), self.r1.at[i, k])
                return unused

            lax.fori_loop(0, 4, one, 0)
            self.second().start()
        elif n == 3:
            self.landed(self.r2, 2).wait_recv()

            def one(i, unused):
                add_rows(self.block(i, x, y), self.r2.at[i])
                return unused

            lax.fori_loop(0, 4, one, 0)
            for copy in self.columns():
                copy.start()
        else:
            total = self.block(z, x, y)[...].astype(jnp.float32)
            for m in range(1, 4):
                self.landed(self.rz.at[m - 1], 2 + m).wait_recv()
                total = total + self.rz[m - 1].astype(jnp.float32)
            out = self.out.at[self.cut] if self.cut else self.out
            out[...] = total

    def finish(self):
        for copy in [self.core(), self.first(), self.second()] + self.columns():
            copy.wait_send()


def unit_shape(shape, cut):
    cut = tuple(cut) + (slice(None),) * (len(shape) - len(cut))
    return tuple(len(range(*s.indices(d))) for s, d in zip(cut, shape))


def collect_scratch(plan, shapes, dtype, inside):
    scratch = []
    for i, cut, order in plan:
        m = unit_shape(shapes[i], cut)
        leads = [] if i in inside else [(4, 2, 2)]
        leads += [(4, 2, 2), (4, 2), (4,), (3,)]
        scratch += [pltpu.VMEM(lead + m, dtype) for lead in leads]
    return scratch


def collect_units(plan, parts, outs, bufs, inside, send, recv):
    units, bufs = [], list(bufs)
    for n, (i, cut, order) in enumerate(plan):
        own = None if i in inside else bufs.pop(0)
        units.append(Collect(parts[i], outs[i], cut, order, own, bufs.pop(0), bufs.pop(0), bufs.pop(0), bufs.pop(0), send.at[n], recv.at[n]))
    return units


STAGES = 5


def waves(units, width=2):
    rows = [units[i : i + width] for i in range(0, len(units), width)]
    steps = []
    for t in range(len(rows) + STAGES - 1 if rows else 0):
        steps.append([(unit, n) for n in units[0].heavy for unit in (rows[t - n] if 0 <= t - n < len(rows) else [])])
    return steps


def go(step):
    for unit, n in step:
        unit.stage(n)


def square_sum(refs, tile):
    tile[...] = jnp.zeros_like(tile)
    for ref in refs:
        v = ref[...]
        v = (v * v).reshape(-1, v.shape[-1])
        v = jnp.sum(v.reshape(-1, 8, v.shape[-1]), axis=0)
        for i in range(0, v.shape[-1], 128):
            tile[...] += v[:, i : i + 128]


def total_square(norm, tiles, send, recv):
    z, x, y, c = spot()
    mine = x * 4 + y * 2 + c
    copies = []

    def push(slot, n, to):
        copies.append(pltpu.make_async_remote_copy(
            src_ref=tiles.at[slot], dst_ref=tiles.at[slot], send_sem=send.at[n], recv_sem=recv.at[n], device_id=to, device_id_type=MESH))
        copies[-1].start()

    def pull(slot, n):
        ref = tiles.at[slot]
        pltpu.make_async_remote_copy(
            src_ref=ref, dst_ref=ref, send_sem=send.at[n], recv_sem=recv.at[n], device_id=device(z, x, y, 1 - c), device_id_type=MESH).wait_recv()

    for n in range(1, 8):
        push(mine, n, device(z, x ^ (n >> 2), y ^ ((n >> 1) & 1), c ^ (n & 1)))
    for n in range(1, 8):
        pull(mine ^ n, n)
    total = tiles[0]
    for n in range(1, 8):
        total = total + tiles[n]
    tiles[8 + z] = total
    for n in range(1, 4):
        push(8 + z, 7 + n, device(z ^ n, x, y, c))
    for n in range(1, 4):
        pull(8 + (z ^ n), 7 + n)
    norm[...] = (tiles[8] + tiles[9]) + (tiles[10] + tiles[11])
    for copy in copies:
        copy.wait_send()


def take_rows(win_ref, g, cut):
    return gapped(take_group(win_ref, g), cut)


def halo_copies(edges_ref, win_ref, send, recv):
    z, x, y, c = spot()
    h = y * 2 + c
    n = edges_ref.shape[0]

    def to(other):
        return {"seq": z * 2 + x, "head": other}

    def copy(src, dst, k, other):
        return pltpu.make_async_remote_copy(
            src_ref=src, dst_ref=dst, send_sem=send.at[k], recv_sem=recv.at[k], device_id=to(other), device_id_type=MESH)

    after = copy(edges_ref.at[n - HALF : n], win_ref.at[0:HALF], 0, h + 1)
    before = copy(edges_ref.at[0:HALF], win_ref.at[n + HALF : n + 2 * HALF], 1, h - 1)
    from_before = copy(win_ref.at[0:HALF], win_ref.at[0:HALF], 0, h ^ 1)
    from_after = copy(win_ref.at[n + HALF : n + 2 * HALF], win_ref.at[n + HALF : n + 2 * HALF], 1, h ^ 1)
    return (h < 3, after), (h > 0, before), (h > 0, from_before), (h < 3, from_after)


def halo_start(edges_ref, win_ref, send, recv):
    for ok, copy in halo_copies(edges_ref, win_ref, send, recv)[:2]:
        pl.when(ok)(copy.start)


def halo_end(edges_ref, win_ref, send, recv):
    n = edges_ref.shape[0]
    after, before, from_before, from_after = halo_copies(edges_ref, win_ref, send, recv)
    for (ok, copy), rows in ((from_before, slice(0, HALF)), (from_after, slice(n + HALF, n + 2 * HALF))):
        pl.when(ok)(copy.wait_recv)

        @pl.when(jnp.logical_not(ok))
        def _(rows=rows):
            win_ref[rows, :] = jnp.zeros((HALF, win_ref.shape[1]), win_ref.dtype)

    for ok, copy in (after, before):
        pl.when(ok)(copy.wait_send)


def open_kernel(plan, n_in, early, *refs):
    cut_ref, frames_ref = refs[:2]
    owns = refs[2 : 2 + n_in]
    out_ref, cols_ref = refs[2 + n_in : 4 + n_in]
    wholes = refs[4 + n_in : 4 + 2 * n_in]
    win_ref, cols_s, low_s, w_s, wp_s, send, recv, hsend, hrecv, wsem, csem = refs[4 + 2 * n_in :]
    cut = cut_ref[0]
    greet(halo=True)
    halo_start(frames_ref, win_ref, hsend, hrecv)
    units = [Spread(owns[i], wholes[i], where, order, send.at[n], recv.at[n]) for n, (i, where, order) in enumerate(plan)]
    steps = waves(units)
    go(steps[0])
    win_ref[HALF : HALF + OWN, :] = frames_ref[...]
    out_ref[...] = jnp.zeros_like(out_ref)
    wp_s[...] = jnp.zeros_like(wp_s)
    go(steps[1])
    halo_end(frames_ref, win_ref, hsend, hrecv)

    def columns(g, unused):
        cols_s[g] = im2col(take_rows(win_ref, g, cut), ZROWS)
        return unused

    def load(half, z):
        return pltpu.make_async_copy(wholes[0].at[z, :, :, :, 4 * half : 4 * half + 4], w_s.at[z], wsem.at[z])

    def product(g):
        z, x, y = g // 4, (g // 2) % 2, g % 2
        for h in range(2):
            for a in range(4):
                wp_s[h * 128 + a * 32 : h * 128 + a * 32 + 24, :] = w_s[z, x, y, h, a]
        return lax.dot_general(cols_s[g], wp_s[...], (((1,), (1,)), ((), ())), preferred_element_type=jnp.float32)

    def low(g, unused):
        low_s[g] = product(g)
        return unused

    def high(g, unused):
        z = jnp.concatenate([low_s[g], product(g)], axis=1)
        z = jnp.concatenate([z[:, 0:128], z[:, 256:384], z[:, 128:256], z[:, 384:512]], axis=1)
        put_group(out_ref, g, pick_own(fold_out(z), cut))
        return unused

    def keep(chunk):
        span = pl.ds(4 * chunk, 4)
        return pltpu.make_async_copy(cols_s.at[span], cols_ref.at[span], csem.at[chunk])

    t = 2
    for chunk in range(4):
        lax.fori_loop(4 * chunk, 4 * chunk + 4, columns, 0)
        keep(chunk).start()
        go(steps[t])
        t += 1
    done = 0
    while t < len(steps) or done < 2:
        if done < 2 and t - STAGES >= early[done]:
            for z in range(4):
                load(done, z).start()
            for z in range(4):
                load(done, z).wait()
                lax.fori_loop(4 * z, 4 * z + 4, (low, high)[done], 0)
                if t < len(steps) and z % 2 == 1:
                    go(steps[t])
                    t += 1
            done += 1
        elif t < len(steps):
            go(steps[t])
            t += 1
    for unit in units:
        unit.finish()
    for chunk in range(4):
        keep(chunk).wait()


def open_step(cut, frames, shards, plan, early, collective_id=1):
    n = len(shards)
    vmem = pl.BlockSpec(memory_space=pltpu.VMEM)
    anywhere = pl.BlockSpec(memory_space=pl.ANY)
    return pl.pallas_call(
        functools.partial(open_kernel, plan, n, early),
        in_specs=[pl.BlockSpec(memory_space=pltpu.SMEM), vmem] + [anywhere] * n,
        out_specs=[vmem, anywhere] + [anywhere] * n,
        out_shape=[jax.ShapeDtypeStruct((OWN, 768), jnp.float32), jax.ShapeDtypeStruct((16, ZROWS, 768), jnp.bfloat16)]
        + [jax.ShapeDtypeStruct((4, 2, 2, 2) + s.shape, s.dtype) for s in shards],
        scratch_shapes=[
            pltpu.VMEM((WIN, 768), jnp.bfloat16),
            pltpu.VMEM((16, ZROWS, 768), jnp.bfloat16),
            pltpu.VMEM((16, ZROWS, 256), jnp.float32),
            pltpu.VMEM((4, 2, 2, 2, 4, 24, 768), jnp.bfloat16),
            pltpu.VMEM((256, 768), jnp.bfloat16),
            pltpu.SemaphoreType.DMA((len(plan), 9)),
            pltpu.SemaphoreType.DMA((len(plan), 10)),
            pltpu.SemaphoreType.DMA((2,)),
            pltpu.SemaphoreType.DMA((2,)),
            pltpu.SemaphoreType.DMA((4,)),
            pltpu.SemaphoreType.DMA((4,)),
        ],
        compiler_params=pltpu.CompilerParams(collective_id=collective_id, has_side_effects=True, vmem_limit_bytes=56 * 2**20),
    )(cut, frames, *shards)


HEADS_HERE = 3
ROWS_HERE = 192 * HEADS_HERE


def group_copy(src, dst, send, recv, other):
    return pltpu.make_async_remote_copy(
        src_ref=src, dst_ref=dst, send_sem=send, recv_sem=recv, device_id={"head": other}, device_id_type=MESH
    )


def spaced(steps, slots):
    out = [[] for _ in range(slots)]
    for t, step in enumerate(steps):
        out[min(t * slots // max(len(steps), 1), slots - 1)].append(step)
    return out


def go_at(slot, by_slot):
    for t, steps in enumerate(by_slot):
        if steps:

            @pl.when(slot == t)
            def _(steps=steps):
                for step in steps:
                    go(step)


def fill_heads(seg_ref, qkv_ref, h, k_s, q_s):
    n = seg_ref.shape[1]
    seg = seg_ref[...]
    row = lax.broadcasted_iota(jnp.int32, (64, n), 0)
    mark = jnp.where(row < 2, jnp.where(seg == row, 1.0, 0.0), 0.0)
    push = jnp.where(row < 2, jnp.where(seg == row, 0.0, FAR), 0.0)
    at = pl.multiple_of(h * 192, 64)
    keys = qkv_ref[pl.ds(at + 64, 64), :].astype(jnp.float32)
    k_s[...] = jnp.transpose(jnp.concatenate([keys, mark], axis=0)).astype(jnp.bfloat16)
    queries = qkv_ref[pl.ds(at, 64), :].astype(jnp.float32) * 0.125
    q_s[...] = jnp.concatenate([queries, push], axis=0).astype(jnp.bfloat16)


def attend_kernel(plan, n_in, *refs):
    seg_ref, packed_ref = refs[:2]
    owns = refs[2 : 2 + n_in]
    qkv_ref, ctx_ref, lse_ref, o_ref = refs[2 + n_in : 6 + n_in]
    wholes = refs[6 + n_in : 6 + 2 * n_in]
    k_s, q_s, ctx_s, asend, arecv, csend, crecv, osem, send, recv = refs[6 + 2 * n_in :]
    z, x, y, c = spot()
    me = y * 2 + c
    size = packed_ref.shape[1]
    greet(group=True)

    def bring(h, d):
        return group_copy(
            packed_ref.at[pl.ds((me ^ d) * ROWS_HERE + h * 192, 192)],
            qkv_ref.at[pl.ds(h * 192, 192), d * size : d * size + size],
            asend.at[h, d - 1], arecv.at[h, d - 1], me ^ d,
        )

    def give(h, d):
        return group_copy(
            ctx_s.at[pl.ds(h * 64, 64), d * size : d * size + size],
            ctx_ref.at[pl.ds(me * 64 * HEADS_HERE + h * 64, 64)],
            csend.at[h, d - 1], crecv.at[h, d - 1], me ^ d,
        )

    def given(h, d):
        ref = ctx_ref.at[pl.ds((me ^ d) * 64 * HEADS_HERE + h * 64, 64)]
        return group_copy(ref, ref, csend.at[h, d - 1], crecv.at[h, d - 1], me ^ d)

    own = pltpu.make_async_copy(packed_ref.at[pl.ds(me * ROWS_HERE, ROWS_HERE)], qkv_ref.at[:, 0:size], osem)
    own.start()
    for d in (2, 3, 1):
        bring(0, d).start()
    units = [Spread(owns[i], wholes[i], where, order, send.at[n], recv.at[n]) for n, (i, where, order) in enumerate(plan)]
    steps = waves(units)
    go(steps[0] if steps else [])
    tiles = 4 * size // QF
    by_slot = spaced(steps[1:], HEADS_HERE * tiles)
    own.wait()

    def head(h, unused):
        for d in (1, 2, 3):
            bring(h, d).wait_recv()

        @pl.when(h < HEADS_HERE - 1)
        def _():
            for d in (2, 3, 1):
                bring(jnp.minimum(h + 1, HEADS_HERE - 1), d).start()

        fill_heads(seg_ref, qkv_ref, h, k_s, q_s)

        def tile(i, unused):
            at = pl.ds(pl.multiple_of(i * QF, QF), QF)
            s = jnp.dot(k_s[...], q_s[:, at], preferred_element_type=jnp.float32)
            peak = jnp.max(fold_rows(s, jnp.maximum), axis=0, keepdims=True)
            e = jnp.exp(s - peak)
            denom = jnp.sum(fold_rows(e, jnp.add), axis=0, keepdims=True)
            values = qkv_ref[pl.ds(pl.multiple_of(h * 192 + 128, 64), 64), :]
            o = jnp.dot(values, e.astype(jnp.bfloat16), preferred_element_type=jnp.float32) * (1.0 / denom)
            rows = pl.ds(pl.multiple_of(h * 64, 64), 64)
            o_ref[rows, at] = o
            ctx_s[rows, at] = o.astype(jnp.bfloat16)
            lse_ref[h, :, at] = peak + jnp.log(denom)
            go_at(h * tiles + i, by_slot)
            return unused

        lax.fori_loop(0, tiles, tile, 0, unroll=True)
        for d in (2, 3, 1):
            give(h, d).start()
        ctx_ref[pl.ds(pl.multiple_of(me * 64 * HEADS_HERE + h * 64, 64), 64), :] = ctx_s[pl.ds(pl.multiple_of(h * 64, 64), 64), 0:size]
        return unused

    lax.fori_loop(0, HEADS_HERE, head, 0)
    for h in range(HEADS_HERE):
        for d in (1, 2, 3):
            given(h, d).wait_recv()
            give(h, d).wait_send()
            bring(h, d).wait_send()
    for unit in units:
        unit.finish()


def attend(seg, packed, shards, plan, collective_id=3):
    n = len(shards)
    size = packed.shape[1]
    vmem = pl.BlockSpec(memory_space=pltpu.VMEM)
    anywhere = pl.BlockSpec(memory_space=pl.ANY)
    sem = pltpu.SemaphoreType.DMA
    return pl.pallas_call(
        functools.partial(attend_kernel, plan, n),
        in_specs=[vmem, anywhere] + [anywhere] * n,
        out_specs=[vmem] * 4 + [anywhere] * n,
        out_shape=[
            jax.ShapeDtypeStruct((ROWS_HERE, 4 * size), jnp.bfloat16),
            jax.ShapeDtypeStruct((768, size), jnp.bfloat16),
            jax.ShapeDtypeStruct((HEADS_HERE, 1, 4 * size), jnp.float32),
            jax.ShapeDtypeStruct((64 * HEADS_HERE, 4 * size), jnp.float32),
        ]
        + [jax.ShapeDtypeStruct((4, 2, 2, 2) + s.shape, s.dtype) for s in shards],
        scratch_shapes=[
            pltpu.VMEM((4 * size, 128), jnp.bfloat16),
            pltpu.VMEM((128, 4 * size), jnp.bfloat16),
            pltpu.VMEM((64 * HEADS_HERE, 4 * size), jnp.bfloat16),
            sem((3, 3)), sem((3, 3)), sem((3, 3)), sem((3, 3)), sem,
            sem((max(len(plan), 1), 9)), sem((max(len(plan), 1), 10)),
        ],
        compiler_params=pltpu.CompilerParams(collective_id=collective_id, has_side_effects=True, vmem_limit_bytes=50 * 2**20),
    )(seg, packed, *shards)


def attend_back_kernel(plan, n_in, *refs):
    seg_ref, qkv_ref, lse_ref, o_ref, gc_ref = refs[:5]
    parts = refs[5 : 5 + n_in]
    gp_ref, norm_ref = refs[5 + n_in : 7 + n_in]
    outs = refs[7 + n_in : 7 + 2 * n_in]
    k_s, q_s, v_s, do_s, dk_s, dv_s, dq_s, gp_s, asend, arecv, csend, crecv, osem, send, recv = refs[7 + 2 * n_in : 22 + 2 * n_in]
    bufs = refs[22 + 2 * n_in :]
    z, x, y, c = spot()
    me = y * 2 + c
    size = gc_ref.shape[1]
    greet(group=True)

    def bring(h, d):
        return group_copy(
            gc_ref.at[pl.ds((me ^ d) * 64 * HEADS_HERE + h * 64, 64)],
            do_s.at[pl.ds(h * 64, 64), d * size : d * size + size],
            asend.at[h, d - 1], arecv.at[h, d - 1], me ^ d,
        )

    def give(h, d):
        return group_copy(
            gp_s.at[pl.ds(h * 192, 192), d * size : d * size + size],
            gp_ref.at[pl.ds(me * ROWS_HERE + h * 192, 192)],
            csend.at[h, d - 1], crecv.at[h, d - 1], me ^ d,
        )

    def given(h, d):
        ref = gp_ref.at[pl.ds((me ^ d) * ROWS_HERE + h * 192, 192)]
        return group_copy(ref, ref, csend.at[h, d - 1], crecv.at[h, d - 1], me ^ d)

    own = pltpu.make_async_copy(gc_ref.at[pl.ds(me * 64 * HEADS_HERE, 64 * HEADS_HERE)], do_s.at[:, 0:size], osem)
    own.start()
    for h in range(HEADS_HERE):
        for d in (2, 3, 1):
            bring(h, d).start()
    units = collect_units(plan, parts, outs, bufs, (), send, recv)
    steps = waves(units)
    go(steps[0] if steps else [])
    tiles = 4 * size // QT
    by_slot = spaced(steps[1:], HEADS_HERE * tiles)
    own.wait()

    def head(h, unused):
        for d in (1, 2, 3):
            bring(h, d).wait_recv()
        fill_heads(seg_ref, qkv_ref, h, k_s, q_s)
        first = pl.multiple_of(h * 192, 64)
        v_s[...] = jnp.transpose(qkv_ref[pl.ds(first + 128, 64), :].astype(jnp.float32)).astype(jnp.bfloat16)
        dk_s[...] = jnp.zeros_like(dk_s)
        dv_s[...] = jnp.zeros_like(dv_s)
        rows = pl.ds(pl.multiple_of(h * 64, 64), 64)

        def tile(i, unused):
            at = pl.ds(pl.multiple_of(i * QT, QT), QT)
            q = q_s[:, at]
            do = do_s[rows, at]
            delta = jnp.sum(do.astype(jnp.float32) * o_ref[rows, at], axis=0, keepdims=True)
            s = jnp.dot(k_s[...], q, preferred_element_type=jnp.float32)
            p = jnp.exp(s - lse_ref[h, :, at])
            dp = jnp.dot(v_s[...], do, preferred_element_type=jnp.float32)
            ds = (p * (dp - delta)).astype(jnp.bfloat16)
            p = p.astype(jnp.bfloat16)
            nt = (((1,), (1,)), ((), ()))
            dv_s[...] += lax.dot_general(do, p, nt, preferred_element_type=jnp.float32)
            dk_s[...] += lax.dot_general(q[:64], ds, nt, preferred_element_type=jnp.float32)
            dq_s[:, at] = jnp.dot(qkv_ref[pl.ds(first + 64, 64), :], ds, preferred_element_type=jnp.float32) * 0.125
            go_at(h * tiles + i, by_slot)
            return unused

        lax.fori_loop(0, tiles, tile, 0)
        gp_s[pl.ds(first, 64), :] = dq_s[...].astype(jnp.bfloat16)
        gp_s[pl.ds(first + 64, 64), :] = dk_s[...].astype(jnp.bfloat16)
        gp_s[pl.ds(first + 128, 64), :] = dv_s[...].astype(jnp.bfloat16)
        for d in (2, 3, 1):
            give(h, d).start()
        gp_ref[pl.ds(pl.multiple_of(me * ROWS_HERE + h * 192, 64), 192), :] = gp_s[pl.ds(first, 192), 0:size]
        return unused

    lax.fori_loop(0, HEADS_HERE, head, 0)
    for h in range(HEADS_HERE):
        for d in (1, 2, 3):
            given(h, d).wait_recv()
            give(h, d).wait_send()
            bring(h, d).wait_send()
    for unit in units:
        unit.finish()
    square_sum(outs, norm_ref)


def attend_back(seg, qkv, lse, o, gc, parts, plan, collective_id=4):
    n = len(parts)
    size = gc.shape[1]
    shapes = [p.shape[4:] for p in parts]
    vmem = pl.BlockSpec(memory_space=pltpu.VMEM)
    anywhere = pl.BlockSpec(memory_space=pl.ANY)
    sem = pltpu.SemaphoreType.DMA
    return pl.pallas_call(
        functools.partial(attend_back_kernel, plan, n),
        in_specs=[vmem] * 4 + [anywhere] + [anywhere] * n,
        out_specs=[vmem] * 2 + [vmem] * n,
        out_shape=[jax.ShapeDtypeStruct((4 * ROWS_HERE, size), jnp.bfloat16), jax.ShapeDtypeStruct((8, 128), jnp.float32)]
        + [jax.ShapeDtypeStruct(s, jnp.float32) for s in shapes],
        scratch_shapes=[
            pltpu.VMEM((4 * size, 128), jnp.bfloat16),
            pltpu.VMEM((128, 4 * size), jnp.bfloat16),
            pltpu.VMEM((4 * size, 64), jnp.bfloat16),
            pltpu.VMEM((64 * HEADS_HERE, 4 * size), jnp.bfloat16),
            pltpu.VMEM((64, 4 * size), jnp.float32),
            pltpu.VMEM((64, 4 * size), jnp.float32),
            pltpu.VMEM((64, 4 * size), jnp.float32),
            pltpu.VMEM((ROWS_HERE, 4 * size), jnp.bfloat16),
            sem((3, 3)), sem((3, 3)), sem((3, 3)), sem((3, 3)), sem,
            sem((max(len(plan), 1), 9)), sem((max(len(plan), 1), 10)),
        ]
        + collect_scratch(plan, shapes, jnp.bfloat16, ()),
        compiler_params=pltpu.CompilerParams(collective_id=collective_id, has_side_effects=True, vmem_limit_bytes=58 * 2**20),
    )(seg, qkv, lse, o, gc, *parts)


def close_kernel(side_plan, main_plan, n_in, *refs):
    cut_ref, cols_ref, grad_ref, conv_ref = refs[:4]
    parts = refs[4 : 4 + n_in]
    dx_ref, norm_ref, conv_out = refs[4 + n_in : 7 + n_in]
    outs = refs[7 + n_in : 7 + 2 * n_in]
    (gwin_s, taps_s, cols_s, dw_s, w_s, wp_s, send, recv, msend, mrecv, hsend, hrecv, wsem, csem) = refs[7 + 2 * n_in : 21 + 2 * n_in]
    bufs = refs[21 + 2 * n_in :]
    cut, last = cut_ref[0], cut_ref[1]
    greet(plane=True)
    halo_start(grad_ref, gwin_s, hsend, hrecv)
    count = len(collect_scratch(side_plan, [o.shape for o in outs], jnp.bfloat16, ()))
    side = collect_units(side_plan, parts, outs, bufs[:count], (), send, recv)
    main = collect_units(main_plan, [dw_s], [conv_out], bufs[count:], (0,), msend, mrecv)
    side_steps, main_steps = waves(side), waves(main)
    go(side_steps[0])
    gwin_s[HALF : HALF + OWN, :] = grad_ref[...]
    dx_ref[...] = jnp.zeros_like(dx_ref)
    wp_s[...] = jnp.zeros_like(wp_s)
    halo_end(grad_ref, gwin_s, hsend, hrecv)

    def load(z):
        return pltpu.make_async_copy(conv_ref.at[z], w_s.at[z % 2], wsem.at[z % 2])

    load(0).start()
    load(1).start()
    begin = jnp.where(cut <= HALF, 2 * HALF, HALF)
    end = jnp.where(last > 0, EXT, jnp.where(cut <= HALF + OWN, OWN + 2 * HALF, OWN + HALF))

    def pick(k):
        return pltpu.make_async_copy(cols_ref.at[pl.ds(2 * k, 2)], cols_s.at[k % 2], csem.at[k % 2])

    pick(0).start()
    row = lax.broadcasted_iota(jnp.int32, (ZROWS, 256), 0) + HALF
    owned = (row >= begin) & (row < end)
    by_slot = spaced(side_steps[1:], 8)

    def product(k, m, taps, half):
        own = jnp.concatenate([taps[HALF : HALF + ZROWS, h * 256 + half * 128 : h * 256 + half * 128 + 128] for h in range(2)], axis=1)
        own = jnp.where(owned, own.astype(jnp.float32), 0.0).astype(jnp.bfloat16)
        dw = lax.dot_general(own, cols_s[k % 2, m], (((0,), (0,)), ((), ())), preferred_element_type=jnp.float32).astype(jnp.bfloat16)
        for h in range(2):
            for a in range(4):
                dw_s[k // 2, k % 2, m, h, 4 * half + a] = dw[h * 128 + a * 32 : h * 128 + a * 32 + 24]

    def weights_low(k, unused):
        pick((k + 1) % 8).start()
        pick(k).wait()
        taps = [taps_of(take_rows(gwin_s, 2 * k + m, cut)) for m in range(2)]
        for m in range(2):
            taps_s[2 * k + m] = taps[m]
            product(k, m, taps[m], 0)
        go_at(k, by_slot)
        return unused

    lax.fori_loop(0, 8, weights_low, 0)
    soon = max(len(main) // 4, 1)
    by_slot = spaced(main_steps[:soon], 8)

    def weights_high(k, unused):
        go_at(k, by_slot)
        pl.when(k < 7)(lambda: pick(k + 1).start())
        pick(k).wait()
        for m in range(2):
            product(k, m, taps_s[2 * k + m], 1)
        return unused

    lax.fori_loop(0, 8, weights_high, 0)
    more = spaced(main_steps[soon:], 8)

    def inputs(k, unused):
        go_at(k, more)
        pl.when(k % 2 == 0)(lambda: load(k // 2).wait())
        for m in range(2):
            for h in range(2):
                for a in range(8):
                    wp_s[m, h * 256 + a * 32 : h * 256 + a * 32 + 24, :] = w_s[(k // 2) % 2, k % 2, m, h, a]
        outs = [jnp.dot(taps_s[2 * k + m], wp_s[m], preferred_element_type=jnp.float32) for m in range(2)]
        for m in range(2):
            put_group(dx_ref, 2 * k + m, pick_own(fold_back(outs[m]), cut))
        pl.when((k % 2 == 1) & (k < 4))(lambda: load(k // 2 + 2).start())
        return unused

    lax.fori_loop(0, 8, inputs, 0)
    for unit in side + main:
        unit.finish()
    square_sum([conv_out] + list(outs), norm_ref)


def close_step(cut, columns, grad, conv, parts, side_plan, main_plan, collective_id=2):
    n = len(parts)
    shapes = [p.shape[4:] for p in parts]
    vmem = pl.BlockSpec(memory_space=pltpu.VMEM)
    anywhere = pl.BlockSpec(memory_space=pl.ANY)
    sem = pltpu.SemaphoreType.DMA
    low = jnp.bfloat16
    return pl.pallas_call(
        functools.partial(close_kernel, side_plan, main_plan, n),
        in_specs=[pl.BlockSpec(memory_space=pltpu.SMEM), anywhere, vmem, anywhere] + [anywhere] * n,
        out_specs=[vmem] * (3 + n),
        out_shape=[
            jax.ShapeDtypeStruct((OWN, 768), jnp.float32),
            jax.ShapeDtypeStruct((8, 128), jnp.float32),
            jax.ShapeDtypeStruct(conv.shape[4:], jnp.float32),
        ]
        + [jax.ShapeDtypeStruct(s, jnp.float32) for s in shapes],
        scratch_shapes=[
            pltpu.VMEM((WIN, 768), low),
            pltpu.VMEM((16, EXT, 512), low),
            pltpu.VMEM((2, 2, ZROWS, 768), low),
            pltpu.VMEM(conv.shape, low),
            pltpu.VMEM((2,) + conv.shape[1:], low),
            pltpu.VMEM((2, 512, 768), low),
            sem((len(side_plan), 9)), sem((len(side_plan), 10)), sem((len(main_plan), 9)), sem((len(main_plan), 10)),
            sem((2,)), sem((2,)), sem((2,)), sem((2,)),
        ]
        + collect_scratch(side_plan, shapes, low, ())
        + collect_scratch(main_plan, [conv.shape[4:]], low, (0,)),
        compiler_params=pltpu.CompilerParams(collective_id=collective_id, has_side_effects=True, vmem_limit_bytes=60 * 2**20),
    )(cut, columns, grad, conv, *parts)


def norm_kernel(n_in, *refs):
    ins, norm_ref, tiles, send, recv = refs[:n_in], refs[n_in], refs[n_in + 1], refs[n_in + 2], refs[n_in + 3]
    greet(plane=True)
    z, x, y, c = spot()
    mine = tiles.at[x * 4 + y * 2 + c]
    square_sum(ins[1:], mine)
    mine[...] += ins[0][...]
    total_square(norm_ref, tiles, send, recv)


def norm_step(tile, sums, collective_id=5):
    n = 1 + len(sums)
    vmem = pl.BlockSpec(memory_space=pltpu.VMEM)
    return pl.pallas_call(
        functools.partial(norm_kernel, n),
        in_specs=[vmem] * n,
        out_specs=vmem,
        out_shape=jax.ShapeDtypeStruct((8, 128), jnp.float32),
        scratch_shapes=[pltpu.VMEM((12, 8, 128), jnp.float32), pltpu.SemaphoreType.DMA((11,)), pltpu.SemaphoreType.DMA((11,))],
        compiler_params=pltpu.CompilerParams(collective_id=collective_id, has_side_effects=True, vmem_limit_bytes=32 * 2**20),
    )(tile, *sums)


S = slice


def sliced(index, axis, size, count, orders, first=0):
    step = size // count
    return [
        (index, (S(None),) * axis + (S(step * i, step * i + step),), orders[(first + i) % len(orders)]) for i in range(count)
    ]


def open_plan():
    even = ("xy", "yx")
    return sliced(0, 0, 8, 8, even) + sliced(1, 1, 2304, 2, even) + [(3, (), "xy"), (2, (), "yx")]


def attend_plan():
    return sliced(0, 1, 3072, 4, ("yx",)) + sliced(1, 0, 96, 3, ("yx",))


def attend_back_plan():
    plan = []
    for a in range(3):
        plan += [(1, (S(32 * a, 32 * a + 32), S(384 * i, 384 * i + 384)), ("xy", "yx")[i]) for i in range(2)]
    return plan + [(0, (), "xy")]


def side_plan():
    return sliced(0, 1, 2304, 2, ("xy", "yx")) + [(1, (), "xy")]


def main_plan():
    plan = []
    for a in range(8):
        plan += [(0, (S(a, a + 1), S(None), S(384 * i, 384 * i + 384)), ("xy", "yx")[i]) for i in range(2)]
    return plan


def by_chips():
    return lax.axis_size("seq") == 8 and lax.axis_size("head") == 4


def gather_weights(parts):
    return [lax.all_gather(p, ("seq", "head"), axis=0) for p in parts]


def collect_grads(parts):
    outs = [lax.psum_scatter(p.astype(jnp.float32), ("seq", "head"), scatter_dimension=0, tiled=False) for p in parts]
    square = jnp.zeros((), jnp.float32)
    for out in outs:
        square = square + jnp.sum(out * out)
    return outs, lax.psum(square, ("seq", "head"))


def by_owner(part):
    return part.reshape((4, 2, 2, 2) + part.shape[1:])


def trade(pieces):
    count = lax.axis_size("head")
    return [pieces[0]] + [lax.ppermute(pieces[d], "head", [(i, i ^ d) for i in range(count)]) for d in range(1, count)]


def by_partner(stacked):
    me = lax.axis_index("head")
    return [lax.dynamic_index_in_dim(stacked, me ^ d, 0, keepdims=False) for d in range(stacked.shape[0])]


def from_partner(pieces):
    me = lax.axis_index("head")
    stacked = jnp.stack(pieces)
    return jnp.concatenate([lax.dynamic_index_in_dim(stacked, me ^ j, 0, keepdims=False) for j in range(len(pieces))], axis=0)


def shards(
    frames, output_grad, segment_ids, qkv_weight, proj_weight, up_weight, down_weight, conv_weight, bias_gains, ffn_bias,
    qkv_first, proj_first, up_first, down_first, conv_first, bias_gains_first, ffn_bias_first,
    qkv_second, proj_second, up_second, down_second, conv_second, bias_gains_second, ffn_bias_second,
):
    low_type = jnp.bfloat16
    f32 = jnp.float32
    count = lax.axis_size("seq") * lax.axis_size("head")
    row_count, model_width = frames.shape
    head_groups = lax.axis_size("head")
    head_index = lax.axis_index("head")
    kernel_len, conv_rows, group_width = conv_weight.shape
    vec_rows, vec_cols = bias_gains.shape
    ffn_cols = ffn_bias.shape[0]
    conv_low = conv_weight.astype(low_type).reshape(16, 8, conv_rows, group_width).transpose(1, 2, 0, 3).reshape(8, conv_rows, 768)
    small = jnp.concatenate([bias_gains.astype(low_type).reshape(-1), ffn_bias.astype(low_type)])
    small = jnp.pad(small, (0, 2048 - small.shape[0])).reshape(16, 128)
    own_parts = [
        conv_low, qkv_weight.astype(low_type), proj_weight.astype(low_type), up_weight.astype(low_type), down_weight.astype(low_type), small
    ]
    seg_group = segment_ids[0]
    half_kernel = kernel_len // 2
    boundary = jnp.sum((seg_group == 0).astype(jnp.int32))
    cut = jnp.clip(boundary - head_index * row_count + half_kernel, 0, row_count + kernel_len)
    cut = jnp.stack([cut, (head_index == head_groups - 1).astype(jnp.int32)]).astype(jnp.int32)
    if by_chips():
        early = own_parts[:3] + own_parts[5:]
        conv_pre, conv_columns, *parts = open_step(cut, frames, early, open_plan(), (1, 3))
        all_conv, all_qkv, all_proj, all_small = [w.reshape((32,) + w.shape[4:]) for w in parts]
        whole_conv = parts[0]
        all_up, all_down = gather_weights(own_parts[3:5])
    else:
        all_conv, all_qkv, all_proj, all_up, all_down, all_small = gather_weights(own_parts)
    full_qkv = all_qkv.reshape(model_width, -1)
    full_proj = all_proj.reshape(model_width, -1)
    full_conv = all_conv.reshape(16, 2, 24 // conv_rows, 8, conv_rows, 768).transpose(0, 1, 3, 2, 4, 5).reshape(16, 2, 8, 24, 768)
    all_small = all_small.reshape(count, 2048).astype(f32)
    vectors = all_small[:, : vec_rows * vec_cols].reshape(count, vec_rows, vec_cols).transpose(1, 0, 2).reshape(vec_rows, model_width)
    full_ffn = all_small[:, vec_rows * vec_cols : vec_rows * vec_cols + ffn_cols].reshape(-1)

    seg_rows = jnp.concatenate(by_partner(seg_group.reshape(head_groups, 1, row_count)), axis=1)

    if not by_chips():
        window = with_halo(frames, (("head", 0),), half_kernel)
        conv_pre = conv_fwd(cut, window, full_conv)
    conv_pre = conv_pre + vectors[0]
    conv_act, conv_act_back = jax.vjp(gelu_exact, conv_pre)
    hidden_one = frames.astype(f32) + conv_act
    attn_in = hidden_one.astype(low_type)
    zero_part = jnp.zeros((HEADS, HEAD_DIM), f32)
    qkv_bias = jnp.stack(
        [vectors[1].reshape(HEADS, HEAD_DIM), zero_part, vectors[2].reshape(HEADS, HEAD_DIM)], axis=1
    ).reshape(3 * model_width)
    packed = (
        lax.dot_general(full_qkv, attn_in, (((0,), (1,)), ((), ())), preferred_element_type=f32) + qkv_bias[:, None]
    ).astype(low_type)
    if by_chips():
        heads_qkv, context, log_sums, context_wide = attend(seg_rows, packed, [], [])
    else:
        blocks = trade(by_partner(packed.reshape(head_groups, -1, row_count)))
        fwd = attn_fwd(seg_rows, blocks)
        context = from_partner(trade(fwd[:4]))
    full_up = all_up.reshape(model_width, -1)
    full_down = all_down.reshape(-1, model_width)
    attn_out = lax.dot_general(context, full_proj, (((0,), (0,)), ((), ())), preferred_element_type=f32) + vectors[3]
    normed_one, norm_one_back = jax.vjp(layer_norm, hidden_one + attn_out, vectors[4], vectors[5])
    ffn_in = normed_one.astype(low_type)
    up_act, up_back = jax.vjp(gelu_exact, jnp.dot(ffn_in, full_up, preferred_element_type=f32) + full_ffn)
    hidden_mid = up_act.astype(low_type)
    hidden_three = normed_one + jnp.dot(hidden_mid, full_down, preferred_element_type=f32) + vectors[6]
    layer_out_full, norm_two_back = jax.vjp(layer_norm, hidden_three, vectors[7], vectors[8])
    grad_three, grad_gain_two, grad_shift_two = norm_two_back(output_grad.astype(f32))
    grad_ffn = grad_three.astype(low_type)
    grad_down = jnp.einsum("tf,td->fd", hidden_mid, grad_ffn, preferred_element_type=f32).astype(low_type)
    grad_down_bias = jnp.sum(grad_ffn.astype(f32), axis=0)
    (grad_up_pre,) = up_back(jnp.einsum("td,fd->tf", grad_ffn, full_down, preferred_element_type=f32))
    grad_up_low = grad_up_pre.astype(low_type)
    grad_up = jnp.einsum("td,tf->df", ffn_in, grad_up_low, preferred_element_type=f32).astype(low_type)
    grad_ffn_bias = jnp.sum(grad_up_low.astype(f32), axis=0)
    grad_normed = grad_three + jnp.einsum("tf,df->td", grad_up_low, full_up, preferred_element_type=f32)
    grad_two, grad_gain_one, grad_shift_one = norm_one_back(grad_normed)
    grad_attn = grad_two.astype(low_type)
    grad_proj = jnp.dot(context, grad_attn, preferred_element_type=f32).astype(low_type)
    grad_proj_bias = jnp.sum(grad_attn.astype(f32), axis=0)
    grad_context = lax.dot_general(full_proj, grad_attn, (((1,), (1,)), ((), ())), preferred_element_type=f32).astype(low_type)
    grad_proj, grad_up, grad_down = [
        g.reshape((count,) + w.shape) for g, w in ((grad_proj, proj_weight), (grad_up, up_weight), (grad_down, down_weight))
    ]
    if by_chips():
        sum_up = lax.psum_scatter(grad_up, ("seq", "head"), scatter_dimension=0, tiled=False).astype(f32)
        grad_packed, square_tile, sum_proj, sum_down = attend_back(
            seg_rows, heads_qkv, log_sums, context_wide, grad_context, [by_owner(grad_proj), by_owner(grad_down)], attend_back_plan()
        )
    else:
        grad_blocks = trade(by_partner(grad_context.reshape(head_groups, -1, row_count)))
        grad_packed = from_partner(trade(attn_bwd(seg_rows, blocks, grad_blocks, fwd[4], fwd[5])))
    grad_qkv = lax.dot_general(attn_in, grad_packed, (((0,), (1,)), ((), ())), preferred_element_type=f32).astype(low_type)
    grad_split = jnp.sum(grad_packed.astype(f32), axis=1).reshape(HEADS, 3, HEAD_DIM)
    grad_query_bias = grad_split[:, 0].reshape(model_width)
    grad_value_bias = grad_split[:, 2].reshape(model_width)
    grad_hidden_one = grad_two + lax.dot_general(grad_packed, full_qkv, (((0,), (1,)), ((), ())), preferred_element_type=f32)
    (grad_conv_pre,) = conv_act_back(grad_hidden_one)
    grad_conv_low = grad_conv_pre.astype(low_type)
    grad_conv_bias = jnp.sum(grad_conv_low.astype(f32), axis=0)
    grad_vectors = jnp.stack(
        [
            grad_conv_bias, grad_query_bias, grad_value_bias, grad_proj_bias, grad_gain_one, grad_shift_one,
            grad_down_bias, grad_gain_two, grad_shift_two,
        ],
        axis=0,
    )
    grad_small = jnp.concatenate(
        [grad_vectors.reshape(vec_rows, count, vec_cols).transpose(1, 0, 2).reshape(count, -1), grad_ffn_bias.reshape(count, ffn_cols)], axis=1
    )
    grad_small = jnp.pad(grad_small, ((0, 0), (0, 2048 - grad_small.shape[1]))).astype(low_type).reshape(count, 16, 128)
    grad_qkv = grad_qkv.reshape((count,) + qkv_weight.shape)
    if by_chips():
        grad_frames_conv, norm_tile, sum_conv, sum_qkv, sum_small = close_step(
            cut, conv_columns, grad_conv_low, whole_conv, [by_owner(grad_qkv), by_owner(grad_small)], side_plan(), main_plan()
        )
        square_total = jnp.sum(norm_step(norm_tile + square_tile, [sum_up]))
    else:
        grad_window = with_halo(grad_conv_low, (("head", 0),), half_kernel)
        grad_frames_conv, grad_conv = conv_bwd(cut, window, grad_window, full_conv)
        grad_conv = grad_conv.reshape(16, 2, 8, 24 // conv_rows, conv_rows, 768).transpose(0, 1, 3, 2, 4, 5).reshape(count, 8, conv_rows, 768)
        (sum_conv, sum_qkv, sum_proj, sum_up, sum_down, sum_small), square_total = collect_grads(
            [grad_conv, grad_qkv, grad_proj, grad_up, grad_down, grad_small]
        )
    frames_grad = grad_hidden_one + grad_frames_conv
    sum_conv = sum_conv.reshape(8, conv_rows, 16, group_width).transpose(2, 0, 1, 3).reshape(conv_weight.shape)
    sum_small = sum_small.reshape(-1)
    sum_vectors = sum_small[: vec_rows * vec_cols].reshape(vec_rows, vec_cols)
    sum_ffn_bias = sum_small[vec_rows * vec_cols : vec_rows * vec_cols + ffn_cols]
    summed = (sum_qkv, sum_proj, sum_up, sum_down, sum_conv, sum_vectors, sum_ffn_bias)
    grad_norm = jnp.sqrt(square_total)
    factor = jnp.minimum(1.0, clip_bound / grad_norm)
    masters = (qkv_weight, proj_weight, up_weight, down_weight, conv_weight, bias_gains, ffn_bias)
    firsts = (qkv_first, proj_first, up_first, down_first, conv_first, bias_gains_first, ffn_bias_first)
    seconds = (qkv_second, proj_second, up_second, down_second, conv_second, bias_gains_second, ffn_bias_second)
    news, first_news, second_news = [], [], []
    for index in range(7):
        decay = matrix_decay if index < 5 else 0.0
        new_weight, first_new, second_new = adam_update(
            masters[index], summed[index] * factor, firsts[index], seconds[index], weight_rates[index], decay
        )
        news.append(new_weight)
        first_news.append(first_new)
        second_news.append(second_new)
    return (layer_out_full.astype(low_type), frames_grad, grad_norm, *news, *first_news, *second_news)


def solution(mesh):
    rows, both = P(("seq", "head"), None), ("seq", "head")
    weights = (rows, rows, rows, rows, P(None, both, None), P(None, both), P(both))
    return jax.shard_map(
        shards,
        mesh=mesh,
        in_specs=(rows, rows, P("seq", None)) + weights * 3,
        out_specs=(rows, rows, P()) + weights * 3,
        check_vma=False,
    )
```

```python
import functools

import jax
import jax.numpy as jnp
from jax import lax
from jax.experimental import pallas as pl
from jax.experimental.pallas import tpu as pltpu
from jax.sharding import PartitionSpec as P

HEADS = 12
HEAD_DIM = 64
STEP = 10


norm_eps = 1e-05
beta_first = 0.9
beta_second = 0.999
adam_eps = 1e-08
weight_rates = (0.02, 0.1, 0.02, 0.02, 0.02, 0.2, 0.2)
matrix_decay = 0.01
clip_bound = 1.0


def with_halo(cells, sides, width):
    for axis, dim in sides:
        count = lax.axis_size(axis)
        ends = count - 1
        head = lax.slice_in_dim(cells, 0, width, axis=dim)
        tail = lax.slice_in_dim(cells, cells.shape[dim] - width, cells.shape[dim], axis=dim)
        cells = jnp.concatenate(
            [
                lax.ppermute(tail, axis, [(i, (i + 1) % count) for i in range(ends)]),
                cells,
                lax.ppermute(head, axis, [((i + 1) % count, i) for i in range(ends)]),
            ],
            axis=dim,
        )
    return cells


def layer_norm(values, scale_gain, shift_row):
    center = values - jnp.mean(values, axis=-1, keepdims=True)
    spread = jnp.mean(center * center, axis=-1, keepdims=True)
    return center * lax.rsqrt(spread + norm_eps) * scale_gain + shift_row


def gelu_exact(values):
    return jax.nn.gelu(values, approximate=False)


def adam_update(weight, grad, first, second, rate, decay):
    first_new = beta_first * first + (1.0 - beta_first) * grad
    second_new = beta_second * second + (1.0 - beta_second) * grad * grad
    first_hat = first_new / (1.0 - beta_first**STEP)
    second_hat = second_new / (1.0 - beta_second**STEP)
    new_weight = weight - rate * (first_hat / (jnp.sqrt(second_hat) + adam_eps) + decay * weight)
    return (new_weight, first_new, second_new)


HALF = 64
OWN = 512
WIN = OWN + 2 * HALF
EXT = WIN + HALF
ZROWS = OWN + HALF + 8
CGW = 48

def up(v, n):
    return pltpu.roll(v, v.shape[0] - n, 0)

def down(v, n):
    return pltpu.roll(v, n, 0)

def left(v, n):
    return pltpu.roll(v, v.shape[1] - n, 1)

def right(v, n):
    return pltpu.roll(v, n, 1)

def place(g):
    tile = jnp.minimum(g * CGW // 128, 4)
    return pl.ds(pl.multiple_of(tile * 128, 128), 256), g * CGW - tile * 128

def take_group(ref, g):
    lanes, rem = place(g)
    wide = ref[:, lanes].astype(jnp.float32)
    return pltpu.roll(wide, 256 - rem, 1)[:, :128]

def gapped(xg, cut):
    row = lax.broadcasted_iota(jnp.int32, (EXT, 128), 0)
    zero = jnp.zeros((HALF, 128), jnp.float32)
    before = jnp.concatenate([xg, zero], axis=0)
    after = jnp.concatenate([zero, xg], axis=0)
    return jnp.where(row < cut, before, jnp.where(row < cut + HALF, 0.0, after))

def im2col(xg, rows):
    lane = lax.broadcasted_iota(jnp.int32, (rows, 128), 1)
    turned = {off: (right(xg, off) if off else xg) for off in range(0, 128, 16)}
    cols = []
    for v in range(6):
        acc = None
        for r in range(16):
            lo = CGW * r
            if lo + CGW <= 128 * v or lo >= 128 * (v + 1):
                continue
            piece = turned[lo % 128][8 * r : 8 * r + rows, :]
            acc = piece if acc is None else jnp.where(lane >= lo - 128 * v, piece, acc)
        cols.append(acc.astype(jnp.bfloat16))
    return jnp.concatenate(cols, axis=1)

def pad_weights(w_ref, wp_ref):
    for h in range(2):
        for a in range(8):
            wp_ref[pl.ds(h * 256 + a * 32, 24), :] = w_ref[0, h, a]

def fold_out(z):
    lane = lax.broadcasted_iota(jnp.int32, (ZROWS, 128), 1)
    u = []
    for h in range(2):
        t = z[:, h * 256 : h * 256 + 128] + up(z[:, h * 256 + 128 : h * 256 + 256], 4)
        u.append(t + left(up(t, 2), 64))
    v = jnp.where(lane < 64, u[0], right(u[1], 64))
    o = v + left(up(v, 1), 32)
    return jnp.where(lane < 24, o, left(o, 40))[: OWN + HALF]

def pick_own(o, cut):
    row = lax.broadcasted_iota(jnp.int32, (OWN, 128), 0) + HALF
    return jnp.where(row < cut, o[:OWN], o[HALF : OWN + HALF])

def put_group(out_ref, g, o):
    lanes, rem = place(g)
    lane = lax.broadcasted_iota(jnp.int32, (OWN, 128), 1)
    o = jnp.where(lane < CGW, o, 0.0)
    wide = jnp.concatenate([o, jnp.zeros((OWN, 128), jnp.float32)], axis=1)
    out_ref[:, lanes] += pltpu.roll(wide, rem, 1)

def conv_fwd_kernel(cut_ref, x_ref, w_ref, out_ref, wp_ref):
    g = pl.program_id(0)
    cut = cut_ref[0]
    @pl.when(g == 0)
    def _():
        wp_ref[...] = jnp.zeros_like(wp_ref)
        out_ref[...] = jnp.zeros_like(out_ref)
    pad_weights(w_ref, wp_ref)
    cols = im2col(gapped(take_group(x_ref, g), cut), ZROWS)
    z = lax.dot_general(cols, wp_ref[...], (((1,), (1,)), ((), ())), preferred_element_type=jnp.float32)
    put_group(out_ref, g, pick_own(fold_out(z), cut))

def conv_fwd(cut, xw, w):
    return pl.pallas_call(
        conv_fwd_kernel,
        grid_spec=pltpu.PrefetchScalarGridSpec(
            num_scalar_prefetch=1, grid=(16,),
            in_specs=[pl.BlockSpec((WIN, 768), lambda g, c: (0, 0)),
                      pl.BlockSpec((1, 2, 8, 24, 768), lambda g, c: (g, 0, 0, 0, 0))],
            out_specs=pl.BlockSpec((OWN, 768), lambda g, c: (0, 0)),
            scratch_shapes=[pltpu.VMEM((512, 768), jnp.bfloat16)]),
        out_shape=jax.ShapeDtypeStruct((OWN, 768), jnp.float32),
        compiler_params=pltpu.CompilerParams(vmem_limit_bytes=50 * 2**20),
        cost_estimate=pl.CostEstimate(flops=2 * 16 * 584 * 768 * 512, bytes_accessed=12_000_000, transcendentals=0),
    )(cut, xw, w)

def taps_of(gg):
    lane = lax.broadcasted_iota(jnp.int32, (EXT, 128), 1)
    low = jnp.where(lane < 24, gg, 0.0)
    high = jnp.where((lane >= 64) & (lane < 88), right(gg, 40), 0.0)
    s = low + high
    q = s + right(down(s, 1), 32)
    q2 = down(q, 2)
    parts = []
    for h in range(2):
        if h == 0:
            r = jnp.where(lane < 64, q, right(q2, 64))
        else:
            r = jnp.where(lane < 64, right(q, 64), q2)
        parts += [r, down(r, 4)]
    return jnp.concatenate([p.astype(jnp.bfloat16) for p in parts], axis=1)

def fold_back(z):
    n = OWN + HALF
    lane = lax.broadcasted_iota(jnp.int32, (n, 128), 1)
    a = [z[HALF:, 128 * i : 128 * i + 128] + z[: EXT - HALF, 384 + 128 * i : 512 + 128 * i] for i in range(3)]
    acc = None
    for r in range(8):
        lo = CGW * r
        first = HALF - 8 * r
        tile, off = lo // 128, lo % 128
        piece = a[tile][first : first + n]
        if off:
            piece = left(piece, off)
        if off + CGW > 128:
            piece = jnp.where(lane < 128 - off, piece, right(a[tile + 1][first : first + n], 128 - off))
        acc = piece if acc is None else acc + piece
    return acc

def conv_bwd_kernel(cut_ref, x_ref, g_ref, w_ref, dx_ref, dw_ref, wp_ref):
    g = pl.program_id(0)
    cut = cut_ref[0]
    @pl.when(g == 0)
    def _():
        wp_ref[...] = jnp.zeros_like(wp_ref)
        dx_ref[...] = jnp.zeros_like(dx_ref)
    pad_weights(w_ref, wp_ref)
    taps = taps_of(gapped(take_group(g_ref, g), cut))
    z = jnp.dot(taps, wp_ref[...], preferred_element_type=jnp.float32)
    put_group(dx_ref, g, pick_own(fold_back(z), cut))
    cols = im2col(gapped(take_group(x_ref, g), cut), ZROWS)
    row = lax.broadcasted_iota(jnp.int32, (ZROWS, 512), 0) + HALF
    begin = jnp.where(cut <= HALF, 2 * HALF, HALF)
    end = jnp.where(cut_ref[1] > 0, EXT, jnp.where(cut <= HALF + OWN, OWN + 2 * HALF, OWN + HALF))
    own = jnp.where((row >= begin) & (row < end), taps[HALF : HALF + ZROWS].astype(jnp.float32), 0.0).astype(jnp.bfloat16)
    dw = lax.dot_general(own, cols, (((0,), (0,)), ((), ())), preferred_element_type=jnp.float32)
    for h in range(2):
        for a in range(8):
            dw_ref[0, h, a] = dw[h * 256 + a * 32 : h * 256 + a * 32 + 24].astype(dw_ref.dtype)

def conv_bwd(cut, xw, gw, w, dtype=jnp.bfloat16):
    return pl.pallas_call(
        conv_bwd_kernel,
        grid_spec=pltpu.PrefetchScalarGridSpec(
            num_scalar_prefetch=1, grid=(16,),
            in_specs=[pl.BlockSpec((WIN, 768), lambda g, c: (0, 0)),
                      pl.BlockSpec((WIN, 768), lambda g, c: (0, 0)),
                      pl.BlockSpec((1, 2, 8, 24, 768), lambda g, c: (g, 0, 0, 0, 0))],
            out_specs=[pl.BlockSpec((OWN, 768), lambda g, c: (0, 0)),
                       pl.BlockSpec((1, 2, 8, 24, 768), lambda g, c: (g, 0, 0, 0, 0))],
            scratch_shapes=[pltpu.VMEM((512, 768), jnp.bfloat16)]),
        out_shape=[jax.ShapeDtypeStruct((OWN, 768), jnp.float32), jax.ShapeDtypeStruct((16, 2, 8, 24, 768), dtype)],
        compiler_params=pltpu.CompilerParams(vmem_limit_bytes=50 * 2**20),
        cost_estimate=pl.CostEstimate(flops=4 * 16 * 640 * 768 * 512, bytes_accessed=22_000_000, transcendentals=0),
    )(cut, xw, gw, w)


QT = 256
QF = 512
FAR = -1e30

def fold_rows(v, op):
    while v.shape[0] > 8:
        n = v.shape[0] // 2
        v = op(v[:n], v[n:])
    return v


def fill_keys(seg_ref, blocks, kq_ref, q_ref):
    n = seg_ref.shape[1]
    seg = seg_ref[...]
    row = lax.broadcasted_iota(jnp.int32, (64, n), 0)
    mark = jnp.where(row < 2, jnp.where(seg == row, 1.0, 0.0), 0.0)
    push = jnp.where(row < 2, jnp.where(seg == row, 0.0, FAR), 0.0)
    keys = jnp.concatenate([b[64:128, :] for b in blocks], axis=1).astype(jnp.float32)
    kq_ref[...] = jnp.transpose(jnp.concatenate([keys, mark], axis=0)).astype(jnp.bfloat16)
    queries = jnp.concatenate([b[0:64, :] for b in blocks], axis=1).astype(jnp.float32) * 0.125
    q_ref[...] = jnp.concatenate([queries, push], axis=0).astype(jnp.bfloat16)

def attn_fwd_kernel(seg_ref, b0, b1, b2, b3, c0, c1, c2, c3, lse_ref, o_ref, k_s, q_s, v_s):
    blocks = (b0, b1, b2, b3)
    n = seg_ref.shape[1]
    size = b0.shape[1]
    fill_keys(seg_ref, blocks, k_s, q_s)
    v_s[...] = jnp.concatenate([b[128:192, :] for b in blocks], axis=1)

    def tile(i, unused):
        at = pl.ds(pl.multiple_of(i * QT, QT), QT)
        s = jnp.dot(k_s[...], q_s[:, at], preferred_element_type=jnp.float32)
        peak = jnp.max(fold_rows(s, jnp.maximum), axis=0, keepdims=True)
        e = jnp.exp(s - peak)
        denom = jnp.sum(fold_rows(e, jnp.add), axis=0, keepdims=True)
        o = jnp.dot(v_s[...], e.astype(jnp.bfloat16), preferred_element_type=jnp.float32)
        o_ref[0, :, at] = o * (1.0 / denom)
        lse_ref[0, :, at] = peak + jnp.log(denom)
        return unused

    lax.fori_loop(0, n // QT, tile, 0)
    for j, c in enumerate((c0, c1, c2, c3)):
        c[...] = o_ref[0, :, j * size : (j + 1) * size].astype(jnp.bfloat16)

def attn_fwd(seg, blocks):
    size = blocks[0].shape[1]
    n = 4 * size
    heads = blocks[0].shape[0] // 192
    return pl.pallas_call(
        attn_fwd_kernel,
        grid=(heads,),
        in_specs=[pl.BlockSpec((1, n), lambda h: (0, 0))] + [pl.BlockSpec((192, size), lambda h: (h, 0))] * 4,
        out_specs=[pl.BlockSpec((64, size), lambda h: (h, 0))] * 4
        + [pl.BlockSpec((1, 1, n), lambda h: (h, 0, 0)), pl.BlockSpec((1, 64, n), lambda h: (h, 0, 0))],
        out_shape=[jax.ShapeDtypeStruct((heads * 64, size), jnp.bfloat16)] * 4
        + [jax.ShapeDtypeStruct((heads, 1, n), jnp.float32), jax.ShapeDtypeStruct((heads, 64, n), jnp.float32)],
        scratch_shapes=[pltpu.VMEM((n, 128), jnp.bfloat16), pltpu.VMEM((128, n), jnp.bfloat16), pltpu.VMEM((64, n), jnp.bfloat16)],
        compiler_params=pltpu.CompilerParams(vmem_limit_bytes=50 * 2**20),
        cost_estimate=pl.CostEstimate(flops=heads * n * n * 256, bytes_accessed=6_000_000, transcendentals=heads * n * n),
    )(seg, *blocks)

def attn_bwd_kernel(seg_ref, b0, b1, b2, b3, d0, d1, d2, d3, lse_ref, o_ref, g0, g1, g2, g3, k_s, q_s, v_s, kt_s, do_s, dk_s, dv_s, dq_s):
    blocks = (b0, b1, b2, b3)
    n = seg_ref.shape[1]
    size = b0.shape[1]
    fill_keys(seg_ref, blocks, k_s, q_s)
    v_s[...] = jnp.transpose(jnp.concatenate([b[128:192, :] for b in blocks], axis=1).astype(jnp.float32)).astype(jnp.bfloat16)
    kt_s[...] = jnp.concatenate([b[64:128, :] for b in blocks], axis=1)
    do_s[...] = jnp.concatenate([d[...] for d in (d0, d1, d2, d3)], axis=1)
    dk_s[...] = jnp.zeros_like(dk_s)
    dv_s[...] = jnp.zeros_like(dv_s)

    def tile(i, unused):
        at = pl.ds(pl.multiple_of(i * QT, QT), QT)
        q = q_s[:, at]
        do = do_s[:, at]
        delta = jnp.sum(do.astype(jnp.float32) * o_ref[0, :, at], axis=0, keepdims=True)
        s = jnp.dot(k_s[...], q, preferred_element_type=jnp.float32)
        p = jnp.exp(s - lse_ref[0, :, at])
        dp = jnp.dot(v_s[...], do, preferred_element_type=jnp.float32)
        ds = (p * (dp - delta)).astype(jnp.bfloat16)
        p = p.astype(jnp.bfloat16)
        nt = (((1,), (1,)), ((), ()))
        dv_s[...] += lax.dot_general(do, p, nt, preferred_element_type=jnp.float32)
        dk_s[...] += lax.dot_general(q[:64], ds, nt, preferred_element_type=jnp.float32)
        dq_s[:, at] = jnp.dot(kt_s[...], ds, preferred_element_type=jnp.float32) * 0.125
        return unused

    lax.fori_loop(0, n // QT, tile, 0)
    for j, g in enumerate((g0, g1, g2, g3)):
        span = slice(j * size, (j + 1) * size)
        g[0:64, :] = dq_s[:, span].astype(jnp.bfloat16)
        g[64:128, :] = dk_s[:, span].astype(jnp.bfloat16)
        g[128:192, :] = dv_s[:, span].astype(jnp.bfloat16)

def attn_bwd(seg, blocks, grads, lse, o):
    size = blocks[0].shape[1]
    n = 4 * size
    heads = blocks[0].shape[0] // 192
    return pl.pallas_call(
        attn_bwd_kernel,
        grid=(heads,),
        in_specs=[pl.BlockSpec((1, n), lambda h: (0, 0))] + [pl.BlockSpec((192, size), lambda h: (h, 0))] * 4
        + [pl.BlockSpec((64, size), lambda h: (h, 0))] * 4
        + [pl.BlockSpec((1, 1, n), lambda h: (h, 0, 0)), pl.BlockSpec((1, 64, n), lambda h: (h, 0, 0))],
        out_specs=[pl.BlockSpec((192, size), lambda h: (h, 0))] * 4,
        out_shape=[jax.ShapeDtypeStruct((heads * 192, size), jnp.bfloat16)] * 4,
        scratch_shapes=[pltpu.VMEM((n, 128), jnp.bfloat16), pltpu.VMEM((128, n), jnp.bfloat16), pltpu.VMEM((n, 64), jnp.bfloat16),
                        pltpu.VMEM((64, n), jnp.bfloat16), pltpu.VMEM((64, n), jnp.bfloat16),
                        pltpu.VMEM((64, n), jnp.float32), pltpu.VMEM((64, n), jnp.float32), pltpu.VMEM((64, n), jnp.float32)],
        compiler_params=pltpu.CompilerParams(vmem_limit_bytes=50 * 2**20),
        cost_estimate=pl.CostEstimate(flops=heads * n * n * 640, bytes_accessed=10_000_000, transcendentals=heads * n * n),
    )(seg, *blocks, *grads, lse, o)


MESH = pl.DeviceIdType.MESH
EVERY = slice(None)


def spot():
    seq, head = lax.axis_index("seq"), lax.axis_index("head")
    return seq // 2, seq % 2, head // 2, head % 2


def device(z, x, y, c):
    return {"seq": z * 2 + x, "head": y * 2 + c}


def hail(where):
    pl.semaphore_signal(pltpu.get_barrier_semaphore(), inc=1, device_id=where, device_id_type=MESH)


def greet(plane=False, group=False, halo=False):
    z, x, y, c = spot()
    for n in range(1, 4):
        hail(device(z ^ n, x, y, c))
    if plane:
        for n in range(1, 8):
            hail(device(z, x ^ (n >> 2), y ^ ((n >> 1) & 1), c ^ (n & 1)))
        pl.semaphore_wait(pltpu.get_barrier_semaphore(), 10)
        return
    count = 6
    hail(device(z, x, y, 1 - c))
    hail(device(z, x, 1 - y, c))
    hail(device(z, 1 - x, y, c))
    if group:
        hail(device(z, x, 1 - y, 1 - c))
        count = count + 1
    elif halo:
        far = y != c
        pl.when(far)(lambda: hail(device(z, x, 1 - y, 1 - c)))
        count = count + jnp.where(far, 1, 0)
    pl.semaphore_wait(pltpu.get_barrier_semaphore(), count)


class Unit:
    def remote(self, src, dst, n, to):
        return pltpu.make_async_remote_copy(
            src_ref=src, dst_ref=dst, send_sem=self.send.at[n], recv_sem=self.recv.at[n], device_id=to, device_id_type=MESH
        )

    def landed(self, ref, n):
        z, x, y, c = spot()
        return self.remote(ref, ref, n, device(z, x, y, 1 - c))


class Spread(Unit):
    heavy = (2, 1, 0, 3, 4)

    def __init__(self, own, whole, cut, order, send, recv):
        self.own, self.whole, self.cut, self.order, self.send, self.recv = own, whole, cut, order, send, recv

    def block(self, done, **given):
        z, x, y, c = spot()
        here = {"z": z, "x": x, "y": y, "c": c}
        lead = tuple(given[a] if a in given else (EVERY if a in done else here[a]) for a in "zxyc")
        return self.whole.at[lead + self.cut]

    def mine(self):
        return self.own.at[self.cut] if self.cut else self.own

    def columns(self):
        z, x, y, c = spot()
        return [self.remote(self.mine(), self.block(""), n - 1, device(z ^ n, x, y, c)) for n in range(1, 4)]

    def swap(self, k):
        z, x, y, c = spot()
        axis = (self.order + "c")[k]
        ref = self.block("z" + self.order[:k])
        to = {"x": device(z, 1 - x, y, c), "y": device(z, x, 1 - y, c), "c": device(z, x, y, 1 - c)}[axis]
        return self.remote(ref, ref, 3 + k, to)

    def swapped(self, k):
        z, x, y, c = spot()
        axis = (self.order + "c")[k]
        return self.landed(self.block("z" + self.order[:k], **{axis: {"x": 1 - x, "y": 1 - y, "c": 1 - c}[axis]}), 3 + k)

    def stage(self, n):
        z, x, y, c = spot()
        if n < 2:
            local = pltpu.make_async_copy(self.mine(), self.block(""), self.recv.at[6])
            local.start() if n == 0 else local.wait()
        if n == 0:
            for copy in self.columns():
                copy.start()
        elif n == 1:
            for m in range(1, 4):
                self.landed(self.block("", z=z ^ m), m - 1).wait_recv()
            self.swap(0).start()
        else:
            self.swapped(n - 2).wait_recv()
            if n < 4:
                self.swap(n - 1).start()

    def finish(self):
        for copy in self.columns() + [self.swap(k) for k in range(3)]:
            copy.wait_send()


def add_rows(dst, src):
    dst[...] = (dst[...].astype(jnp.float32) + src[...].astype(jnp.float32)).astype(dst.dtype)


class Collect(Unit):
    heavy = (0, 1, 2, 3, 4)

    def __init__(self, parts, out, cut, order, own, rc, r1, r2, rz, send, recv):
        self.parts, self.out, self.cut, self.order, self.send, self.recv = parts, out, cut, order, send, recv
        self.own, self.rc, self.r1, self.r2, self.rz = own, rc, r1, r2, rz

    def block(self, *lead):
        if self.own is None:
            z, x, y, c = spot()
            return self.parts.at[tuple(lead) + (c,) + self.cut]
        return self.own.at[tuple(lead)]

    def core(self):
        z, x, y, c = spot()
        return self.remote(self.parts.at[(EVERY, EVERY, EVERY, 1 - c) + self.cut], self.rc, 0, device(z, x, y, 1 - c))

    def load(self):
        z, x, y, c = spot()
        return pltpu.make_async_copy(self.parts.at[(EVERY, EVERY, EVERY, c) + self.cut], self.own, self.recv.at[6])

    def first(self):
        z, x, y, c = spot()
        if self.order[0] == "x":
            return self.remote(self.block(EVERY, 1 - x, EVERY), self.r1, 1, device(z, 1 - x, y, c))
        return self.remote(self.block(EVERY, EVERY, 1 - y), self.r1, 1, device(z, x, 1 - y, c))

    def second(self):
        z, x, y, c = spot()
        if self.order[0] == "x":
            return self.remote(self.block(EVERY, x, 1 - y), self.r2, 2, device(z, x, 1 - y, c))
        return self.remote(self.block(EVERY, 1 - x, y), self.r2, 2, device(z, 1 - x, y, c))

    def columns(self):
        z, x, y, c = spot()
        return [self.remote(self.block(z ^ n, x, y), self.rz.at[n - 1], 2 + n, device(z ^ n, x, y, c)) for n in range(1, 4)]

    def stage(self, n):
        z, x, y, c = spot()
        if n == 0:
            self.core().start()
            if self.own is not None:
                self.load().start()
        elif n == 1:
            self.landed(self.rc, 0).wait_recv()
            if self.own is not None:
                self.load().wait()

            def one(i, unused):
                for k in range(2):
                    for m in range(2):
                        add_rows(self.block(i, k, m), self.rc.at[i, k, m])
                return unused

            lax.fori_loop(0, 4, one, 0)
            self.first().start()
        elif n == 2:
            self.landed(self.r1, 1).wait_recv()

            def one(i, unused):
                for k in range(2):
                    add_rows(self.block(i, x, k) if self.order[0] == "x" else self.block(i, k, y), self.r1.at[i, k])
                return unused

            lax.fori_loop(0, 4, one, 0)
            self.second().start()
        elif n == 3:
            self.landed(self.r2, 2).wait_recv()

            def one(i, unused):
                add_rows(self.block(i, x, y), self.r2.at[i])
                return unused

            lax.fori_loop(0, 4, one, 0)
            for copy in self.columns():
                copy.start()
        else:
            total = self.block(z, x, y)[...].astype(jnp.float32)
            for m in range(1, 4):
                self.landed(self.rz.at[m - 1], 2 + m).wait_recv()
                total = total + self.rz[m - 1].astype(jnp.float32)
            out = self.out.at[self.cut] if self.cut else self.out
            out[...] = total

    def finish(self):
        for copy in [self.core(), self.first(), self.second()] + self.columns():
            copy.wait_send()


def unit_shape(shape, cut):
    cut = tuple(cut) + (slice(None),) * (len(shape) - len(cut))
    return tuple(len(range(*s.indices(d))) for s, d in zip(cut, shape))


def collect_scratch(plan, shapes, dtype, inside):
    scratch = []
    for i, cut, order in plan:
        m = unit_shape(shapes[i], cut)
        leads = [] if i in inside else [(4, 2, 2)]
        leads += [(4, 2, 2), (4, 2), (4,), (3,)]
        scratch += [pltpu.VMEM(lead + m, dtype) for lead in leads]
    return scratch


def collect_units(plan, parts, outs, bufs, inside, send, recv):
    units, bufs = [], list(bufs)
    for n, (i, cut, order) in enumerate(plan):
        own = None if i in inside else bufs.pop(0)
        units.append(Collect(parts[i], outs[i], cut, order, own, bufs.pop(0), bufs.pop(0), bufs.pop(0), bufs.pop(0), send.at[n], recv.at[n]))
    return units


STAGES = 5


def waves(units, width=2):
    rows = [units[i : i + width] for i in range(0, len(units), width)]
    steps = []
    for t in range(len(rows) + STAGES - 1 if rows else 0):
        steps.append([(unit, n) for n in units[0].heavy for unit in (rows[t - n] if 0 <= t - n < len(rows) else [])])
    return steps


def go(step):
    for unit, n in step:
        unit.stage(n)


def square_sum(refs, tile):
    tile[...] = jnp.zeros_like(tile)
    for ref in refs:
        v = ref[...]
        v = (v * v).reshape(-1, v.shape[-1])
        v = jnp.sum(v.reshape(-1, 8, v.shape[-1]), axis=0)
        for i in range(0, v.shape[-1], 128):
            tile[...] += v[:, i : i + 128]


def total_square(norm, tiles, send, recv):
    z, x, y, c = spot()
    mine = x * 4 + y * 2 + c
    copies = []

    def push(slot, n, to):
        copies.append(pltpu.make_async_remote_copy(
            src_ref=tiles.at[slot], dst_ref=tiles.at[slot], send_sem=send.at[n], recv_sem=recv.at[n], device_id=to, device_id_type=MESH))
        copies[-1].start()

    def pull(slot, n):
        ref = tiles.at[slot]
        pltpu.make_async_remote_copy(
            src_ref=ref, dst_ref=ref, send_sem=send.at[n], recv_sem=recv.at[n], device_id=device(z, x, y, 1 - c), device_id_type=MESH).wait_recv()

    for n in range(1, 8):
        push(mine, n, device(z, x ^ (n >> 2), y ^ ((n >> 1) & 1), c ^ (n & 1)))
    for n in range(1, 8):
        pull(mine ^ n, n)
    total = tiles[0]
    for n in range(1, 8):
        total = total + tiles[n]
    tiles[8 + z] = total
    for n in range(1, 4):
        push(8 + z, 7 + n, device(z ^ n, x, y, c))
    for n in range(1, 4):
        pull(8 + (z ^ n), 7 + n)
    norm[...] = (tiles[8] + tiles[9]) + (tiles[10] + tiles[11])
    for copy in copies:
        copy.wait_send()


def take_rows(win_ref, g, cut):
    return gapped(take_group(win_ref, g), cut)


def halo_copies(edges_ref, win_ref, send, recv):
    z, x, y, c = spot()
    h = y * 2 + c
    n = edges_ref.shape[0]

    def to(other):
        return {"seq": z * 2 + x, "head": other}

    def copy(src, dst, k, other):
        return pltpu.make_async_remote_copy(
            src_ref=src, dst_ref=dst, send_sem=send.at[k], recv_sem=recv.at[k], device_id=to(other), device_id_type=MESH)

    after = copy(edges_ref.at[n - HALF : n], win_ref.at[0:HALF], 0, h + 1)
    before = copy(edges_ref.at[0:HALF], win_ref.at[n + HALF : n + 2 * HALF], 1, h - 1)
    from_before = copy(win_ref.at[0:HALF], win_ref.at[0:HALF], 0, h ^ 1)
    from_after = copy(win_ref.at[n + HALF : n + 2 * HALF], win_ref.at[n + HALF : n + 2 * HALF], 1, h ^ 1)
    return (h < 3, after), (h > 0, before), (h > 0, from_before), (h < 3, from_after)


def halo_start(edges_ref, win_ref, send, recv):
    for ok, copy in halo_copies(edges_ref, win_ref, send, recv)[:2]:
        pl.when(ok)(copy.start)


def halo_end(edges_ref, win_ref, send, recv):
    n = edges_ref.shape[0]
    after, before, from_before, from_after = halo_copies(edges_ref, win_ref, send, recv)
    for (ok, copy), rows in ((from_before, slice(0, HALF)), (from_after, slice(n + HALF, n + 2 * HALF))):
        pl.when(ok)(copy.wait_recv)

        @pl.when(jnp.logical_not(ok))
        def _(rows=rows):
            win_ref[rows, :] = jnp.zeros((HALF, win_ref.shape[1]), win_ref.dtype)

    for ok, copy in (after, before):
        pl.when(ok)(copy.wait_send)


def open_kernel(plan, n_in, early, *refs):
    cut_ref, frames_ref = refs[:2]
    owns = refs[2 : 2 + n_in]
    out_ref, cols_ref = refs[2 + n_in : 4 + n_in]
    wholes = refs[4 + n_in : 4 + 2 * n_in]
    win_ref, cols_s, low_s, w_s, wp_s, send, recv, hsend, hrecv, wsem, csem = refs[4 + 2 * n_in :]
    cut = cut_ref[0]
    greet(halo=True)
    halo_start(frames_ref, win_ref, hsend, hrecv)
    units = [Spread(owns[i], wholes[i], where, order, send.at[n], recv.at[n]) for n, (i, where, order) in enumerate(plan)]
    steps = waves(units)
    go(steps[0])
    win_ref[HALF : HALF + OWN, :] = frames_ref[...]
    out_ref[...] = jnp.zeros_like(out_ref)
    wp_s[...] = jnp.zeros_like(wp_s)
    go(steps[1])
    halo_end(frames_ref, win_ref, hsend, hrecv)

    def columns(g, unused):
        cols_s[g] = im2col(take_rows(win_ref, g, cut), ZROWS)
        return unused

    def load(half, z):
        return pltpu.make_async_copy(wholes[0].at[z, :, :, :, 4 * half : 4 * half + 4], w_s.at[z], wsem.at[z])

    def product(g):
        z, x, y = g // 4, (g // 2) % 2, g % 2
        for h in range(2):
            for a in range(4):
                wp_s[h * 128 + a * 32 : h * 128 + a * 32 + 24, :] = w_s[z, x, y, h, a]
        return lax.dot_general(cols_s[g], wp_s[...], (((1,), (1,)), ((), ())), preferred_element_type=jnp.float32)

    def low(g, unused):
        low_s[g] = product(g)
        return unused

    def high(g, unused):
        z = jnp.concatenate([low_s[g], product(g)], axis=1)
        z = jnp.concatenate([z[:, 0:128], z[:, 256:384], z[:, 128:256], z[:, 384:512]], axis=1)
        put_group(out_ref, g, pick_own(fold_out(z), cut))
        return unused

    def keep(chunk):
        span = pl.ds(4 * chunk, 4)
        return pltpu.make_async_copy(cols_s.at[span], cols_ref.at[span], csem.at[chunk])

    t = 2
    for chunk in range(4):
        lax.fori_loop(4 * chunk, 4 * chunk + 4, columns, 0)
        keep(chunk).start()
        go(steps[t])
        t += 1
    done = 0
    while t < len(steps) or done < 2:
        if done < 2 and t - STAGES >= early[done]:
            for z in range(4):
                load(done, z).start()
            for z in range(4):
                load(done, z).wait()
                lax.fori_loop(4 * z, 4 * z + 4, (low, high)[done], 0)
                if t < len(steps) and z % 2 == 1:
                    go(steps[t])
                    t += 1
            done += 1
        elif t < len(steps):
            go(steps[t])
            t += 1
    for unit in units:
        unit.finish()
    for chunk in range(4):
        keep(chunk).wait()


def open_step(cut, frames, shards, plan, early, collective_id=1):
    n = len(shards)
    vmem = pl.BlockSpec(memory_space=pltpu.VMEM)
    anywhere = pl.BlockSpec(memory_space=pl.ANY)
    return pl.pallas_call(
        functools.partial(open_kernel, plan, n, early),
        in_specs=[pl.BlockSpec(memory_space=pltpu.SMEM), vmem] + [anywhere] * n,
        out_specs=[vmem, anywhere] + [anywhere] * n,
        out_shape=[jax.ShapeDtypeStruct((OWN, 768), jnp.float32), jax.ShapeDtypeStruct((16, ZROWS, 768), jnp.bfloat16)]
        + [jax.ShapeDtypeStruct((4, 2, 2, 2) + s.shape, s.dtype) for s in shards],
        scratch_shapes=[
            pltpu.VMEM((WIN, 768), jnp.bfloat16),
            pltpu.VMEM((16, ZROWS, 768), jnp.bfloat16),
            pltpu.VMEM((16, ZROWS, 256), jnp.float32),
            pltpu.VMEM((4, 2, 2, 2, 4, 24, 768), jnp.bfloat16),
            pltpu.VMEM((256, 768), jnp.bfloat16),
            pltpu.SemaphoreType.DMA((len(plan), 9)),
            pltpu.SemaphoreType.DMA((len(plan), 10)),
            pltpu.SemaphoreType.DMA((2,)),
            pltpu.SemaphoreType.DMA((2,)),
            pltpu.SemaphoreType.DMA((4,)),
            pltpu.SemaphoreType.DMA((4,)),
        ],
        compiler_params=pltpu.CompilerParams(collective_id=collective_id, has_side_effects=True, vmem_limit_bytes=56 * 2**20),
    )(cut, frames, *shards)


HEADS_HERE = 3
ROWS_HERE = 192 * HEADS_HERE


def group_copy(src, dst, send, recv, other):
    return pltpu.make_async_remote_copy(
        src_ref=src, dst_ref=dst, send_sem=send, recv_sem=recv, device_id={"head": other}, device_id_type=MESH
    )


def spaced(steps, slots):
    out = [[] for _ in range(slots)]
    for t, step in enumerate(steps):
        out[min(t * slots // max(len(steps), 1), slots - 1)].append(step)
    return out


def go_at(slot, by_slot):
    for t, steps in enumerate(by_slot):
        if steps:

            @pl.when(slot == t)
            def _(steps=steps):
                for step in steps:
                    go(step)


def fill_heads(seg_ref, qkv_ref, h, k_s, q_s):
    n = seg_ref.shape[1]
    seg = seg_ref[...]
    row = lax.broadcasted_iota(jnp.int32, (64, n), 0)
    mark = jnp.where(row < 2, jnp.where(seg == row, 1.0, 0.0), 0.0)
    push = jnp.where(row < 2, jnp.where(seg == row, 0.0, FAR), 0.0)
    at = pl.multiple_of(h * 192, 64)
    keys = qkv_ref[pl.ds(at + 64, 64), :].astype(jnp.float32)
    k_s[...] = jnp.transpose(jnp.concatenate([keys, mark], axis=0)).astype(jnp.bfloat16)
    queries = qkv_ref[pl.ds(at, 64), :].astype(jnp.float32) * 0.125
    q_s[...] = jnp.concatenate([queries, push], axis=0).astype(jnp.bfloat16)


def attend_kernel(plan, n_in, *refs):
    seg_ref, packed_ref = refs[:2]
    owns = refs[2 : 2 + n_in]
    qkv_ref, ctx_ref, lse_ref, o_ref = refs[2 + n_in : 6 + n_in]
    wholes = refs[6 + n_in : 6 + 2 * n_in]
    k_s, q_s, ctx_s, asend, arecv, csend, crecv, osem, send, recv = refs[6 + 2 * n_in :]
    z, x, y, c = spot()
    me = y * 2 + c
    size = packed_ref.shape[1]
    greet(group=True)

    def bring(h, d):
        return group_copy(
            packed_ref.at[pl.ds((me ^ d) * ROWS_HERE + h * 192, 192)],
            qkv_ref.at[pl.ds(h * 192, 192), d * size : d * size + size],
            asend.at[h, d - 1], arecv.at[h, d - 1], me ^ d,
        )

    def give(h, d):
        return group_copy(
            ctx_s.at[pl.ds(h * 64, 64), d * size : d * size + size],
            ctx_ref.at[pl.ds(me * 64 * HEADS_HERE + h * 64, 64)],
            csend.at[h, d - 1], crecv.at[h, d - 1], me ^ d,
        )

    def given(h, d):
        ref = ctx_ref.at[pl.ds((me ^ d) * 64 * HEADS_HERE + h * 64, 64)]
        return group_copy(ref, ref, csend.at[h, d - 1], crecv.at[h, d - 1], me ^ d)

    own = pltpu.make_async_copy(packed_ref.at[pl.ds(me * ROWS_HERE, ROWS_HERE)], qkv_ref.at[:, 0:size], osem)
    own.start()
    for d in (2, 3, 1):
        bring(0, d).start()
    units = [Spread(owns[i], wholes[i], where, order, send.at[n], recv.at[n]) for n, (i, where, order) in enumerate(plan)]
    steps = waves(units)
    go(steps[0] if steps else [])
    tiles = 4 * size // QF
    by_slot = spaced(steps[1:], HEADS_HERE * tiles)
    own.wait()

    def head(h, unused):
        for d in (1, 2, 3):
            bring(h, d).wait_recv()

        @pl.when(h < HEADS_HERE - 1)
        def _():
            for d in (2, 3, 1):
                bring(jnp.minimum(h + 1, HEADS_HERE - 1), d).start()

        fill_heads(seg_ref, qkv_ref, h, k_s, q_s)

        def tile(i, unused):
            at = pl.ds(pl.multiple_of(i * QF, QF), QF)
            s = jnp.dot(k_s[...], q_s[:, at], preferred_element_type=jnp.float32)
            peak = jnp.max(fold_rows(s, jnp.maximum), axis=0, keepdims=True)
            e = jnp.exp(s - peak)
            denom = jnp.sum(fold_rows(e, jnp.add), axis=0, keepdims=True)
            values = qkv_ref[pl.ds(pl.multiple_of(h * 192 + 128, 64), 64), :]
            o = jnp.dot(values, e.astype(jnp.bfloat16), preferred_element_type=jnp.float32) * (1.0 / denom)
            rows = pl.ds(pl.multiple_of(h * 64, 64), 64)
            o_ref[rows, at] = o
            ctx_s[rows, at] = o.astype(jnp.bfloat16)
            lse_ref[h, :, at] = peak + jnp.log(denom)
            go_at(h * tiles + i, by_slot)
            return unused

        lax.fori_loop(0, tiles, tile, 0, unroll=True)
        for d in (2, 3, 1):
            give(h, d).start()
        ctx_ref[pl.ds(pl.multiple_of(me * 64 * HEADS_HERE + h * 64, 64), 64), :] = ctx_s[pl.ds(pl.multiple_of(h * 64, 64), 64), 0:size]
        return unused

    lax.fori_loop(0, HEADS_HERE, head, 0)
    for h in range(HEADS_HERE):
        for d in (1, 2, 3):
            given(h, d).wait_recv()
            give(h, d).wait_send()
            bring(h, d).wait_send()
    for unit in units:
        unit.finish()


def attend(seg, packed, shards, plan, collective_id=3):
    n = len(shards)
    size = packed.shape[1]
    vmem = pl.BlockSpec(memory_space=pltpu.VMEM)
    anywhere = pl.BlockSpec(memory_space=pl.ANY)
    sem = pltpu.SemaphoreType.DMA
    return pl.pallas_call(
        functools.partial(attend_kernel, plan, n),
        in_specs=[vmem, anywhere] + [anywhere] * n,
        out_specs=[vmem] * 4 + [anywhere] * n,
        out_shape=[
            jax.ShapeDtypeStruct((ROWS_HERE, 4 * size), jnp.bfloat16),
            jax.ShapeDtypeStruct((768, size), jnp.bfloat16),
            jax.ShapeDtypeStruct((HEADS_HERE, 1, 4 * size), jnp.float32),
            jax.ShapeDtypeStruct((64 * HEADS_HERE, 4 * size), jnp.float32),
        ]
        + [jax.ShapeDtypeStruct((4, 2, 2, 2) + s.shape, s.dtype) for s in shards],
        scratch_shapes=[
            pltpu.VMEM((4 * size, 128), jnp.bfloat16),
            pltpu.VMEM((128, 4 * size), jnp.bfloat16),
            pltpu.VMEM((64 * HEADS_HERE, 4 * size), jnp.bfloat16),
            sem((3, 3)), sem((3, 3)), sem((3, 3)), sem((3, 3)), sem,
            sem((max(len(plan), 1), 9)), sem((max(len(plan), 1), 10)),
        ],
        compiler_params=pltpu.CompilerParams(collective_id=collective_id, has_side_effects=True, vmem_limit_bytes=50 * 2**20),
    )(seg, packed, *shards)


def attend_back_kernel(plan, n_in, *refs):
    seg_ref, qkv_ref, lse_ref, o_ref, gc_ref = refs[:5]
    parts = refs[5 : 5 + n_in]
    gp_ref, norm_ref = refs[5 + n_in : 7 + n_in]
    outs = refs[7 + n_in : 7 + 2 * n_in]
    k_s, q_s, v_s, do_s, dk_s, dv_s, dq_s, gp_s, asend, arecv, csend, crecv, osem, send, recv = refs[7 + 2 * n_in : 22 + 2 * n_in]
    bufs = refs[22 + 2 * n_in :]
    z, x, y, c = spot()
    me = y * 2 + c
    size = gc_ref.shape[1]
    greet(group=True)

    def bring(h, d):
        return group_copy(
            gc_ref.at[pl.ds((me ^ d) * 64 * HEADS_HERE + h * 64, 64)],
            do_s.at[pl.ds(h * 64, 64), d * size : d * size + size],
            asend.at[h, d - 1], arecv.at[h, d - 1], me ^ d,
        )

    def give(h, d):
        return group_copy(
            gp_s.at[pl.ds(h * 192, 192), d * size : d * size + size],
            gp_ref.at[pl.ds(me * ROWS_HERE + h * 192, 192)],
            csend.at[h, d - 1], crecv.at[h, d - 1], me ^ d,
        )

    def given(h, d):
        ref = gp_ref.at[pl.ds((me ^ d) * ROWS_HERE + h * 192, 192)]
        return group_copy(ref, ref, csend.at[h, d - 1], crecv.at[h, d - 1], me ^ d)

    own = pltpu.make_async_copy(gc_ref.at[pl.ds(me * 64 * HEADS_HERE, 64 * HEADS_HERE)], do_s.at[:, 0:size], osem)
    own.start()
    for h in range(HEADS_HERE):
        for d in (2, 3, 1):
            bring(h, d).start()
    units = collect_units(plan, parts, outs, bufs, (), send, recv)
    steps = waves(units)
    go(steps[0] if steps else [])
    tiles = 4 * size // QT
    by_slot = spaced(steps[1:], HEADS_HERE * tiles)
    own.wait()

    def head(h, unused):
        for d in (1, 2, 3):
            bring(h, d).wait_recv()
        fill_heads(seg_ref, qkv_ref, h, k_s, q_s)
        first = pl.multiple_of(h * 192, 64)
        v_s[...] = jnp.transpose(qkv_ref[pl.ds(first + 128, 64), :].astype(jnp.float32)).astype(jnp.bfloat16)
        dk_s[...] = jnp.zeros_like(dk_s)
        dv_s[...] = jnp.zeros_like(dv_s)
        rows = pl.ds(pl.multiple_of(h * 64, 64), 64)

        def tile(i, unused):
            at = pl.ds(pl.multiple_of(i * QT, QT), QT)
            q = q_s[:, at]
            do = do_s[rows, at]
            delta = jnp.sum(do.astype(jnp.float32) * o_ref[rows, at], axis=0, keepdims=True)
            s = jnp.dot(k_s[...], q, preferred_element_type=jnp.float32)
            p = jnp.exp(s - lse_ref[h, :, at])
            dp = jnp.dot(v_s[...], do, preferred_element_type=jnp.float32)
            ds = (p * (dp - delta)).astype(jnp.bfloat16)
            p = p.astype(jnp.bfloat16)
            nt = (((1,), (1,)), ((), ()))
            dv_s[...] += lax.dot_general(do, p, nt, preferred_element_type=jnp.float32)
            dk_s[...] += lax.dot_general(q[:64], ds, nt, preferred_element_type=jnp.float32)
            dq_s[:, at] = jnp.dot(qkv_ref[pl.ds(first + 64, 64), :], ds, preferred_element_type=jnp.float32) * 0.125
            go_at(h * tiles + i, by_slot)
            return unused

        lax.fori_loop(0, tiles, tile, 0)
        gp_s[pl.ds(first, 64), :] = dq_s[...].astype(jnp.bfloat16)
        gp_s[pl.ds(first + 64, 64), :] = dk_s[...].astype(jnp.bfloat16)
        gp_s[pl.ds(first + 128, 64), :] = dv_s[...].astype(jnp.bfloat16)
        for d in (2, 3, 1):
            give(h, d).start()
        gp_ref[pl.ds(pl.multiple_of(me * ROWS_HERE + h * 192, 64), 192), :] = gp_s[pl.ds(first, 192), 0:size]
        return unused

    lax.fori_loop(0, HEADS_HERE, head, 0)
    for h in range(HEADS_HERE):
        for d in (1, 2, 3):
            given(h, d).wait_recv()
            give(h, d).wait_send()
            bring(h, d).wait_send()
    for unit in units:
        unit.finish()
    square_sum(outs, norm_ref)


def attend_back(seg, qkv, lse, o, gc, parts, plan, collective_id=4):
    n = len(parts)
    size = gc.shape[1]
    shapes = [p.shape[4:] for p in parts]
    vmem = pl.BlockSpec(memory_space=pltpu.VMEM)
    anywhere = pl.BlockSpec(memory_space=pl.ANY)
    sem = pltpu.SemaphoreType.DMA
    return pl.pallas_call(
        functools.partial(attend_back_kernel, plan, n),
        in_specs=[vmem] * 4 + [anywhere] + [anywhere] * n,
        out_specs=[vmem] * 2 + [vmem] * n,
        out_shape=[jax.ShapeDtypeStruct((4 * ROWS_HERE, size), jnp.bfloat16), jax.ShapeDtypeStruct((8, 128), jnp.float32)]
        + [jax.ShapeDtypeStruct(s, jnp.float32) for s in shapes],
        scratch_shapes=[
            pltpu.VMEM((4 * size, 128), jnp.bfloat16),
            pltpu.VMEM((128, 4 * size), jnp.bfloat16),
            pltpu.VMEM((4 * size, 64), jnp.bfloat16),
            pltpu.VMEM((64 * HEADS_HERE, 4 * size), jnp.bfloat16),
            pltpu.VMEM((64, 4 * size), jnp.float32),
            pltpu.VMEM((64, 4 * size), jnp.float32),
            pltpu.VMEM((64, 4 * size), jnp.float32),
            pltpu.VMEM((ROWS_HERE, 4 * size), jnp.bfloat16),
            sem((3, 3)), sem((3, 3)), sem((3, 3)), sem((3, 3)), sem,
            sem((max(len(plan), 1), 9)), sem((max(len(plan), 1), 10)),
        ]
        + collect_scratch(plan, shapes, jnp.bfloat16, ()),
        compiler_params=pltpu.CompilerParams(collective_id=collective_id, has_side_effects=True, vmem_limit_bytes=58 * 2**20),
    )(seg, qkv, lse, o, gc, *parts)


def close_kernel(side_plan, main_plan, n_in, *refs):
    cut_ref, cols_ref, grad_ref, conv_ref = refs[:4]
    parts = refs[4 : 4 + n_in]
    dx_ref, norm_ref, conv_out = refs[4 + n_in : 7 + n_in]
    outs = refs[7 + n_in : 7 + 2 * n_in]
    (gwin_s, taps_s, cols_s, dw_s, w_s, wp_s, send, recv, msend, mrecv, hsend, hrecv, wsem, csem) = refs[7 + 2 * n_in : 21 + 2 * n_in]
    bufs = refs[21 + 2 * n_in :]
    cut, last = cut_ref[0], cut_ref[1]
    greet(plane=True)
    halo_start(grad_ref, gwin_s, hsend, hrecv)
    count = len(collect_scratch(side_plan, [o.shape for o in outs], jnp.bfloat16, ()))
    side = collect_units(side_plan, parts, outs, bufs[:count], (), send, recv)
    main = collect_units(main_plan, [dw_s], [conv_out], bufs[count:], (0,), msend, mrecv)
    side_steps, main_steps = waves(side), waves(main)
    go(side_steps[0])
    gwin_s[HALF : HALF + OWN, :] = grad_ref[...]
    dx_ref[...] = jnp.zeros_like(dx_ref)
    wp_s[...] = jnp.zeros_like(wp_s)
    halo_end(grad_ref, gwin_s, hsend, hrecv)

    def load(z):
        return pltpu.make_async_copy(conv_ref.at[z], w_s.at[z % 2], wsem.at[z % 2])

    load(0).start()
    load(1).start()
    begin = jnp.where(cut <= HALF, 2 * HALF, HALF)
    end = jnp.where(last > 0, EXT, jnp.where(cut <= HALF + OWN, OWN + 2 * HALF, OWN + HALF))

    def pick(k):
        return pltpu.make_async_copy(cols_ref.at[pl.ds(2 * k, 2)], cols_s.at[k % 2], csem.at[k % 2])

    pick(0).start()
    row = lax.broadcasted_iota(jnp.int32, (ZROWS, 256), 0) + HALF
    owned = (row >= begin) & (row < end)
    by_slot = spaced(side_steps[1:], 8)

    def product(k, m, taps, half):
        own = jnp.concatenate([taps[HALF : HALF + ZROWS, h * 256 + half * 128 : h * 256 + half * 128 + 128] for h in range(2)], axis=1)
        own = jnp.where(owned, own.astype(jnp.float32), 0.0).astype(jnp.bfloat16)
        dw = lax.dot_general(own, cols_s[k % 2, m], (((0,), (0,)), ((), ())), preferred_element_type=jnp.float32).astype(jnp.bfloat16)
        for h in range(2):
            for a in range(4):
                dw_s[k // 2, k % 2, m, h, 4 * half + a] = dw[h * 128 + a * 32 : h * 128 + a * 32 + 24]

    def weights_low(k, unused):
        pick((k + 1) % 8).start()
        pick(k).wait()
        taps = [taps_of(take_rows(gwin_s, 2 * k + m, cut)) for m in range(2)]
        for m in range(2):
            taps_s[2 * k + m] = taps[m]
            product(k, m, taps[m], 0)
        go_at(k, by_slot)
        return unused

    lax.fori_loop(0, 8, weights_low, 0)
    soon = max(len(main) // 4, 1)
    by_slot = spaced(main_steps[:soon], 8)

    def weights_high(k, unused):
        go_at(k, by_slot)
        pl.when(k < 7)(lambda: pick(k + 1).start())
        pick(k).wait()
        for m in range(2):
            product(k, m, taps_s[2 * k + m], 1)
        return unused

    lax.fori_loop(0, 8, weights_high, 0)
    more = spaced(main_steps[soon:], 8)

    def inputs(k, unused):
        go_at(k, more)
        pl.when(k % 2 == 0)(lambda: load(k // 2).wait())
        for m in range(2):
            for h in range(2):
                for a in range(8):
                    wp_s[m, h * 256 + a * 32 : h * 256 + a * 32 + 24, :] = w_s[(k // 2) % 2, k % 2, m, h, a]
        outs = [jnp.dot(taps_s[2 * k + m], wp_s[m], preferred_element_type=jnp.float32) for m in range(2)]
        for m in range(2):
            put_group(dx_ref, 2 * k + m, pick_own(fold_back(outs[m]), cut))
        pl.when((k % 2 == 1) & (k < 4))(lambda: load(k // 2 + 2).start())
        return unused

    lax.fori_loop(0, 8, inputs, 0)
    for unit in side + main:
        unit.finish()
    square_sum([conv_out] + list(outs), norm_ref)


def close_step(cut, columns, grad, conv, parts, side_plan, main_plan, collective_id=2):
    n = len(parts)
    shapes = [p.shape[4:] for p in parts]
    vmem = pl.BlockSpec(memory_space=pltpu.VMEM)
    anywhere = pl.BlockSpec(memory_space=pl.ANY)
    sem = pltpu.SemaphoreType.DMA
    low = jnp.bfloat16
    return pl.pallas_call(
        functools.partial(close_kernel, side_plan, main_plan, n),
        in_specs=[pl.BlockSpec(memory_space=pltpu.SMEM), anywhere, vmem, anywhere] + [anywhere] * n,
        out_specs=[vmem] * (3 + n),
        out_shape=[
            jax.ShapeDtypeStruct((OWN, 768), jnp.float32),
            jax.ShapeDtypeStruct((8, 128), jnp.float32),
            jax.ShapeDtypeStruct(conv.shape[4:], jnp.float32),
        ]
        + [jax.ShapeDtypeStruct(s, jnp.float32) for s in shapes],
        scratch_shapes=[
            pltpu.VMEM((WIN, 768), low),
            pltpu.VMEM((16, EXT, 512), low),
            pltpu.VMEM((2, 2, ZROWS, 768), low),
            pltpu.VMEM(conv.shape, low),
            pltpu.VMEM((2,) + conv.shape[1:], low),
            pltpu.VMEM((2, 512, 768), low),
            sem((len(side_plan), 9)), sem((len(side_plan), 10)), sem((len(main_plan), 9)), sem((len(main_plan), 10)),
            sem((2,)), sem((2,)), sem((2,)), sem((2,)),
        ]
        + collect_scratch(side_plan, shapes, low, ())
        + collect_scratch(main_plan, [conv.shape[4:]], low, (0,)),
        compiler_params=pltpu.CompilerParams(collective_id=collective_id, has_side_effects=True, vmem_limit_bytes=60 * 2**20),
    )(cut, columns, grad, conv, *parts)


def norm_kernel(n_in, *refs):
    ins, norm_ref, tiles, send, recv = refs[:n_in], refs[n_in], refs[n_in + 1], refs[n_in + 2], refs[n_in + 3]
    greet(plane=True)
    z, x, y, c = spot()
    mine = tiles.at[x * 4 + y * 2 + c]
    square_sum(ins[1:], mine)
    mine[...] += ins[0][...]
    total_square(norm_ref, tiles, send, recv)


def norm_step(tile, sums, collective_id=5):
    n = 1 + len(sums)
    vmem = pl.BlockSpec(memory_space=pltpu.VMEM)
    return pl.pallas_call(
        functools.partial(norm_kernel, n),
        in_specs=[vmem] * n,
        out_specs=vmem,
        out_shape=jax.ShapeDtypeStruct((8, 128), jnp.float32),
        scratch_shapes=[pltpu.VMEM((12, 8, 128), jnp.float32), pltpu.SemaphoreType.DMA((11,)), pltpu.SemaphoreType.DMA((11,))],
        compiler_params=pltpu.CompilerParams(collective_id=collective_id, has_side_effects=True, vmem_limit_bytes=32 * 2**20),
    )(tile, *sums)


FCH = 512


def norm_of(h, gain, shift):
    center = h - jnp.mean(h, axis=1, keepdims=True)
    r = lax.rsqrt(jnp.mean(center * center, axis=1, keepdims=True) + norm_eps)
    z = center * r
    return z, r, z * gain + shift


def norm_back(g, z, r, gain):
    gz = g * gain
    return r * (gz - jnp.mean(gz, axis=1, keepdims=True) - z * jnp.mean(gz * z, axis=1, keepdims=True))


def gelu_both(v):
    phi = 0.5 + 0.5 * lax.erf(v * (0.5**0.5))
    return v * phi, phi + v * (jnp.exp(-0.5 * v * v) * 0.3989422804014327)


def ffn_kernel(
    ctx_ref, proj_ref, up_ref, down_ref, h1_ref, og_ref, vec_ref, fb_ref,
    out_ref, mid_ref, gup_ref, gffn_ref, fin_ref, gtwo_ref, gattn_ref, gctx_ref, gvec_ref, gfb_ref,
    proj_s, up_s, down_s, slope_s, z_s, acc_s, g3_s, sem,
):
    f32, low = jnp.float32, jnp.bfloat16
    chunks = fb_ref.shape[1] // FCH
    nt = (((1,), (1,)), ((), ()))

    def fetch(k):
        if k == 0:
            return pltpu.make_async_copy(proj_ref, proj_s, sem.at[0])
        j = (k - 1) // 2
        if k % 2:
            return pltpu.make_async_copy(up_ref.at[:, j * FCH : j * FCH + FCH], up_s.at[j], sem.at[k])
        return pltpu.make_async_copy(down_ref.at[j * FCH : j * FCH + FCH, :], down_s.at[j], sem.at[k])

    for k in range(1 + 2 * chunks):
        fetch(k).start()
    row = lambda n: vec_ref[n : n + 1, :]
    fetch(0).wait()
    attn = lax.dot_general(ctx_ref[...], proj_s[...], (((0,), (0,)), ((), ())), preferred_element_type=f32)
    z1, r1, n1 = norm_of(h1_ref[...] + (attn + row(3)), row(4), row(5))
    z_s[...] = z1
    acc_s[...] = n1 + row(6)
    fin_ref[...] = n1.astype(low)
    for j in range(chunks):
        fetch(1 + 2 * j).wait()
        at = slice(j * FCH, j * FCH + FCH)
        pre = jnp.dot(fin_ref[...], up_s[j], preferred_element_type=f32) + fb_ref[:, at]
        act, slope = gelu_both(pre)
        slope_s[:, at] = slope
        mid_ref[:, at] = act.astype(low)
        fetch(2 + 2 * j).wait()
        acc_s[...] += jnp.dot(mid_ref[:, at], down_s[j], preferred_element_type=f32)
    z3, r3, out = norm_of(acc_s[...], row(7), row(8))
    out_ref[...] = out.astype(low)
    og = og_ref[...].astype(f32)
    gvec_ref[7:8, :] = jnp.sum(og * z3, axis=0, keepdims=True)
    gvec_ref[8:9, :] = jnp.sum(og, axis=0, keepdims=True)
    g3 = norm_back(og, z3, r3, row(7))
    g3_s[...] = g3
    gffn_ref[...] = g3.astype(low)
    gvec_ref[6:7, :] = jnp.sum(gffn_ref[...].astype(f32), axis=0, keepdims=True)
    for j in range(chunks):
        at = slice(j * FCH, j * FCH + FCH)
        gu = (lax.dot_general(gffn_ref[...], down_s[j], nt, preferred_element_type=f32) * slope_s[:, at]).astype(low)
        gup_ref[:, at] = gu
        gfb_ref[:, at] = jnp.sum(gu.astype(f32), axis=0, keepdims=True)
        g3_s[...] += lax.dot_general(gu, up_s[j], nt, preferred_element_type=f32)
    gn = g3_s[...]
    z1 = z_s[...]
    gvec_ref[4:5, :] = jnp.sum(gn * z1, axis=0, keepdims=True)
    gvec_ref[5:6, :] = jnp.sum(gn, axis=0, keepdims=True)
    g2 = norm_back(gn, z1, r1, row(4))
    gtwo_ref[...] = g2
    gattn_ref[...] = g2.astype(low)
    gvec_ref[3:4, :] = jnp.sum(gattn_ref[...].astype(f32), axis=0, keepdims=True)
    gctx_ref[...] = lax.dot_general(proj_s[...], gattn_ref[...], nt, preferred_element_type=f32).astype(low)


def ffn_step(context, proj, up, down, hidden_one, output_grad, vectors, ffn_bias):
    rows, width = hidden_one.shape
    hidden = up.shape[1]
    low, f32 = jnp.bfloat16, jnp.float32
    vmem = pl.BlockSpec(memory_space=pltpu.VMEM)
    anywhere = pl.BlockSpec(memory_space=pl.ANY)
    shape = jax.ShapeDtypeStruct
    chunks = hidden // FCH
    return pl.pallas_call(
        ffn_kernel,
        in_specs=[vmem, anywhere, anywhere, anywhere, vmem, vmem, vmem, vmem],
        out_specs=[vmem] * 10,
        out_shape=[
            shape((rows, width), low), shape((rows, hidden), low), shape((rows, hidden), low), shape((rows, width), low),
            shape((rows, width), low), shape((rows, width), f32), shape((rows, width), low), shape((width, rows), low),
            shape((9, width), f32), shape((1, hidden), f32),
        ],
        scratch_shapes=[
            pltpu.VMEM((width, width), low), pltpu.VMEM((chunks, width, FCH), low), pltpu.VMEM((chunks, FCH, width), low),
            pltpu.VMEM((rows, hidden), f32), pltpu.VMEM((rows, width), f32), pltpu.VMEM((rows, width), f32), pltpu.VMEM((rows, width), f32),
            pltpu.SemaphoreType.DMA((1 + 2 * chunks,)),
        ],
        compiler_params=pltpu.CompilerParams(vmem_limit_bytes=56 * 2**20),
        cost_estimate=pl.CostEstimate(flops=2 * rows * width * (4 * hidden + 2 * width), bytes_accessed=24_000_000, transcendentals=2 * rows * hidden),
    )(context, proj, up, down, hidden_one, output_grad, vectors, ffn_bias)


S = slice


def sliced(index, axis, size, count, orders, first=0):
    step = size // count
    return [
        (index, (S(None),) * axis + (S(step * i, step * i + step),), orders[(first + i) % len(orders)]) for i in range(count)
    ]


def open_plan():
    even = ("xy", "yx")
    return sliced(0, 0, 8, 8, even) + sliced(1, 1, 2304, 2, even) + [(3, (), "xy"), (2, (), "yx")]


def attend_plan():
    return sliced(0, 1, 3072, 4, ("yx",)) + sliced(1, 0, 96, 3, ("yx",))


def attend_back_plan():
    plan = []
    for a in range(3):
        plan += [(1, (S(32 * a, 32 * a + 32), S(384 * i, 384 * i + 384)), ("xy", "yx")[i]) for i in range(2)]
    return plan + [(0, (), "xy")]


def side_plan():
    return sliced(0, 1, 2304, 2, ("xy", "yx")) + [(1, (), "xy")]


def main_plan():
    plan = []
    for a in range(8):
        plan += [(0, (S(a, a + 1), S(None), S(384 * i, 384 * i + 384)), ("xy", "yx")[i]) for i in range(2)]
    return plan


def by_chips():
    return lax.axis_size("seq") == 8 and lax.axis_size("head") == 4


def gather_weights(parts):
    return [lax.all_gather(p, ("seq", "head"), axis=0) for p in parts]


def collect_grads(parts):
    outs = [lax.psum_scatter(p.astype(jnp.float32), ("seq", "head"), scatter_dimension=0, tiled=False) for p in parts]
    square = jnp.zeros((), jnp.float32)
    for out in outs:
        square = square + jnp.sum(out * out)
    return outs, lax.psum(square, ("seq", "head"))


def by_owner(part):
    return part.reshape((4, 2, 2, 2) + part.shape[1:])


def trade(pieces):
    count = lax.axis_size("head")
    return [pieces[0]] + [lax.ppermute(pieces[d], "head", [(i, i ^ d) for i in range(count)]) for d in range(1, count)]


def by_partner(stacked):
    me = lax.axis_index("head")
    return [lax.dynamic_index_in_dim(stacked, me ^ d, 0, keepdims=False) for d in range(stacked.shape[0])]


def from_partner(pieces):
    me = lax.axis_index("head")
    stacked = jnp.stack(pieces)
    return jnp.concatenate([lax.dynamic_index_in_dim(stacked, me ^ j, 0, keepdims=False) for j in range(len(pieces))], axis=0)


def shards(
    frames, output_grad, segment_ids, qkv_weight, proj_weight, up_weight, down_weight, conv_weight, bias_gains, ffn_bias,
    qkv_first, proj_first, up_first, down_first, conv_first, bias_gains_first, ffn_bias_first,
    qkv_second, proj_second, up_second, down_second, conv_second, bias_gains_second, ffn_bias_second,
):
    low_type = jnp.bfloat16
    f32 = jnp.float32
    count = lax.axis_size("seq") * lax.axis_size("head")
    row_count, model_width = frames.shape
    head_groups = lax.axis_size("head")
    head_index = lax.axis_index("head")
    kernel_len, conv_rows, group_width = conv_weight.shape
    vec_rows, vec_cols = bias_gains.shape
    ffn_cols = ffn_bias.shape[0]
    conv_low = conv_weight.astype(low_type).reshape(16, 8, conv_rows, group_width).transpose(1, 2, 0, 3).reshape(8, conv_rows, 768)
    small = jnp.concatenate([bias_gains.astype(low_type).reshape(-1), ffn_bias.astype(low_type)])
    small = jnp.pad(small, (0, 2048 - small.shape[0])).reshape(16, 128)
    own_parts = [
        conv_low, qkv_weight.astype(low_type), proj_weight.astype(low_type), up_weight.astype(low_type), down_weight.astype(low_type), small
    ]
    seg_group = segment_ids[0]
    half_kernel = kernel_len // 2
    boundary = jnp.sum((seg_group == 0).astype(jnp.int32))
    cut = jnp.clip(boundary - head_index * row_count + half_kernel, 0, row_count + kernel_len)
    cut = jnp.stack([cut, (head_index == head_groups - 1).astype(jnp.int32)]).astype(jnp.int32)
    if by_chips():
        early = own_parts[:3] + own_parts[5:]
        conv_pre, conv_columns, *parts = open_step(cut, frames, early, open_plan(), (1, 3))
        all_conv, all_qkv, all_proj, all_small = [w.reshape((32,) + w.shape[4:]) for w in parts]
        whole_conv = parts[0]
        all_up, all_down = gather_weights(own_parts[3:5])
    else:
        all_conv, all_qkv, all_proj, all_up, all_down, all_small = gather_weights(own_parts)
    full_qkv = all_qkv.reshape(model_width, -1)
    full_proj = all_proj.reshape(model_width, -1)
    full_conv = all_conv.reshape(16, 2, 24 // conv_rows, 8, conv_rows, 768).transpose(0, 1, 3, 2, 4, 5).reshape(16, 2, 8, 24, 768)
    all_small = all_small.reshape(count, 2048).astype(f32)
    vectors = all_small[:, : vec_rows * vec_cols].reshape(count, vec_rows, vec_cols).transpose(1, 0, 2).reshape(vec_rows, model_width)
    full_ffn = all_small[:, vec_rows * vec_cols : vec_rows * vec_cols + ffn_cols].reshape(-1)

    seg_rows = jnp.concatenate(by_partner(seg_group.reshape(head_groups, 1, row_count)), axis=1)

    if not by_chips():
        window = with_halo(frames, (("head", 0),), half_kernel)
        conv_pre = conv_fwd(cut, window, full_conv)
    conv_pre = conv_pre + vectors[0]
    conv_act, conv_act_back = jax.vjp(gelu_exact, conv_pre)
    hidden_one = frames.astype(f32) + conv_act
    attn_in = hidden_one.astype(low_type)
    zero_part = jnp.zeros((HEADS, HEAD_DIM), f32)
    qkv_bias = jnp.stack(
        [vectors[1].reshape(HEADS, HEAD_DIM), zero_part, vectors[2].reshape(HEADS, HEAD_DIM)], axis=1
    ).reshape(3 * model_width)
    packed = (
        lax.dot_general(full_qkv, attn_in, (((0,), (1,)), ((), ())), preferred_element_type=f32) + qkv_bias[:, None]
    ).astype(low_type)
    if by_chips():
        heads_qkv, context, log_sums, context_wide = attend(seg_rows, packed, [], [])
    else:
        blocks = trade(by_partner(packed.reshape(head_groups, -1, row_count)))
        fwd = attn_fwd(seg_rows, blocks)
        context = from_partner(trade(fwd[:4]))
    full_up = all_up.reshape(model_width, -1)
    full_down = all_down.reshape(-1, model_width)
    (
        layer_out, hidden_mid, grad_up_low, grad_ffn, ffn_in, grad_two, grad_attn, grad_context, grad_rows, grad_ffn_bias
    ) = ffn_step(context, full_proj, full_up, full_down, hidden_one, output_grad, vectors, full_ffn[None])
    grad_down = jnp.einsum("tf,td->fd", hidden_mid, grad_ffn, preferred_element_type=f32).astype(low_type)
    grad_up = jnp.einsum("td,tf->df", ffn_in, grad_up_low, preferred_element_type=f32).astype(low_type)
    grad_proj = jnp.dot(context, grad_attn, preferred_element_type=f32).astype(low_type)
    grad_proj, grad_up, grad_down = [
        g.reshape((count,) + w.shape) for g, w in ((grad_proj, proj_weight), (grad_up, up_weight), (grad_down, down_weight))
    ]
    if by_chips():
        sum_up = lax.psum_scatter(grad_up, ("seq", "head"), scatter_dimension=0, tiled=False).astype(f32)
        grad_packed, square_tile, sum_proj, sum_down = attend_back(
            seg_rows, heads_qkv, log_sums, context_wide, grad_context, [by_owner(grad_proj), by_owner(grad_down)], attend_back_plan()
        )
    else:
        grad_blocks = trade(by_partner(grad_context.reshape(head_groups, -1, row_count)))
        grad_packed = from_partner(trade(attn_bwd(seg_rows, blocks, grad_blocks, fwd[4], fwd[5])))
    grad_qkv = lax.dot_general(attn_in, grad_packed, (((0,), (1,)), ((), ())), preferred_element_type=f32).astype(low_type)
    grad_split = jnp.sum(grad_packed.astype(f32), axis=1).reshape(HEADS, 3, HEAD_DIM)
    grad_query_bias = grad_split[:, 0].reshape(model_width)
    grad_value_bias = grad_split[:, 2].reshape(model_width)
    grad_hidden_one = grad_two + lax.dot_general(grad_packed, full_qkv, (((0,), (1,)), ((), ())), preferred_element_type=f32)
    (grad_conv_pre,) = conv_act_back(grad_hidden_one)
    grad_conv_low = grad_conv_pre.astype(low_type)
    grad_conv_bias = jnp.sum(grad_conv_low.astype(f32), axis=0)
    grad_vectors = jnp.concatenate([jnp.stack([grad_conv_bias, grad_query_bias, grad_value_bias], axis=0), grad_rows[3:]], axis=0)
    grad_small = jnp.concatenate(
        [grad_vectors.reshape(vec_rows, count, vec_cols).transpose(1, 0, 2).reshape(count, -1), grad_ffn_bias.reshape(count, ffn_cols)], axis=1
    )
    grad_small = jnp.pad(grad_small, ((0, 0), (0, 2048 - grad_small.shape[1]))).astype(low_type).reshape(count, 16, 128)
    grad_qkv = grad_qkv.reshape((count,) + qkv_weight.shape)
    if by_chips():
        grad_frames_conv, norm_tile, sum_conv, sum_qkv, sum_small = close_step(
            cut, conv_columns, grad_conv_low, whole_conv, [by_owner(grad_qkv), by_owner(grad_small)], side_plan(), main_plan()
        )
        square_total = jnp.sum(norm_step(norm_tile + square_tile, [sum_up]))
    else:
        grad_window = with_halo(grad_conv_low, (("head", 0),), half_kernel)
        grad_frames_conv, grad_conv = conv_bwd(cut, window, grad_window, full_conv)
        grad_conv = grad_conv.reshape(16, 2, 8, 24 // conv_rows, conv_rows, 768).transpose(0, 1, 3, 2, 4, 5).reshape(count, 8, conv_rows, 768)
        (sum_conv, sum_qkv, sum_proj, sum_up, sum_down, sum_small), square_total = collect_grads(
            [grad_conv, grad_qkv, grad_proj, grad_up, grad_down, grad_small]
        )
    frames_grad = grad_hidden_one + grad_frames_conv
    sum_conv = sum_conv.reshape(8, conv_rows, 16, group_width).transpose(2, 0, 1, 3).reshape(conv_weight.shape)
    sum_small = sum_small.reshape(-1)
    sum_vectors = sum_small[: vec_rows * vec_cols].reshape(vec_rows, vec_cols)
    sum_ffn_bias = sum_small[vec_rows * vec_cols : vec_rows * vec_cols + ffn_cols]
    summed = (sum_qkv, sum_proj, sum_up, sum_down, sum_conv, sum_vectors, sum_ffn_bias)
    grad_norm = jnp.sqrt(square_total)
    factor = jnp.minimum(1.0, clip_bound / grad_norm)
    masters = (qkv_weight, proj_weight, up_weight, down_weight, conv_weight, bias_gains, ffn_bias)
    firsts = (qkv_first, proj_first, up_first, down_first, conv_first, bias_gains_first, ffn_bias_first)
    seconds = (qkv_second, proj_second, up_second, down_second, conv_second, bias_gains_second, ffn_bias_second)
    news, first_news, second_news = [], [], []
    for index in range(7):
        decay = matrix_decay if index < 5 else 0.0
        new_weight, first_new, second_new = adam_update(
            masters[index], summed[index] * factor, firsts[index], seconds[index], weight_rates[index], decay
        )
        news.append(new_weight)
        first_news.append(first_new)
        second_news.append(second_new)
    return (layer_out, frames_grad, grad_norm, *news, *first_news, *second_news)


def solution(mesh):
    rows, both = P(("seq", "head"), None), ("seq", "head")
    weights = (rows, rows, rows, rows, P(None, both, None), P(None, both), P(both))
    return jax.shard_map(
        shards,
        mesh=mesh,
        in_specs=(rows, rows, P("seq", None)) + weights * 3,
        out_specs=(rows, rows, P()) + weights * 3,
        check_vma=False,
    )
```

```python
import functools

import jax
import jax.numpy as jnp
from jax import lax
from jax.experimental import pallas as pl
from jax.experimental.pallas import tpu as pltpu
from jax.sharding import PartitionSpec as P

HEADS = 12
HEAD_DIM = 64
STEP = 10


norm_eps = 1e-05
beta_first = 0.9
beta_second = 0.999
adam_eps = 1e-08
weight_rates = (0.02, 0.1, 0.02, 0.02, 0.02, 0.2, 0.2)
matrix_decay = 0.01
clip_bound = 1.0


def with_halo(cells, sides, width):
    for axis, dim in sides:
        count = lax.axis_size(axis)
        ends = count - 1
        head = lax.slice_in_dim(cells, 0, width, axis=dim)
        tail = lax.slice_in_dim(cells, cells.shape[dim] - width, cells.shape[dim], axis=dim)
        cells = jnp.concatenate(
            [
                lax.ppermute(tail, axis, [(i, (i + 1) % count) for i in range(ends)]),
                cells,
                lax.ppermute(head, axis, [((i + 1) % count, i) for i in range(ends)]),
            ],
            axis=dim,
        )
    return cells


def layer_norm(values, scale_gain, shift_row):
    center = values - jnp.mean(values, axis=-1, keepdims=True)
    spread = jnp.mean(center * center, axis=-1, keepdims=True)
    return center * lax.rsqrt(spread + norm_eps) * scale_gain + shift_row


def gelu_exact(values):
    return jax.nn.gelu(values, approximate=False)


def adam_update(weight, grad, first, second, rate, decay):
    first_new = beta_first * first + (1.0 - beta_first) * grad
    second_new = beta_second * second + (1.0 - beta_second) * grad * grad
    first_hat = first_new / (1.0 - beta_first**STEP)
    second_hat = second_new / (1.0 - beta_second**STEP)
    new_weight = weight - rate * (first_hat / (jnp.sqrt(second_hat) + adam_eps) + decay * weight)
    return (new_weight, first_new, second_new)


HALF = 64
OWN = 512
WIN = OWN + 2 * HALF
EXT = WIN + HALF
ZROWS = OWN + HALF + 8
CGW = 48

def up(v, n):
    return pltpu.roll(v, v.shape[0] - n, 0)

def down(v, n):
    return pltpu.roll(v, n, 0)

def left(v, n):
    return pltpu.roll(v, v.shape[1] - n, 1)

def right(v, n):
    return pltpu.roll(v, n, 1)

def place(g):
    tile = jnp.minimum(g * CGW // 128, 4)
    return pl.ds(pl.multiple_of(tile * 128, 128), 256), g * CGW - tile * 128

def take_group(ref, g):
    lanes, rem = place(g)
    wide = ref[:, lanes].astype(jnp.float32)
    return pltpu.roll(wide, 256 - rem, 1)[:, :128]

def gapped(xg, cut):
    row = lax.broadcasted_iota(jnp.int32, (EXT, 128), 0)
    zero = jnp.zeros((HALF, 128), jnp.float32)
    before = jnp.concatenate([xg, zero], axis=0)
    after = jnp.concatenate([zero, xg], axis=0)
    return jnp.where(row < cut, before, jnp.where(row < cut + HALF, 0.0, after))

def im2col(xg, rows):
    lane = lax.broadcasted_iota(jnp.int32, (rows, 128), 1)
    turned = {off: (right(xg, off) if off else xg) for off in range(0, 128, 16)}
    cols = []
    for v in range(6):
        acc = None
        for r in range(16):
            lo = CGW * r
            if lo + CGW <= 128 * v or lo >= 128 * (v + 1):
                continue
            piece = turned[lo % 128][8 * r : 8 * r + rows, :]
            acc = piece if acc is None else jnp.where(lane >= lo - 128 * v, piece, acc)
        cols.append(acc.astype(jnp.bfloat16))
    return jnp.concatenate(cols, axis=1)

def pad_weights(w_ref, wp_ref):
    for h in range(2):
        for a in range(8):
            wp_ref[pl.ds(h * 256 + a * 32, 24), :] = w_ref[0, h, a]

def fold_out(z):
    lane = lax.broadcasted_iota(jnp.int32, (ZROWS, 128), 1)
    u = []
    for h in range(2):
        t = z[:, h * 256 : h * 256 + 128] + up(z[:, h * 256 + 128 : h * 256 + 256], 4)
        u.append(t + left(up(t, 2), 64))
    v = jnp.where(lane < 64, u[0], right(u[1], 64))
    o = v + left(up(v, 1), 32)
    return jnp.where(lane < 24, o, left(o, 40))[: OWN + HALF]

def pick_own(o, cut):
    row = lax.broadcasted_iota(jnp.int32, (OWN, 128), 0) + HALF
    return jnp.where(row < cut, o[:OWN], o[HALF : OWN + HALF])

def put_group(out_ref, g, o):
    lanes, rem = place(g)
    lane = lax.broadcasted_iota(jnp.int32, (OWN, 128), 1)
    o = jnp.where(lane < CGW, o, 0.0)
    wide = jnp.concatenate([o, jnp.zeros((OWN, 128), jnp.float32)], axis=1)
    out_ref[:, lanes] += pltpu.roll(wide, rem, 1)

def conv_fwd_kernel(cut_ref, x_ref, w_ref, out_ref, wp_ref):
    g = pl.program_id(0)
    cut = cut_ref[0]
    @pl.when(g == 0)
    def _():
        wp_ref[...] = jnp.zeros_like(wp_ref)
        out_ref[...] = jnp.zeros_like(out_ref)
    pad_weights(w_ref, wp_ref)
    cols = im2col(gapped(take_group(x_ref, g), cut), ZROWS)
    z = lax.dot_general(cols, wp_ref[...], (((1,), (1,)), ((), ())), preferred_element_type=jnp.float32)
    put_group(out_ref, g, pick_own(fold_out(z), cut))

def conv_fwd(cut, xw, w):
    return pl.pallas_call(
        conv_fwd_kernel,
        grid_spec=pltpu.PrefetchScalarGridSpec(
            num_scalar_prefetch=1, grid=(16,),
            in_specs=[pl.BlockSpec((WIN, 768), lambda g, c: (0, 0)),
                      pl.BlockSpec((1, 2, 8, 24, 768), lambda g, c: (g, 0, 0, 0, 0))],
            out_specs=pl.BlockSpec((OWN, 768), lambda g, c: (0, 0)),
            scratch_shapes=[pltpu.VMEM((512, 768), jnp.bfloat16)]),
        out_shape=jax.ShapeDtypeStruct((OWN, 768), jnp.float32),
        compiler_params=pltpu.CompilerParams(vmem_limit_bytes=50 * 2**20),
        cost_estimate=pl.CostEstimate(flops=2 * 16 * 584 * 768 * 512, bytes_accessed=12_000_000, transcendentals=0),
    )(cut, xw, w)

def taps_of(gg):
    lane = lax.broadcasted_iota(jnp.int32, (EXT, 128), 1)
    low = jnp.where(lane < 24, gg, 0.0)
    high = jnp.where((lane >= 64) & (lane < 88), right(gg, 40), 0.0)
    s = low + high
    q = s + right(down(s, 1), 32)
    q2 = down(q, 2)
    parts = []
    for h in range(2):
        if h == 0:
            r = jnp.where(lane < 64, q, right(q2, 64))
        else:
            r = jnp.where(lane < 64, right(q, 64), q2)
        parts += [r, down(r, 4)]
    return jnp.concatenate([p.astype(jnp.bfloat16) for p in parts], axis=1)

def fold_back(z):
    n = OWN + HALF
    lane = lax.broadcasted_iota(jnp.int32, (n, 128), 1)
    a = [z[HALF:, 128 * i : 128 * i + 128] + z[: EXT - HALF, 384 + 128 * i : 512 + 128 * i] for i in range(3)]
    acc = None
    for r in range(8):
        lo = CGW * r
        first = HALF - 8 * r
        tile, off = lo // 128, lo % 128
        piece = a[tile][first : first + n]
        if off:
            piece = left(piece, off)
        if off + CGW > 128:
            piece = jnp.where(lane < 128 - off, piece, right(a[tile + 1][first : first + n], 128 - off))
        acc = piece if acc is None else acc + piece
    return acc

def conv_bwd_kernel(cut_ref, x_ref, g_ref, w_ref, dx_ref, dw_ref, wp_ref):
    g = pl.program_id(0)
    cut = cut_ref[0]
    @pl.when(g == 0)
    def _():
        wp_ref[...] = jnp.zeros_like(wp_ref)
        dx_ref[...] = jnp.zeros_like(dx_ref)
    pad_weights(w_ref, wp_ref)
    taps = taps_of(gapped(take_group(g_ref, g), cut))
    z = jnp.dot(taps, wp_ref[...], preferred_element_type=jnp.float32)
    put_group(dx_ref, g, pick_own(fold_back(z), cut))
    cols = im2col(gapped(take_group(x_ref, g), cut), ZROWS)
    row = lax.broadcasted_iota(jnp.int32, (ZROWS, 512), 0) + HALF
    begin = jnp.where(cut <= HALF, 2 * HALF, HALF)
    end = jnp.where(cut_ref[1] > 0, EXT, jnp.where(cut <= HALF + OWN, OWN + 2 * HALF, OWN + HALF))
    own = jnp.where((row >= begin) & (row < end), taps[HALF : HALF + ZROWS].astype(jnp.float32), 0.0).astype(jnp.bfloat16)
    dw = lax.dot_general(own, cols, (((0,), (0,)), ((), ())), preferred_element_type=jnp.float32)
    for h in range(2):
        for a in range(8):
            dw_ref[0, h, a] = dw[h * 256 + a * 32 : h * 256 + a * 32 + 24].astype(dw_ref.dtype)

def conv_bwd(cut, xw, gw, w, dtype=jnp.bfloat16):
    return pl.pallas_call(
        conv_bwd_kernel,
        grid_spec=pltpu.PrefetchScalarGridSpec(
            num_scalar_prefetch=1, grid=(16,),
            in_specs=[pl.BlockSpec((WIN, 768), lambda g, c: (0, 0)),
                      pl.BlockSpec((WIN, 768), lambda g, c: (0, 0)),
                      pl.BlockSpec((1, 2, 8, 24, 768), lambda g, c: (g, 0, 0, 0, 0))],
            out_specs=[pl.BlockSpec((OWN, 768), lambda g, c: (0, 0)),
                       pl.BlockSpec((1, 2, 8, 24, 768), lambda g, c: (g, 0, 0, 0, 0))],
            scratch_shapes=[pltpu.VMEM((512, 768), jnp.bfloat16)]),
        out_shape=[jax.ShapeDtypeStruct((OWN, 768), jnp.float32), jax.ShapeDtypeStruct((16, 2, 8, 24, 768), dtype)],
        compiler_params=pltpu.CompilerParams(vmem_limit_bytes=50 * 2**20),
        cost_estimate=pl.CostEstimate(flops=4 * 16 * 640 * 768 * 512, bytes_accessed=22_000_000, transcendentals=0),
    )(cut, xw, gw, w)


QT = 256
QF = 512
FAR = -1e30

def fold_rows(v, op):
    while v.shape[0] > 8:
        n = v.shape[0] // 2
        v = op(v[:n], v[n:])
    return v


def fill_keys(seg_ref, blocks, kq_ref, q_ref):
    n = seg_ref.shape[1]
    seg = seg_ref[...]
    row = lax.broadcasted_iota(jnp.int32, (64, n), 0)
    mark = jnp.where(row < 2, jnp.where(seg == row, 1.0, 0.0), 0.0)
    push = jnp.where(row < 2, jnp.where(seg == row, 0.0, FAR), 0.0)
    keys = jnp.concatenate([b[64:128, :] for b in blocks], axis=1).astype(jnp.float32)
    kq_ref[...] = jnp.transpose(jnp.concatenate([keys, mark], axis=0)).astype(jnp.bfloat16)
    queries = jnp.concatenate([b[0:64, :] for b in blocks], axis=1).astype(jnp.float32) * 0.125
    q_ref[...] = jnp.concatenate([queries, push], axis=0).astype(jnp.bfloat16)

def attn_fwd_kernel(seg_ref, b0, b1, b2, b3, c0, c1, c2, c3, lse_ref, o_ref, k_s, q_s, v_s):
    blocks = (b0, b1, b2, b3)
    n = seg_ref.shape[1]
    size = b0.shape[1]
    fill_keys(seg_ref, blocks, k_s, q_s)
    v_s[...] = jnp.concatenate([b[128:192, :] for b in blocks], axis=1)

    def tile(i, unused):
        at = pl.ds(pl.multiple_of(i * QT, QT), QT)
        s = jnp.dot(k_s[...], q_s[:, at], preferred_element_type=jnp.float32)
        peak = jnp.max(fold_rows(s, jnp.maximum), axis=0, keepdims=True)
        e = jnp.exp(s - peak)
        denom = jnp.sum(fold_rows(e, jnp.add), axis=0, keepdims=True)
        o = jnp.dot(v_s[...], e.astype(jnp.bfloat16), preferred_element_type=jnp.float32)
        o_ref[0, :, at] = o * (1.0 / denom)
        lse_ref[0, :, at] = peak + jnp.log(denom)
        return unused

    lax.fori_loop(0, n // QT, tile, 0)
    for j, c in enumerate((c0, c1, c2, c3)):
        c[...] = o_ref[0, :, j * size : (j + 1) * size].astype(jnp.bfloat16)

def attn_fwd(seg, blocks):
    size = blocks[0].shape[1]
    n = 4 * size
    heads = blocks[0].shape[0] // 192
    return pl.pallas_call(
        attn_fwd_kernel,
        grid=(heads,),
        in_specs=[pl.BlockSpec((1, n), lambda h: (0, 0))] + [pl.BlockSpec((192, size), lambda h: (h, 0))] * 4,
        out_specs=[pl.BlockSpec((64, size), lambda h: (h, 0))] * 4
        + [pl.BlockSpec((1, 1, n), lambda h: (h, 0, 0)), pl.BlockSpec((1, 64, n), lambda h: (h, 0, 0))],
        out_shape=[jax.ShapeDtypeStruct((heads * 64, size), jnp.bfloat16)] * 4
        + [jax.ShapeDtypeStruct((heads, 1, n), jnp.float32), jax.ShapeDtypeStruct((heads, 64, n), jnp.float32)],
        scratch_shapes=[pltpu.VMEM((n, 128), jnp.bfloat16), pltpu.VMEM((128, n), jnp.bfloat16), pltpu.VMEM((64, n), jnp.bfloat16)],
        compiler_params=pltpu.CompilerParams(vmem_limit_bytes=50 * 2**20),
        cost_estimate=pl.CostEstimate(flops=heads * n * n * 256, bytes_accessed=6_000_000, transcendentals=heads * n * n),
    )(seg, *blocks)

def attn_bwd_kernel(seg_ref, b0, b1, b2, b3, d0, d1, d2, d3, lse_ref, o_ref, g0, g1, g2, g3, k_s, q_s, v_s, kt_s, do_s, dk_s, dv_s, dq_s):
    blocks = (b0, b1, b2, b3)
    n = seg_ref.shape[1]
    size = b0.shape[1]
    fill_keys(seg_ref, blocks, k_s, q_s)
    v_s[...] = jnp.transpose(jnp.concatenate([b[128:192, :] for b in blocks], axis=1).astype(jnp.float32)).astype(jnp.bfloat16)
    kt_s[...] = jnp.concatenate([b[64:128, :] for b in blocks], axis=1)
    do_s[...] = jnp.concatenate([d[...] for d in (d0, d1, d2, d3)], axis=1)
    dk_s[...] = jnp.zeros_like(dk_s)
    dv_s[...] = jnp.zeros_like(dv_s)

    def tile(i, unused):
        at = pl.ds(pl.multiple_of(i * QT, QT), QT)
        q = q_s[:, at]
        do = do_s[:, at]
        delta = jnp.sum(do.astype(jnp.float32) * o_ref[0, :, at], axis=0, keepdims=True)
        s = jnp.dot(k_s[...], q, preferred_element_type=jnp.float32)
        p = jnp.exp(s - lse_ref[0, :, at])
        dp = jnp.dot(v_s[...], do, preferred_element_type=jnp.float32)
        ds = (p * (dp - delta)).astype(jnp.bfloat16)
        p = p.astype(jnp.bfloat16)
        nt = (((1,), (1,)), ((), ()))
        dv_s[...] += lax.dot_general(do, p, nt, preferred_element_type=jnp.float32)
        dk_s[...] += lax.dot_general(q[:64], ds, nt, preferred_element_type=jnp.float32)
        dq_s[:, at] = jnp.dot(kt_s[...], ds, preferred_element_type=jnp.float32) * 0.125
        return unused

    lax.fori_loop(0, n // QT, tile, 0)
    for j, g in enumerate((g0, g1, g2, g3)):
        span = slice(j * size, (j + 1) * size)
        g[0:64, :] = dq_s[:, span].astype(jnp.bfloat16)
        g[64:128, :] = dk_s[:, span].astype(jnp.bfloat16)
        g[128:192, :] = dv_s[:, span].astype(jnp.bfloat16)

def attn_bwd(seg, blocks, grads, lse, o):
    size = blocks[0].shape[1]
    n = 4 * size
    heads = blocks[0].shape[0] // 192
    return pl.pallas_call(
        attn_bwd_kernel,
        grid=(heads,),
        in_specs=[pl.BlockSpec((1, n), lambda h: (0, 0))] + [pl.BlockSpec((192, size), lambda h: (h, 0))] * 4
        + [pl.BlockSpec((64, size), lambda h: (h, 0))] * 4
        + [pl.BlockSpec((1, 1, n), lambda h: (h, 0, 0)), pl.BlockSpec((1, 64, n), lambda h: (h, 0, 0))],
        out_specs=[pl.BlockSpec((192, size), lambda h: (h, 0))] * 4,
        out_shape=[jax.ShapeDtypeStruct((heads * 192, size), jnp.bfloat16)] * 4,
        scratch_shapes=[pltpu.VMEM((n, 128), jnp.bfloat16), pltpu.VMEM((128, n), jnp.bfloat16), pltpu.VMEM((n, 64), jnp.bfloat16),
                        pltpu.VMEM((64, n), jnp.bfloat16), pltpu.VMEM((64, n), jnp.bfloat16),
                        pltpu.VMEM((64, n), jnp.float32), pltpu.VMEM((64, n), jnp.float32), pltpu.VMEM((64, n), jnp.float32)],
        compiler_params=pltpu.CompilerParams(vmem_limit_bytes=50 * 2**20),
        cost_estimate=pl.CostEstimate(flops=heads * n * n * 640, bytes_accessed=10_000_000, transcendentals=heads * n * n),
    )(seg, *blocks, *grads, lse, o)


MESH = pl.DeviceIdType.MESH
EVERY = slice(None)


def spot():
    seq, head = lax.axis_index("seq"), lax.axis_index("head")
    return seq // 2, seq % 2, head // 2, head % 2


def device(z, x, y, c):
    return {"seq": z * 2 + x, "head": y * 2 + c}


def hail(where):
    pl.semaphore_signal(pltpu.get_barrier_semaphore(), inc=1, device_id=where, device_id_type=MESH)


def greet(plane=False, group=False, halo=False):
    z, x, y, c = spot()
    for n in range(1, 4):
        hail(device(z ^ n, x, y, c))
    if plane:
        for n in range(1, 8):
            hail(device(z, x ^ (n >> 2), y ^ ((n >> 1) & 1), c ^ (n & 1)))
        pl.semaphore_wait(pltpu.get_barrier_semaphore(), 10)
        return
    count = 6
    hail(device(z, x, y, 1 - c))
    hail(device(z, x, 1 - y, c))
    hail(device(z, 1 - x, y, c))
    if group:
        hail(device(z, x, 1 - y, 1 - c))
        count = count + 1
    elif halo:
        far = y != c
        pl.when(far)(lambda: hail(device(z, x, 1 - y, 1 - c)))
        count = count + jnp.where(far, 1, 0)
    pl.semaphore_wait(pltpu.get_barrier_semaphore(), count)


class Unit:
    def remote(self, src, dst, n, to):
        return pltpu.make_async_remote_copy(
            src_ref=src, dst_ref=dst, send_sem=self.send.at[n], recv_sem=self.recv.at[n], device_id=to, device_id_type=MESH
        )

    def landed(self, ref, n):
        z, x, y, c = spot()
        return self.remote(ref, ref, n, device(z, x, y, 1 - c))


class Spread(Unit):
    heavy = (2, 1, 0, 3, 4)

    def __init__(self, own, whole, cut, order, send, recv):
        self.own, self.whole, self.cut, self.order, self.send, self.recv = own, whole, cut, order + "c", send, recv

    def block(self, k, **given):
        z, x, y, c = spot()
        here = {"z": z, "x": x, "y": y, "c": c}
        lead = tuple(given[a] if a in given else (EVERY if a in self.order[:k] else here[a]) for a in "zxyc")
        return self.whole.at[lead + self.cut]

    def mine(self):
        return self.own.at[self.cut] if self.cut else self.own

    def copies(self, k):
        z, x, y, c = spot()
        axis = self.order[k]
        ref = self.block(k)
        src = self.mine() if k == 0 else ref
        if axis == "z":
            return [self.remote(src, ref, n - 1, device(z ^ n, x, y, c)) for n in range(1, 4)]
        to = {"x": device(z, 1 - x, y, c), "y": device(z, x, 1 - y, c), "c": device(z, x, y, 1 - c)}[axis]
        return [self.remote(src, ref, 3 + "xyc".index(axis), to)]

    def arrive(self, k):
        z, x, y, c = spot()
        axis = self.order[k]
        if axis == "z":
            for n in range(1, 4):
                self.landed(self.block(k, z=z ^ n), n - 1).wait_recv()
        else:
            self.landed(self.block(k, **{axis: {"x": 1 - x, "y": 1 - y, "c": 1 - c}[axis]}), 3 + "xyc".index(axis)).wait_recv()

    def stage(self, n):
        if n < 2:
            local = pltpu.make_async_copy(self.mine(), self.block(0), self.recv.at[6])
            local.start() if n == 0 else local.wait()
        if n > 0:
            self.arrive(n - 1)
        if n < 4:
            for copy in self.copies(n):
                copy.start()

    def finish(self):
        for k in range(4):
            for copy in self.copies(k):
                copy.wait_send()


def add_rows(dst, src):
    dst[...] = (dst[...].astype(jnp.float32) + src[...].astype(jnp.float32)).astype(dst.dtype)


def rest_of(order, k):
    return [(a, {"z": 4, "x": 2, "y": 2}[a]) for a in "zxy" if a not in order[: k + 1]]


def recv_shapes(order):
    return [((3,) if order[k] == "z" else ()) + tuple(n for a, n in rest_of(order, k)) for k in range(3)]


class Collect(Unit):
    heavy = (0, 1, 2, 3, 4)

    def __init__(self, parts, out, cut, order, own, rc, r0, r1, r2, send, recv):
        self.parts, self.out, self.cut, self.order, self.send, self.recv = parts, out, cut, order, send, recv
        self.own, self.rc, self.r = own, rc, (r0, r1, r2)

    def block(self, k, **given):
        z, x, y, c = spot()
        here = {"z": z, "x": x, "y": y}
        lead = tuple(given[a] if a in given else (here[a] if a in self.order[:k] else EVERY) for a in "zxy")
        if self.own is None:
            return self.parts.at[lead + (c,) + self.cut]
        return self.own.at[lead]

    def core(self):
        z, x, y, c = spot()
        return self.remote(self.parts.at[(EVERY, EVERY, EVERY, 1 - c) + self.cut], self.rc, 0, device(z, x, y, 1 - c))

    def load(self):
        z, x, y, c = spot()
        return pltpu.make_async_copy(self.parts.at[(EVERY, EVERY, EVERY, c) + self.cut], self.own, self.recv.at[7])

    def copies(self, k):
        z, x, y, c = spot()
        axis = self.order[k]
        if axis == "z":
            return [self.remote(self.block(k, z=z ^ n), self.r[k].at[n - 1], 3 + n, device(z ^ n, x, y, c)) for n in range(1, 4)]
        to = {"x": device(z, 1 - x, y, c), "y": device(z, x, 1 - y, c)}[axis]
        return [self.remote(self.block(k, **{axis: {"x": 1 - x, "y": 1 - y}[axis]}), self.r[k], 1 + k, to)]

    def arrive(self, k):
        z, x, y, c = spot()
        axis = self.order[k]
        own = {axis: {"z": z, "x": x, "y": y}[axis]}
        if axis == "z":
            sources = [self.r[k].at[n] for n in range(3)]
            for n in range(3):
                self.landed(sources[n], 4 + n).wait_recv()
        else:
            sources = [self.r[k]]
            self.landed(self.r[k], 1 + k).wait_recv()
        if k == 2:
            total = self.block(k, **own)[...].astype(jnp.float32)
            for source in sources:
                total = total + source[...].astype(jnp.float32)
            out = self.out.at[self.cut] if self.cut else self.out
            out[...] = total.reshape(out.shape)
            return
        rest = rest_of(self.order, k)

        def add(at):
            given = dict(zip([a for a, n in rest], at))
            for source in sources:
                add_rows(self.block(k, **own, **given), source.at[tuple(at)])

        def one(i, unused):
            for n in range(rest[1][1] if len(rest) == 2 else 1):
                add((i, n) if len(rest) == 2 else (i,))
            return unused

        lax.fori_loop(0, rest[0][1], one, 0)

    def stage(self, n):
        if n == 0:
            self.core().start()
            if self.own is not None:
                self.load().start()
            return
        if n == 1:
            self.landed(self.rc, 0).wait_recv()
            if self.own is not None:
                self.load().wait()

            def one(i, unused):
                for k in range(2):
                    for m in range(2):
                        add_rows(self.block(0, z=i, x=k, y=m), self.rc.at[i, k, m])
                return unused

            lax.fori_loop(0, 4, one, 0)
        else:
            self.arrive(n - 2)
        if n < 4:
            for copy in self.copies(n - 1):
                copy.start()

    def finish(self):
        self.core().wait_send()
        for k in range(3):
            for copy in self.copies(k):
                copy.wait_send()


def unit_shape(shape, cut):
    cut = tuple(cut) + (slice(None),) * (len(shape) - len(cut))
    return tuple(len(range(*s.indices(d))) for s, d in zip(cut, shape))


def collect_scratch(plan, shapes, dtype, inside):
    scratch = []
    for i, cut, order in plan:
        m = unit_shape(shapes[i], cut)
        leads = [] if i in inside else [(4, 2, 2)]
        leads += [(4, 2, 2)] + recv_shapes(order)
        scratch += [pltpu.VMEM(lead + m, dtype) for lead in leads]
    return scratch


def collect_units(plan, parts, outs, bufs, inside, send, recv):
    units, bufs = [], list(bufs)
    for n, (i, cut, order) in enumerate(plan):
        own = None if i in inside else bufs.pop(0)
        units.append(Collect(parts[i], outs[i], cut, order, own, bufs.pop(0), bufs.pop(0), bufs.pop(0), bufs.pop(0), send.at[n], recv.at[n]))
    return units


STAGES = 5


def waves(units, width=2, first=2, lag=1):
    rows = [units[:first]] + [units[i : i + width] for i in range(first, len(units), width)] if units else []
    steps = []
    for t in range(len(rows) + lag * (STAGES - 1) if rows else 0):
        steps.append([(unit, n) for n in units[0].heavy for unit in (rows[t - lag * n] if 0 <= t - lag * n < len(rows) else [])])
    return steps


def go(step):
    for unit, n in step:
        unit.stage(n)


def square_sum(refs, tile):
    tile[...] = jnp.zeros_like(tile)
    for ref in refs:
        v = ref[...]
        v = (v * v).reshape(-1, v.shape[-1])
        v = jnp.sum(v.reshape(-1, 8, v.shape[-1]), axis=0)
        for i in range(0, v.shape[-1], 128):
            tile[...] += v[:, i : i + 128]


def total_square(norm, tiles, send, recv):
    z, x, y, c = spot()
    mine = x * 4 + y * 2 + c
    copies = []

    def push(slot, n, to):
        copies.append(pltpu.make_async_remote_copy(
            src_ref=tiles.at[slot], dst_ref=tiles.at[slot], send_sem=send.at[n], recv_sem=recv.at[n], device_id=to, device_id_type=MESH))
        copies[-1].start()

    def pull(slot, n):
        ref = tiles.at[slot]
        pltpu.make_async_remote_copy(
            src_ref=ref, dst_ref=ref, send_sem=send.at[n], recv_sem=recv.at[n], device_id=device(z, x, y, 1 - c), device_id_type=MESH).wait_recv()

    for n in range(1, 8):
        push(mine, n, device(z, x ^ (n >> 2), y ^ ((n >> 1) & 1), c ^ (n & 1)))
    for n in range(1, 8):
        pull(mine ^ n, n)
    total = tiles[0]
    for n in range(1, 8):
        total = total + tiles[n]
    tiles[8 + z] = total
    for n in range(1, 4):
        push(8 + z, 7 + n, device(z ^ n, x, y, c))
    for n in range(1, 4):
        pull(8 + (z ^ n), 7 + n)
    norm[...] = (tiles[8] + tiles[9]) + (tiles[10] + tiles[11])
    for copy in copies:
        copy.wait_send()


FCH = 768
PACK = 4


def norm_of(h, gain, shift):
    center = h - jnp.mean(h, axis=1, keepdims=True)
    r = lax.rsqrt(jnp.mean(center * center, axis=1, keepdims=True) + norm_eps)
    z = center * r
    return z, r, z * gain + shift


def norm_back(g, z, r, gain):
    gz = g * gain
    return r * (gz - jnp.mean(gz, axis=1, keepdims=True) - z * jnp.mean(gz * z, axis=1, keepdims=True))


def gelu_both(v):
    phi = 0.5 + 0.5 * lax.erf(v * (0.5**0.5))
    return v * phi, phi + v * (jnp.exp(-0.5 * v * v) * 0.3989422804014327)


def ffn_kernel(
    ctx_ref, proj_ref, up_ref, down_ref, h1_ref, og_ref, vec_ref, fb_ref,
    out_ref, gtwo_ref, gctx_ref, gvec_ref, gfb_ref, gproj_ref, gup_ref, gdown_ref,
    proj_s, up_s, down_s, proj_p, up_p, down_p, mid_s, gup_s, gffn_s, fin_s, gattn_s, slope_s, z_s, acc_s, g3_s, sem,
):
    f32, low = jnp.float32, jnp.bfloat16
    chunks = fb_ref.shape[1] // FCH
    nt = (((1,), (1,)), ((), ()))
    tn = (((0,), (0,)), ((), ()))

    def ends(k, proj, up, down):
        if k == 0:
            return proj, proj_p
        j = (k - 1) // 2
        if k % 2:
            return up.at[:, j], up_p.at[j]
        return down.at[8 * j : 8 * j + 8], down_p.at[j]

    def fetch(k):
        src, dst = ends(k, proj_ref, up_ref, down_ref)
        return pltpu.make_async_copy(src, dst, sem.at[k])

    def keep(k):
        dst, src = ends(k, gproj_ref, gup_ref, gdown_ref)
        return pltpu.make_async_copy(src, dst, sem.at[k])

    def block(k, n):
        j = (k - 1) // 2
        if k == 0:
            return proj_p.at[n]
        return up_p.at[j, n] if k % 2 else down_p.at[j, n // 4, n % 4]

    def flatten(k, flat):
        fetch(k).wait()

        def two(m, unused):
            pair = [block(k, 2 * m + i)[...].astype(f32) for i in range(2)]
            flat[pl.ds(pl.multiple_of(48 * m, 16), 48), :] = jnp.concatenate(pair, axis=0).astype(low)
            return unused

        lax.fori_loop(0, 16, two, 0, unroll=4)

    def give(k, product):
        for n in range(32):
            block(k, n)[...] = product[24 * n : 24 * n + 24].astype(low)
        keep(k).start()

    for k in range(1 + 2 * chunks):
        fetch(k).start()
    row = lambda n: vec_ref[n : n + 1, :]
    flatten(0, proj_s)
    attn = lax.dot_general(ctx_ref[...], proj_s[...], tn, preferred_element_type=f32)
    z1, r1, n1 = norm_of(h1_ref[...] + (attn + row(3)), row(4), row(5))
    z_s[...] = z1
    acc_s[...] = n1 + row(6)
    fin_s[...] = n1.astype(low)
    for j in range(chunks):
        at = slice(j * FCH, j * FCH + FCH)
        flatten(1 + 2 * j, up_s.at[j])
        pre = jnp.dot(fin_s[...], up_s[j], preferred_element_type=f32) + fb_ref[:, at]
        act, slope = gelu_both(pre)
        slope_s[:, at] = slope
        mid_s[:, at] = act.astype(low)
        flatten(2 + 2 * j, down_s.at[j])
        acc_s[...] += jnp.dot(mid_s[:, at], down_s[j], preferred_element_type=f32)
    z3, r3, out = norm_of(acc_s[...], row(7), row(8))
    out_ref[...] = out.astype(low)
    og = og_ref[...].astype(f32)
    gvec_ref[7:8, :] = jnp.sum(og * z3, axis=0, keepdims=True)
    gvec_ref[8:9, :] = jnp.sum(og, axis=0, keepdims=True)
    g3 = norm_back(og, z3, r3, row(7))
    g3_s[...] = g3
    gffn_s[...] = g3.astype(low)
    gvec_ref[6:7, :] = jnp.sum(gffn_s[...].astype(f32), axis=0, keepdims=True)
    for j in range(chunks):
        at = slice(j * FCH, j * FCH + FCH)
        give(2 + 2 * j, lax.dot_general(mid_s[:, at], gffn_s[...], tn, preferred_element_type=f32))
        gu = (lax.dot_general(gffn_s[...], down_s[j], nt, preferred_element_type=f32) * slope_s[:, at]).astype(low)
        gup_s[:, at] = gu
        gfb_ref[:, at] = jnp.sum(gu.astype(f32), axis=0, keepdims=True)
        g3_s[...] += lax.dot_general(gu, up_s[j], nt, preferred_element_type=f32)
    gn = g3_s[...]
    z1 = z_s[...]
    gvec_ref[4:5, :] = jnp.sum(gn * z1, axis=0, keepdims=True)
    gvec_ref[5:6, :] = jnp.sum(gn, axis=0, keepdims=True)
    g2 = norm_back(gn, z1, r1, row(4))
    gtwo_ref[...] = g2
    gattn_s[...] = g2.astype(low)
    gvec_ref[3:4, :] = jnp.sum(gattn_s[...].astype(f32), axis=0, keepdims=True)
    for j in range(chunks):
        at = slice(j * FCH, j * FCH + FCH)
        give(1 + 2 * j, lax.dot_general(fin_s[...], gup_s[:, at], tn, preferred_element_type=f32))
    gctx_ref[...] = lax.dot_general(proj_s[...], gattn_s[...], nt, preferred_element_type=f32).astype(low)
    give(0, jnp.dot(ctx_ref[...], gattn_s[...], preferred_element_type=f32))
    for k in range(1 + 2 * chunks):
        keep(k).wait()


def ffn_step(context, proj, up, down, hidden_one, output_grad, vectors, ffn_bias):
    rows, width = hidden_one.shape
    hidden = ffn_bias.shape[1]
    low, f32 = jnp.bfloat16, jnp.float32
    vmem = pl.BlockSpec(memory_space=pltpu.VMEM)
    anywhere = pl.BlockSpec(memory_space=pl.ANY)
    shape = jax.ShapeDtypeStruct
    chunks = hidden // FCH
    return pl.pallas_call(
        ffn_kernel,
        in_specs=[vmem, anywhere, anywhere, anywhere, vmem, vmem, vmem, vmem],
        out_specs=[vmem] * 5 + [anywhere] * 3,
        out_shape=[
            shape((rows, width), low), shape((rows, width), f32), shape((width, rows), low),
            shape((9, width), f32), shape((1, hidden), f32), shape(proj.shape, low), shape(up.shape, low), shape(down.shape, low),
        ],
        scratch_shapes=[
            pltpu.VMEM((width, width), low), pltpu.VMEM((chunks, width, FCH), low), pltpu.VMEM((chunks, FCH, width), low),
            pltpu.VMEM((32, 24, width), low), pltpu.VMEM((chunks, 32, 24, FCH), low), pltpu.VMEM((chunks, 8, 4, 24, width), low),
            pltpu.VMEM((rows, hidden), low), pltpu.VMEM((rows, hidden), low),
            pltpu.VMEM((rows, width), low), pltpu.VMEM((rows, width), low), pltpu.VMEM((rows, width), low),
            pltpu.VMEM((rows, hidden), f32), pltpu.VMEM((rows, width), f32), pltpu.VMEM((rows, width), f32), pltpu.VMEM((rows, width), f32),
            pltpu.SemaphoreType.DMA((1 + 2 * chunks,)),
        ],
        compiler_params=pltpu.CompilerParams(vmem_limit_bytes=60 * 2**20),
        cost_estimate=pl.CostEstimate(flops=6 * rows * width * (2 * hidden + width), bytes_accessed=30_000_000, transcendentals=2 * rows * hidden),
    )(context, proj, up, down, hidden_one, output_grad, vectors, ffn_bias)


def prep_kernel(qkv_i, proj_i, up_i, down_i, conv_i, bias, ffn, qkv_o, proj_o, up_o, down_o, conv_o, small_o, qkv, proj, up, down, conv, sem):
    low = jnp.bfloat16
    copies = [
        pltpu.make_async_copy(src, dst, sem.at[n])
        for n, (src, dst) in enumerate(((up_i, up), (down_i, down), (proj_i, proj), (qkv_i, qkv), (conv_i, conv)))
    ]
    for copy in copies:
        copy.start()
    copies[0].wait()
    for j in range(4):
        up_o[j] = up[:, 768 * j : 768 * j + 768].astype(low)
    copies[1].wait()
    for j in range(4):
        down_o[j] = down[24 * j : 24 * j + 24].astype(low)
    copies[2].wait()
    proj_o[...] = proj[...].astype(low)
    copies[3].wait()
    qkv_o[...] = qkv[...].astype(low)
    copies[4].wait()
    rows = conv.shape[1]
    lane = lax.broadcasted_iota(jnp.int32, (rows, 128), 1)
    zero = jnp.zeros((rows, 128 - CGW), jnp.float32)

    def tap(a, unused):
        cols = [None] * 6
        for r in range(16):
            piece = jnp.concatenate([conv[8 * r + a], zero], axis=1)
            lo = CGW * r
            tile, off = lo // 128, lo % 128
            piece = right(piece, off) if off else piece
            cols[tile] = piece if cols[tile] is None else jnp.where(lane >= off, piece, cols[tile])
            if off + CGW > 128:
                cols[tile + 1] = piece
        conv_o[a] = jnp.concatenate(cols, axis=1).astype(low)
        return unused

    lax.fori_loop(0, 8, tap, 0)
    small_o[...] = jnp.zeros_like(small_o)
    n = bias.shape[0]
    small_o[0:n, 0 : bias.shape[1]] = bias[...].astype(low)
    small_o[n : n + 1, 0 : ffn.shape[1]] = ffn[...].astype(low)


def prep_step(qkv, proj, up, down, conv, bias, ffn):
    vmem = pl.BlockSpec(memory_space=pltpu.VMEM)
    anywhere = pl.BlockSpec(memory_space=pl.ANY)
    shapes = [qkv.shape, proj.shape, (PACK, 24, 768), (PACK, 24, 768), (8, conv.shape[1], 768), (16, 128)]
    return pl.pallas_call(
        prep_kernel,
        in_specs=[anywhere] * 5 + [vmem] * 2,
        out_specs=[vmem] * 6,
        out_shape=[jax.ShapeDtypeStruct(s, jnp.bfloat16) for s in shapes],
        scratch_shapes=[pltpu.VMEM(w.shape, jnp.float32) for w in (qkv, proj, up, down, conv)] + [pltpu.SemaphoreType.DMA((5,))],
        compiler_params=pltpu.CompilerParams(vmem_limit_bytes=60 * 2**20),
    )(qkv, proj, up, down, conv, bias, ffn)


def take_rows(win_ref, g, cut):
    return gapped(take_group(win_ref, g), cut)


def halo_copies(edges_ref, win_ref, send, recv):
    z, x, y, c = spot()
    h = y * 2 + c
    n = edges_ref.shape[0]

    def to(other):
        return {"seq": z * 2 + x, "head": other}

    def copy(src, dst, k, other):
        return pltpu.make_async_remote_copy(
            src_ref=src, dst_ref=dst, send_sem=send.at[k], recv_sem=recv.at[k], device_id=to(other), device_id_type=MESH)

    after = copy(edges_ref.at[n - HALF : n], win_ref.at[0:HALF], 0, h + 1)
    before = copy(edges_ref.at[0:HALF], win_ref.at[n + HALF : n + 2 * HALF], 1, h - 1)
    from_before = copy(win_ref.at[0:HALF], win_ref.at[0:HALF], 0, h ^ 1)
    from_after = copy(win_ref.at[n + HALF : n + 2 * HALF], win_ref.at[n + HALF : n + 2 * HALF], 1, h ^ 1)
    return (h < 3, after), (h > 0, before), (h > 0, from_before), (h < 3, from_after)


def halo_start(edges_ref, win_ref, send, recv):
    for ok, copy in halo_copies(edges_ref, win_ref, send, recv)[:2]:
        pl.when(ok)(copy.start)


def halo_end(edges_ref, win_ref, send, recv):
    n = edges_ref.shape[0]
    after, before, from_before, from_after = halo_copies(edges_ref, win_ref, send, recv)
    for (ok, copy), rows in ((from_before, slice(0, HALF)), (from_after, slice(n + HALF, n + 2 * HALF))):
        pl.when(ok)(copy.wait_recv)

        @pl.when(jnp.logical_not(ok))
        def _(rows=rows):
            win_ref[rows, :] = jnp.zeros((HALF, win_ref.shape[1]), win_ref.dtype)

    for ok, copy in (after, before):
        pl.when(ok)(copy.wait_send)


def unpack_small(small_s, vec_ref, fb_ref):
    lane = lax.broadcasted_iota(jnp.int32, (16, 128), 1)
    vec, fb = [None] * 6, [None] * 24
    for n in range(32):
        piece = small_s[n // 8, (n // 4) % 2, (n // 2) % 2, n % 2].astype(jnp.float32)
        for out, width in ((vec, 24), (fb, 96)):
            tile, off = width * n // 128, width * n % 128
            turned = right(piece, off) if off else piece
            out[tile] = turned if out[tile] is None else jnp.where(lane >= off, turned, out[tile])
            if off + width > 128:
                out[tile + 1] = turned
    for i, v in enumerate(vec):
        vec_ref[:, 128 * i : 128 * i + 128] = v
    for i, v in enumerate(fb):
        fb_ref[:, 128 * i : 128 * i + 128] = v[9:10]


def open_kernel(plan, n_in, early, *refs):
    cut_ref, frames_ref = refs[:2]
    owns = refs[2 : 2 + n_in]
    hidden_ref, slope_ref, low_ref, vec_ref, fb_ref, cols_ref = refs[2 + n_in : 8 + n_in]
    wholes = refs[8 + n_in : 8 + 2 * n_in]
    out_ref, win_ref, cols_s, low_s, w_s, wp_s, small_s, send, recv, hsend, hrecv, wsem, csem = refs[8 + 2 * n_in :]
    cut = cut_ref[0]
    greet(halo=True)
    halo_start(frames_ref, win_ref, hsend, hrecv)
    units = [Spread(owns[i], wholes[i], where, order, send.at[n], recv.at[n]) for n, (i, where, order) in enumerate(plan)]
    steps = waves(units, first=3)
    go(steps[0])
    win_ref[HALF : HALF + OWN, :] = frames_ref[...]
    out_ref[...] = jnp.zeros_like(out_ref)
    wp_s[...] = jnp.zeros_like(wp_s)
    go(steps[1])
    halo_end(frames_ref, win_ref, hsend, hrecv)

    def columns(g, unused):
        cols_s[g] = im2col(take_rows(win_ref, g, cut), ZROWS)
        return unused

    def load(half, z):
        return pltpu.make_async_copy(wholes[0].at[z, :, :, :, 4 * half : 4 * half + 4], w_s.at[z], wsem.at[z])

    def product(g):
        z, x, y = g // 4, (g // 2) % 2, g % 2
        for h in range(2):
            for a in range(4):
                wp_s[h * 128 + a * 32 : h * 128 + a * 32 + 24, :] = w_s[z, x, y, h, a]
        return lax.dot_general(cols_s[g], wp_s[...], (((1,), (1,)), ((), ())), preferred_element_type=jnp.float32)

    def low(g, unused):
        low_s[g] = product(g)
        return unused

    def high(g, unused):
        z = jnp.concatenate([low_s[g], product(g)], axis=1)
        z = jnp.concatenate([z[:, 0:128], z[:, 256:384], z[:, 128:256], z[:, 384:512]], axis=1)
        put_group(out_ref, g, pick_own(fold_out(z), cut))
        return unused

    def keep(chunk):
        span = pl.ds(4 * chunk, 4)
        return pltpu.make_async_copy(cols_s.at[span], cols_ref.at[span], csem.at[chunk])

    t = 2
    for chunk in range(4):
        lax.fori_loop(4 * chunk, 4 * chunk + 4, columns, 0)
        keep(chunk).start()
        go(steps[t])
        t += 1
    def finish():
        copy = pltpu.make_async_copy(wholes[-1], small_s, wsem.at[0])
        copy.start()
        copy.wait()
        unpack_small(small_s, vec_ref, fb_ref)
        act, slope = gelu_both(out_ref[...] + vec_ref[0:1, :])
        hidden = frames_ref[...].astype(jnp.float32) + act
        hidden_ref[...] = hidden
        low_ref[...] = hidden.astype(jnp.bfloat16)
        slope_ref[...] = slope

    done = 0
    while t < len(steps) or done < 3:
        if done == 2:
            finish()
            done += 1
        elif done < 2 and t - STAGES >= early[done]:
            for z in range(4):
                load(done, z).start()
            for z in range(4):
                load(done, z).wait()
                lax.fori_loop(4 * z, 4 * z + 4, (low, high)[done], 0)
                if t < len(steps) and z % 2 == 1:
                    go(steps[t])
                    t += 1
            done += 1
        elif t < len(steps):
            go(steps[t])
            t += 1
    for unit in units:
        unit.finish()
    for chunk in range(4):
        keep(chunk).wait()


def open_step(cut, frames, shards, plan, early, collective_id=1):
    n = len(shards)
    vmem = pl.BlockSpec(memory_space=pltpu.VMEM)
    anywhere = pl.BlockSpec(memory_space=pl.ANY)
    return pl.pallas_call(
        functools.partial(open_kernel, plan, n, early),
        in_specs=[pl.BlockSpec(memory_space=pltpu.SMEM), vmem] + [anywhere] * n,
        out_specs=[vmem] * 5 + [anywhere] + [anywhere] * n,
        out_shape=[
            jax.ShapeDtypeStruct((OWN, 768), jnp.float32),
            jax.ShapeDtypeStruct((OWN, 768), jnp.float32),
            jax.ShapeDtypeStruct((OWN, 768), jnp.bfloat16),
            jax.ShapeDtypeStruct((16, 768), jnp.float32),
            jax.ShapeDtypeStruct((1, 3072), jnp.float32),
            jax.ShapeDtypeStruct((16, ZROWS, 768), jnp.bfloat16),
        ]
        + [jax.ShapeDtypeStruct((4, 2, 2, 2) + s.shape, s.dtype) for s in shards],
        scratch_shapes=[
            pltpu.VMEM((OWN, 768), jnp.float32),
            pltpu.VMEM((WIN, 768), jnp.bfloat16),
            pltpu.VMEM((16, ZROWS, 768), jnp.bfloat16),
            pltpu.VMEM((16, ZROWS, 256), jnp.float32),
            pltpu.VMEM((4, 2, 2, 2, 4, 24, 768), jnp.bfloat16),
            pltpu.VMEM((256, 768), jnp.bfloat16),
            pltpu.VMEM((4, 2, 2, 2, 16, 128), jnp.bfloat16),
            pltpu.SemaphoreType.DMA((len(plan), 9)),
            pltpu.SemaphoreType.DMA((len(plan), 10)),
            pltpu.SemaphoreType.DMA((2,)),
            pltpu.SemaphoreType.DMA((2,)),
            pltpu.SemaphoreType.DMA((4,)),
            pltpu.SemaphoreType.DMA((4,)),
        ],
        compiler_params=pltpu.CompilerParams(collective_id=collective_id, has_side_effects=True, vmem_limit_bytes=56 * 2**20),
    )(cut, frames, *shards)


HEADS_HERE = 3
ROWS_HERE = 192 * HEADS_HERE


def group_copy(src, dst, send, recv, other):
    return pltpu.make_async_remote_copy(
        src_ref=src, dst_ref=dst, send_sem=send, recv_sem=recv, device_id={"head": other}, device_id_type=MESH
    )


def spaced(steps, slots):
    out = [[] for _ in range(slots)]
    for t, step in enumerate(steps):
        out[min(t * slots // max(len(steps), 1), slots - 1)].append(step)
    return out


def go_at(slot, by_slot):
    for t, steps in enumerate(by_slot):
        if steps:

            @pl.when(slot == t)
            def _(steps=steps):
                for step in steps:
                    go(step)


def fill_heads(seg_ref, qkv_ref, h, k_s, q_s):
    n = seg_ref.shape[1]
    seg = seg_ref[...]
    row = lax.broadcasted_iota(jnp.int32, (64, n), 0)
    mark = jnp.where(row < 2, jnp.where(seg == row, 1.0, 0.0), 0.0)
    push = jnp.where(row < 2, jnp.where(seg == row, 0.0, FAR), 0.0)
    at = pl.multiple_of(h * 192, 64)
    keys = qkv_ref[pl.ds(at + 64, 64), :].astype(jnp.float32)
    k_s[...] = jnp.transpose(jnp.concatenate([keys, mark], axis=0)).astype(jnp.bfloat16)
    queries = qkv_ref[pl.ds(at, 64), :].astype(jnp.float32) * 0.125
    q_s[...] = jnp.concatenate([queries, push], axis=0).astype(jnp.bfloat16)


def attend_kernel(plan, n_in, *refs):
    seg_ref, packed_ref = refs[:2]
    owns = refs[2 : 2 + n_in]
    qkv_ref, ctx_ref, lse_ref, o_ref = refs[2 + n_in : 6 + n_in]
    wholes = refs[6 + n_in : 6 + 2 * n_in]
    k_s, q_s, ctx_s, asend, arecv, csend, crecv, osem, send, recv = refs[6 + 2 * n_in :]
    z, x, y, c = spot()
    me = y * 2 + c
    size = packed_ref.shape[1]
    greet(group=True)

    def bring(h, d):
        return group_copy(
            packed_ref.at[pl.ds((me ^ d) * ROWS_HERE + h * 192, 192)],
            qkv_ref.at[pl.ds(h * 192, 192), d * size : d * size + size],
            asend.at[h, d - 1], arecv.at[h, d - 1], me ^ d,
        )

    def give(h, d):
        return group_copy(
            ctx_s.at[pl.ds(h * 64, 64), d * size : d * size + size],
            ctx_ref.at[pl.ds(me * 64 * HEADS_HERE + h * 64, 64)],
            csend.at[h, d - 1], crecv.at[h, d - 1], me ^ d,
        )

    def given(h, d):
        ref = ctx_ref.at[pl.ds((me ^ d) * 64 * HEADS_HERE + h * 64, 64)]
        return group_copy(ref, ref, csend.at[h, d - 1], crecv.at[h, d - 1], me ^ d)

    own = pltpu.make_async_copy(packed_ref.at[pl.ds(me * ROWS_HERE, ROWS_HERE)], qkv_ref.at[:, 0:size], osem)
    own.start()
    for d in (2, 3, 1):
        bring(0, d).start()
    units = [Spread(owns[i], wholes[i], where, order, send.at[n], recv.at[n]) for n, (i, where, order) in enumerate(plan)]
    steps = waves(units)
    go(steps[0] if steps else [])
    tiles = 4 * size // QF
    by_slot = spaced(steps[1:], HEADS_HERE * tiles)
    own.wait()

    def head(h, unused):
        for d in (1, 2, 3):
            bring(h, d).wait_recv()

        @pl.when(h < HEADS_HERE - 1)
        def _():
            for d in (2, 3, 1):
                bring(jnp.minimum(h + 1, HEADS_HERE - 1), d).start()

        fill_heads(seg_ref, qkv_ref, h, k_s, q_s)

        def tile(i, unused):
            at = pl.ds(pl.multiple_of(i * QF, QF), QF)
            s = jnp.dot(k_s[...], q_s[:, at], preferred_element_type=jnp.float32)
            peak = jnp.max(fold_rows(s, jnp.maximum), axis=0, keepdims=True)
            e = jnp.exp(s - peak)
            denom = jnp.sum(fold_rows(e, jnp.add), axis=0, keepdims=True)
            values = qkv_ref[pl.ds(pl.multiple_of(h * 192 + 128, 64), 64), :]
            o = jnp.dot(values, e.astype(jnp.bfloat16), preferred_element_type=jnp.float32) * (1.0 / denom)
            rows = pl.ds(pl.multiple_of(h * 64, 64), 64)
            o_ref[rows, at] = o
            ctx_s[rows, at] = o.astype(jnp.bfloat16)
            lse_ref[h, :, at] = peak + jnp.log(denom)
            go_at(h * tiles + i, by_slot)
            return unused

        lax.fori_loop(0, tiles, tile, 0, unroll=True)
        for d in (2, 3, 1):
            give(h, d).start()
        ctx_ref[pl.ds(pl.multiple_of(me * 64 * HEADS_HERE + h * 64, 64), 64), :] = ctx_s[pl.ds(pl.multiple_of(h * 64, 64), 64), 0:size]
        return unused

    lax.fori_loop(0, HEADS_HERE, head, 0)
    for h in range(HEADS_HERE):
        for d in (1, 2, 3):
            given(h, d).wait_recv()
            give(h, d).wait_send()
            bring(h, d).wait_send()
    for unit in units:
        unit.finish()


def attend(seg, packed, shards, plan, collective_id=3):
    n = len(shards)
    size = packed.shape[1]
    vmem = pl.BlockSpec(memory_space=pltpu.VMEM)
    anywhere = pl.BlockSpec(memory_space=pl.ANY)
    sem = pltpu.SemaphoreType.DMA
    return pl.pallas_call(
        functools.partial(attend_kernel, plan, n),
        in_specs=[vmem, anywhere] + [anywhere] * n,
        out_specs=[vmem] * 4 + [anywhere] * n,
        out_shape=[
            jax.ShapeDtypeStruct((ROWS_HERE, 4 * size), jnp.bfloat16),
            jax.ShapeDtypeStruct((768, size), jnp.bfloat16),
            jax.ShapeDtypeStruct((HEADS_HERE, 1, 4 * size), jnp.float32),
            jax.ShapeDtypeStruct((64 * HEADS_HERE, 4 * size), jnp.float32),
        ]
        + [jax.ShapeDtypeStruct((4, 2, 2, 2) + s.shape, s.dtype) for s in shards],
        scratch_shapes=[
            pltpu.VMEM((4 * size, 128), jnp.bfloat16),
            pltpu.VMEM((128, 4 * size), jnp.bfloat16),
            pltpu.VMEM((64 * HEADS_HERE, 4 * size), jnp.bfloat16),
            sem((3, 3)), sem((3, 3)), sem((3, 3)), sem((3, 3)), sem,
            sem((max(len(plan), 1), 9)), sem((max(len(plan), 1), 10)),
        ],
        compiler_params=pltpu.CompilerParams(collective_id=collective_id, has_side_effects=True, vmem_limit_bytes=50 * 2**20),
    )(seg, packed, *shards)


def attend_back_kernel(plan, n_in, *refs):
    seg_ref, qkv_ref, lse_ref, o_ref, gc_ref = refs[:5]
    parts = refs[5 : 5 + n_in]
    gp_ref, norm_ref = refs[5 + n_in : 7 + n_in]
    outs = refs[7 + n_in : 7 + 2 * n_in]
    k_s, q_s, v_s, do_s, dk_s, dv_s, dq_s, gp_s, asend, arecv, csend, crecv, osem, send, recv = refs[7 + 2 * n_in : 22 + 2 * n_in]
    bufs = refs[22 + 2 * n_in :]
    z, x, y, c = spot()
    me = y * 2 + c
    size = gc_ref.shape[1]
    greet(group=True)

    def bring(h, d):
        return group_copy(
            gc_ref.at[pl.ds((me ^ d) * 64 * HEADS_HERE + h * 64, 64)],
            do_s.at[pl.ds(h * 64, 64), d * size : d * size + size],
            asend.at[h, d - 1], arecv.at[h, d - 1], me ^ d,
        )

    def give(h, d):
        return group_copy(
            gp_s.at[pl.ds(h * 192, 192), d * size : d * size + size],
            gp_ref.at[pl.ds(me * ROWS_HERE + h * 192, 192)],
            csend.at[h, d - 1], crecv.at[h, d - 1], me ^ d,
        )

    def given(h, d):
        ref = gp_ref.at[pl.ds((me ^ d) * ROWS_HERE + h * 192, 192)]
        return group_copy(ref, ref, csend.at[h, d - 1], crecv.at[h, d - 1], me ^ d)

    own = pltpu.make_async_copy(gc_ref.at[pl.ds(me * 64 * HEADS_HERE, 64 * HEADS_HERE)], do_s.at[:, 0:size], osem)
    own.start()
    for h in range(HEADS_HERE):
        for d in (2, 3, 1):
            bring(h, d).start()
    units = collect_units(plan, parts, outs, bufs, (), send, recv)
    steps = waves(units)
    go(steps[0] if steps else [])
    tiles = 4 * size // QT
    by_slot = spaced(steps[1:], HEADS_HERE * tiles)
    own.wait()

    def head(h, unused):
        for d in (1, 2, 3):
            bring(h, d).wait_recv()
        fill_heads(seg_ref, qkv_ref, h, k_s, q_s)
        first = pl.multiple_of(h * 192, 64)
        v_s[...] = jnp.transpose(qkv_ref[pl.ds(first + 128, 64), :].astype(jnp.float32)).astype(jnp.bfloat16)
        dk_s[...] = jnp.zeros_like(dk_s)
        dv_s[...] = jnp.zeros_like(dv_s)
        rows = pl.ds(pl.multiple_of(h * 64, 64), 64)

        def tile(i, unused):
            at = pl.ds(pl.multiple_of(i * QT, QT), QT)
            q = q_s[:, at]
            do = do_s[rows, at]
            delta = jnp.sum(do.astype(jnp.float32) * o_ref[rows, at], axis=0, keepdims=True)
            s = jnp.dot(k_s[...], q, preferred_element_type=jnp.float32)
            p = jnp.exp(s - lse_ref[h, :, at])
            dp = jnp.dot(v_s[...], do, preferred_element_type=jnp.float32)
            ds = (p * (dp - delta)).astype(jnp.bfloat16)
            p = p.astype(jnp.bfloat16)
            nt = (((1,), (1,)), ((), ()))
            dv_s[...] += lax.dot_general(do, p, nt, preferred_element_type=jnp.float32)
            dk_s[...] += lax.dot_general(q[:64], ds, nt, preferred_element_type=jnp.float32)
            dq_s[:, at] = jnp.dot(qkv_ref[pl.ds(first + 64, 64), :], ds, preferred_element_type=jnp.float32) * 0.125
            go_at(h * tiles + i, by_slot)
            return unused

        lax.fori_loop(0, tiles, tile, 0)
        gp_s[pl.ds(first, 64), :] = dq_s[...].astype(jnp.bfloat16)
        gp_s[pl.ds(first + 64, 64), :] = dk_s[...].astype(jnp.bfloat16)
        gp_s[pl.ds(first + 128, 64), :] = dv_s[...].astype(jnp.bfloat16)
        for d in (2, 3, 1):
            give(h, d).start()
        gp_ref[pl.ds(pl.multiple_of(me * ROWS_HERE + h * 192, 64), 192), :] = gp_s[pl.ds(first, 192), 0:size]
        return unused

    lax.fori_loop(0, HEADS_HERE, head, 0)
    for h in range(HEADS_HERE):
        for d in (1, 2, 3):
            given(h, d).wait_recv()
            give(h, d).wait_send()
            bring(h, d).wait_send()
    for unit in units:
        unit.finish()
    square_sum(outs, norm_ref)


def attend_back(seg, qkv, lse, o, gc, parts, plan, collective_id=4):
    n = len(parts)
    size = gc.shape[1]
    shapes = [p.shape[4:] for p in parts]
    vmem = pl.BlockSpec(memory_space=pltpu.VMEM)
    anywhere = pl.BlockSpec(memory_space=pl.ANY)
    sem = pltpu.SemaphoreType.DMA
    return pl.pallas_call(
        functools.partial(attend_back_kernel, plan, n),
        in_specs=[vmem] * 4 + [anywhere] + [anywhere] * n,
        out_specs=[vmem] * 2 + [vmem] * n,
        out_shape=[jax.ShapeDtypeStruct((4 * ROWS_HERE, size), jnp.bfloat16), jax.ShapeDtypeStruct((8, 128), jnp.float32)]
        + [jax.ShapeDtypeStruct(s, jnp.float32) for s in shapes],
        scratch_shapes=[
            pltpu.VMEM((4 * size, 128), jnp.bfloat16),
            pltpu.VMEM((128, 4 * size), jnp.bfloat16),
            pltpu.VMEM((4 * size, 64), jnp.bfloat16),
            pltpu.VMEM((64 * HEADS_HERE, 4 * size), jnp.bfloat16),
            pltpu.VMEM((64, 4 * size), jnp.float32),
            pltpu.VMEM((64, 4 * size), jnp.float32),
            pltpu.VMEM((64, 4 * size), jnp.float32),
            pltpu.VMEM((ROWS_HERE, 4 * size), jnp.bfloat16),
            sem((3, 3)), sem((3, 3)), sem((3, 3)), sem((3, 3)), sem,
            sem((max(len(plan), 1), 9)), sem((max(len(plan), 1), 10)),
        ]
        + collect_scratch(plan, shapes, jnp.bfloat16, ()),
        compiler_params=pltpu.CompilerParams(collective_id=collective_id, has_side_effects=True, vmem_limit_bytes=58 * 2**20),
    )(seg, qkv, lse, o, gc, *parts)


SIDE_SLOTS = 16


def close_kernel(side_plan, main_plan, n_in, *refs):
    cut_ref, cols_ref, grad_ref, conv_ref = refs[:4]
    parts = refs[4 : 4 + n_in]
    dx_ref, norm_ref, conv_out = refs[4 + n_in : 7 + n_in]
    outs = refs[7 + n_in : 7 + 2 * n_in]
    (gwin_s, taps_s, cols_s, dw_s, w_s, wp_s, send, recv, msend, mrecv, hsend, hrecv, wsem, csem) = refs[7 + 2 * n_in : 21 + 2 * n_in]
    bufs = refs[21 + 2 * n_in :]
    cut, last = cut_ref[0], cut_ref[1]
    greet(plane=True)
    halo_start(grad_ref, gwin_s, hsend, hrecv)
    count = len(collect_scratch(side_plan, [o.shape for o in outs], jnp.bfloat16, ()))
    side = collect_units(side_plan, parts, outs, bufs[:count], (), send, recv)
    main = collect_units(main_plan, [dw_s], [conv_out], bufs[count:], (0,), msend, mrecv)
    side_steps, main_steps = waves(side), waves(main)
    go(side_steps[0])
    gwin_s[HALF : HALF + OWN, :] = grad_ref[...]
    dx_ref[...] = jnp.zeros_like(dx_ref)
    wp_s[...] = jnp.zeros_like(wp_s)
    halo_end(grad_ref, gwin_s, hsend, hrecv)

    def load(z):
        return pltpu.make_async_copy(conv_ref.at[z], w_s.at[z % 2], wsem.at[z % 2])

    load(0).start()
    load(1).start()
    begin = jnp.where(cut <= HALF, 2 * HALF, HALF)
    end = jnp.where(last > 0, EXT, jnp.where(cut <= HALF + OWN, OWN + 2 * HALF, OWN + HALF))

    def pick(k):
        return pltpu.make_async_copy(cols_ref.at[pl.ds(2 * k, 2)], cols_s.at[k % 2], csem.at[k % 2])

    pick(0).start()
    row = lax.broadcasted_iota(jnp.int32, (ZROWS, 256), 0) + HALF
    owned = (row >= begin) & (row < end)
    by_slot = spaced(side_steps[1:], SIDE_SLOTS)

    def product(k, m, taps, half):
        own = jnp.concatenate([taps[HALF : HALF + ZROWS, h * 256 + half * 128 : h * 256 + half * 128 + 128] for h in range(2)], axis=1)
        own = jnp.where(owned, own.astype(jnp.float32), 0.0).astype(jnp.bfloat16)
        dw = lax.dot_general(own, cols_s[k % 2, m], (((0,), (0,)), ((), ())), preferred_element_type=jnp.float32).astype(jnp.bfloat16)
        for h in range(2):
            for a in range(4):
                dw_s[k // 2, k % 2, m, h, 4 * half + a] = dw[h * 128 + a * 32 : h * 128 + a * 32 + 24]

    def weights_low(k, unused):
        pick((k + 1) % 8).start()
        pick(k).wait()
        taps = [taps_of(take_rows(gwin_s, 2 * k + m, cut)) for m in range(2)]
        for m in range(2):
            taps_s[2 * k + m] = taps[m]
            product(k, m, taps[m], 0)
        go_at(k, by_slot)
        return unused

    lax.fori_loop(0, 8, weights_low, 0)
    soon = max(len(main) // 4, 1)
    early = spaced(main_steps[:soon], 8)

    def weights_high(k, unused):
        go_at(k + 8, by_slot)
        go_at(k, early)
        pl.when(k < 7)(lambda: pick(k + 1).start())
        pick(k).wait()
        for m in range(2):
            product(k, m, taps_s[2 * k + m], 1)
        return unused

    lax.fori_loop(0, 8, weights_high, 0)
    more = spaced(main_steps[soon:], 8)

    def inputs(k, unused):
        go_at(k, more)
        pl.when(k % 2 == 0)(lambda: load(k // 2).wait())
        for m in range(2):
            for h in range(2):
                for a in range(8):
                    wp_s[m, h * 256 + a * 32 : h * 256 + a * 32 + 24, :] = w_s[(k // 2) % 2, k % 2, m, h, a]
        outs = [jnp.dot(taps_s[2 * k + m], wp_s[m], preferred_element_type=jnp.float32) for m in range(2)]
        for m in range(2):
            put_group(dx_ref, 2 * k + m, pick_own(fold_back(outs[m]), cut))
        pl.when((k % 2 == 1) & (k < 4))(lambda: load(k // 2 + 2).start())
        return unused

    lax.fori_loop(0, 8, inputs, 0)
    for unit in side + main:
        unit.finish()
    square_sum([conv_out] + list(outs), norm_ref)


def close_step(cut, columns, grad, conv, parts, side_plan, main_plan, collective_id=2):
    n = len(parts)
    shapes = [p.shape[4:] for p in parts]
    vmem = pl.BlockSpec(memory_space=pltpu.VMEM)
    anywhere = pl.BlockSpec(memory_space=pl.ANY)
    sem = pltpu.SemaphoreType.DMA
    low = jnp.bfloat16
    return pl.pallas_call(
        functools.partial(close_kernel, side_plan, main_plan, n),
        in_specs=[pl.BlockSpec(memory_space=pltpu.SMEM), anywhere, vmem, anywhere] + [anywhere] * n,
        out_specs=[vmem] * (3 + n),
        out_shape=[
            jax.ShapeDtypeStruct((OWN, 768), jnp.float32),
            jax.ShapeDtypeStruct((8, 128), jnp.float32),
            jax.ShapeDtypeStruct(conv.shape[4:], jnp.float32),
        ]
        + [jax.ShapeDtypeStruct(s, jnp.float32) for s in shapes],
        scratch_shapes=[
            pltpu.VMEM((WIN, 768), low),
            pltpu.VMEM((16, EXT, 512), low),
            pltpu.VMEM((2, 2, ZROWS, 768), low),
            pltpu.VMEM(conv.shape, low),
            pltpu.VMEM((2,) + conv.shape[1:], low),
            pltpu.VMEM((2, 512, 768), low),
            sem((len(side_plan), 9)), sem((len(side_plan), 10)), sem((len(main_plan), 9)), sem((len(main_plan), 10)),
            sem((2,)), sem((2,)), sem((2,)), sem((2,)),
        ]
        + collect_scratch(side_plan, shapes, low, ())
        + collect_scratch(main_plan, [conv.shape[4:]], low, (0,)),
        compiler_params=pltpu.CompilerParams(collective_id=collective_id, has_side_effects=True, vmem_limit_bytes=60 * 2**20),
    )(cut, columns, grad, conv, *parts)


def norm_kernel(n_in, *refs):
    ins, norm_ref, tiles, send, recv = refs[:n_in], refs[n_in], refs[n_in + 1], refs[n_in + 2], refs[n_in + 3]
    greet(plane=True)
    z, x, y, c = spot()
    mine = tiles.at[x * 4 + y * 2 + c]
    square_sum(ins[1:], mine)
    mine[...] += ins[0][...]
    total_square(norm_ref, tiles, send, recv)


def norm_step(tile, sums, collective_id=5):
    n = 1 + len(sums)
    vmem = pl.BlockSpec(memory_space=pltpu.VMEM)
    return pl.pallas_call(
        functools.partial(norm_kernel, n),
        in_specs=[vmem] * n,
        out_specs=vmem,
        out_shape=jax.ShapeDtypeStruct((8, 128), jnp.float32),
        scratch_shapes=[pltpu.VMEM((12, 8, 128), jnp.float32), pltpu.SemaphoreType.DMA((11,)), pltpu.SemaphoreType.DMA((11,))],
        compiler_params=pltpu.CompilerParams(collective_id=collective_id, has_side_effects=True, vmem_limit_bytes=32 * 2**20),
    )(tile, *sums)


S = slice


def sliced(index, axis, size, count, orders, first=0):
    step = size // count
    return [
        (index, (S(None),) * axis + (S(step * i, step * i + step),), orders[(first + i) % len(orders)]) for i in range(count)
    ]


def open_plan():
    even = ("zxy", "zyx")
    plan = sliced(0, 0, 8, 8, even)
    return plan[:1] + [(3, (), "zxy")] + plan[1:] + sliced(1, 1, 2304, 2, even) + [(2, (), "zyx")]


def attend_back_plan():
    plan = []
    for a in range(4):
        plan += [(1, (S(a, a + 1), S(None), S(384 * i, 384 * i + 384)), ("xyz", "yxz")[i]) for i in range(2)]
    return plan + [(0, (), "xyz")]


def side_plan():
    return sliced(0, 1, 2304, 6, ("xyz", "yxz")) + [(1, (), "xyz")]


def main_plan():
    plan = []
    for a in range(8):
        plan += [(0, (S(a, a + 1), S(None), S(384 * i, 384 * i + 384)), ("xyz", "yxz")[i]) for i in range(2)]
    return plan


def by_chips():
    return lax.axis_size("seq") == 8 and lax.axis_size("head") == 4


def gather_weights(parts):
    return [lax.all_gather(p, ("seq", "head"), axis=0) for p in parts]


def collect_grads(parts):
    outs = [lax.psum_scatter(p.astype(jnp.float32), ("seq", "head"), scatter_dimension=0, tiled=False) for p in parts]
    square = jnp.zeros((), jnp.float32)
    for out in outs:
        square = square + jnp.sum(out * out)
    return outs, lax.psum(square, ("seq", "head"))


def by_owner(part):
    return part.reshape((4, 2, 2, 2) + part.shape[1:])


def as_small(rows, ffn):
    n, count, width = rows.shape
    rows = jnp.pad(rows, ((0, 0), (0, 16 - count), (0, 128 - width)))
    return rows + jnp.pad(ffn[:, None], ((0, 0), (count, 15 - count), (0, 128 - ffn.shape[1])))


def trade(pieces):
    count = lax.axis_size("head")
    return [pieces[0]] + [lax.ppermute(pieces[d], "head", [(i, i ^ d) for i in range(count)]) for d in range(1, count)]


def by_partner(stacked):
    me = lax.axis_index("head")
    return [lax.dynamic_index_in_dim(stacked, me ^ d, 0, keepdims=False) for d in range(stacked.shape[0])]


def from_partner(pieces):
    me = lax.axis_index("head")
    stacked = jnp.stack(pieces)
    return jnp.concatenate([lax.dynamic_index_in_dim(stacked, me ^ j, 0, keepdims=False) for j in range(len(pieces))], axis=0)


def shards(
    frames, output_grad, segment_ids, qkv_weight, proj_weight, up_weight, down_weight, conv_weight, bias_gains, ffn_bias,
    qkv_first, proj_first, up_first, down_first, conv_first, bias_gains_first, ffn_bias_first,
    qkv_second, proj_second, up_second, down_second, conv_second, bias_gains_second, ffn_bias_second,
):
    low_type = jnp.bfloat16
    f32 = jnp.float32
    count = lax.axis_size("seq") * lax.axis_size("head")
    row_count, model_width = frames.shape
    head_groups = lax.axis_size("head")
    head_index = lax.axis_index("head")
    kernel_len, conv_rows, group_width = conv_weight.shape
    vec_rows, vec_cols = bias_gains.shape
    ffn_cols = ffn_bias.shape[0]
    if by_chips():
        qkv_low, proj_low, up_low, down_low, conv_low, small = prep_step(
            qkv_weight, proj_weight, up_weight, down_weight, conv_weight, bias_gains, ffn_bias[None]
        )
    else:
        qkv_low, proj_low, up_low, down_low = [w.astype(low_type) for w in (qkv_weight, proj_weight, up_weight, down_weight)]
        conv_low = conv_weight.astype(low_type).reshape(16, 8, conv_rows, group_width).transpose(1, 2, 0, 3).reshape(8, conv_rows, 768)
        small = as_small(bias_gains.astype(low_type)[None], ffn_bias.astype(low_type)[None])[0]
    seg_group = segment_ids[0]
    half_kernel = kernel_len // 2
    boundary = jnp.sum((seg_group == 0).astype(jnp.int32))
    cut = jnp.clip(boundary - head_index * row_count + half_kernel, 0, row_count + kernel_len)
    cut = jnp.stack([cut, (head_index == head_groups - 1).astype(jnp.int32)]).astype(jnp.int32)
    if by_chips():
        hidden_one, conv_slope, attn_in, vectors, full_ffn, conv_columns, *parts = open_step(
            cut, frames, [conv_low, qkv_low, proj_low, small], open_plan(), (1, 3)
        )
        all_conv, all_qkv, all_proj = [w.reshape((32,) + w.shape[4:]) for w in parts[:3]]
        whole_conv = parts[0]
        all_up, all_down = gather_weights([up_low, down_low])
    else:
        all_conv, all_qkv, all_proj, all_up, all_down, all_small = gather_weights([conv_low, qkv_low, proj_low, up_low, down_low, small])
        all_up = all_up.reshape(32, 24, 4, model_width).transpose(0, 2, 1, 3)
        all_down = all_down.reshape(32, 4, 24, model_width)
        all_proj = all_proj.reshape(32, 24, model_width)
    full_qkv = all_qkv.reshape(model_width, -1)
    full_conv = all_conv.reshape(16, 2, 24 // conv_rows, 8, conv_rows, 768).transpose(0, 1, 3, 2, 4, 5).reshape(16, 2, 8, 24, 768)
    if not by_chips():
        vectors = all_small[:, :vec_rows, :vec_cols].astype(f32).transpose(1, 0, 2).reshape(vec_rows, model_width)
        full_ffn = all_small[:, vec_rows, :ffn_cols].astype(f32).reshape(1, -1)
    seg_rows = jnp.concatenate(by_partner(seg_group.reshape(head_groups, 1, row_count)), axis=1)

    if not by_chips():
        window = with_halo(frames, (("head", 0),), half_kernel)
        conv_act, conv_slope = gelu_both(conv_fwd(cut, window, full_conv) + vectors[0])
        hidden_one = frames.astype(f32) + conv_act
        attn_in = hidden_one.astype(low_type)
    zero_part = jnp.zeros((HEADS, HEAD_DIM), f32)
    qkv_bias = jnp.stack(
        [vectors[1].reshape(HEADS, HEAD_DIM), zero_part, vectors[2].reshape(HEADS, HEAD_DIM)], axis=1
    ).reshape(3 * model_width)
    packed = (
        lax.dot_general(full_qkv, attn_in, (((0,), (1,)), ((), ())), preferred_element_type=f32) + qkv_bias[:, None]
    ).astype(low_type)
    if by_chips():
        heads_qkv, context, log_sums, context_wide = attend(seg_rows, packed, [], [])
    else:
        blocks = trade(by_partner(packed.reshape(head_groups, -1, row_count)))
        fwd = attn_fwd(seg_rows, blocks)
        context = from_partner(trade(fwd[:4]))
    layer_out, grad_two, grad_context, grad_rows, grad_ffn_bias, grad_proj, grad_up, grad_down = ffn_step(
        context, all_proj, all_up, all_down, hidden_one, output_grad, vectors, full_ffn
    )
    if by_chips():
        sum_up = lax.psum_scatter(grad_up, ("seq", "head"), scatter_dimension=0, tiled=False).astype(f32)
        grad_packed, square_tile, sum_proj, sum_down = attend_back(
            seg_rows, heads_qkv, log_sums, context_wide, grad_context, [by_owner(grad_proj), by_owner(grad_down)], attend_back_plan()
        )
    else:
        grad_blocks = trade(by_partner(grad_context.reshape(head_groups, -1, row_count)))
        grad_packed = from_partner(trade(attn_bwd(seg_rows, blocks, grad_blocks, fwd[4], fwd[5])))
    grad_qkv = lax.dot_general(attn_in, grad_packed, (((0,), (1,)), ((), ())), preferred_element_type=f32).astype(low_type)
    grad_split = jnp.sum(grad_packed.astype(f32), axis=1).reshape(HEADS, 3, HEAD_DIM)
    grad_query_bias = grad_split[:, 0].reshape(model_width)
    grad_value_bias = grad_split[:, 2].reshape(model_width)
    grad_hidden_one = grad_two + lax.dot_general(grad_packed, full_qkv, (((0,), (1,)), ((), ())), preferred_element_type=f32)
    grad_conv_low = (grad_hidden_one * conv_slope).astype(low_type)
    grad_conv_bias = jnp.sum(grad_conv_low.astype(f32), axis=0)
    grad_vectors = jnp.concatenate([jnp.stack([grad_conv_bias, grad_query_bias, grad_value_bias], axis=0), grad_rows[3:]], axis=0)
    grad_small = as_small(
        grad_vectors.reshape(vec_rows, count, vec_cols).transpose(1, 0, 2).astype(low_type), grad_ffn_bias.reshape(count, ffn_cols).astype(low_type)
    )
    grad_qkv = grad_qkv.reshape((count,) + qkv_weight.shape)
    if by_chips():
        grad_frames_conv, norm_tile, sum_conv, sum_qkv, sum_small = close_step(
            cut, conv_columns, grad_conv_low, whole_conv, [by_owner(grad_qkv), by_owner(grad_small)], side_plan(), main_plan()
        )
        norm_tile = norm_step(norm_tile + square_tile, [sum_up])
        square_total = jnp.sum(norm_tile)
        sum_down = sum_down.reshape(down_weight.shape)
        sum_up = sum_up.transpose(1, 0, 2).reshape(up_weight.shape)
    else:
        grad_window = with_halo(grad_conv_low, (("head", 0),), half_kernel)
        grad_frames_conv, grad_conv = conv_bwd(cut, window, grad_window, full_conv)
        grad_conv = grad_conv.reshape(16, 2, 8, 24 // conv_rows, conv_rows, 768).transpose(0, 1, 3, 2, 4, 5).reshape(count, 8, conv_rows, 768)
        grad_down, grad_proj = [g.reshape((count,) + w.shape) for g, w in ((grad_down, down_weight), (grad_proj, proj_weight))]
        grad_up = grad_up.transpose(0, 2, 1, 3).reshape((count,) + up_weight.shape)
        (sum_conv, sum_qkv, sum_proj, sum_up, sum_down, sum_small), square_total = collect_grads(
            [grad_conv, grad_qkv, grad_proj, grad_up, grad_down, grad_small]
        )
    frames_grad = grad_hidden_one + grad_frames_conv
    sum_vectors = sum_small[:vec_rows, :vec_cols]
    sum_ffn_bias = sum_small[vec_rows, :ffn_cols]
    grad_norm = jnp.sqrt(square_total)
    masters = (qkv_weight, proj_weight, up_weight, down_weight, conv_weight, bias_gains, ffn_bias)
    firsts = (qkv_first, proj_first, up_first, down_first, conv_first, bias_gains_first, ffn_bias_first)
    seconds = (qkv_second, proj_second, up_second, down_second, conv_second, bias_gains_second, ffn_bias_second)
    sum_conv = sum_conv.reshape(8, conv_rows, 16, group_width).transpose(2, 0, 1, 3).reshape(conv_weight.shape)
    summed = (sum_qkv, sum_proj, sum_up, sum_down, sum_conv, sum_vectors, sum_ffn_bias)
    factor = jnp.minimum(1.0, clip_bound / grad_norm)
    news, first_news, second_news = [], [], []
    for index in range(7):
        decay = matrix_decay if index < 5 else 0.0
        new_weight, first_new, second_new = adam_update(
            masters[index], summed[index] * factor, firsts[index], seconds[index], weight_rates[index], decay
        )
        news.append(new_weight)
        first_news.append(first_new)
        second_news.append(second_new)
    return (layer_out, frames_grad, grad_norm, *news, *first_news, *second_news)


def solution(mesh):
    rows, both = P(("seq", "head"), None), ("seq", "head")
    weights = (rows, rows, rows, rows, P(None, both, None), P(None, both), P(both))
    return jax.shard_map(
        shards,
        mesh=mesh,
        in_specs=(rows, rows, P("seq", None)) + weights * 3,
        out_specs=(rows, rows, P()) + weights * 3,
        check_vma=False,
    )
```
